256 devices in a mesh: region: 8 (over x, core), tile: 32 (over z, y).
Axes of the slice: x: 4, y: 4, z: 8, core: 2. Of those that a mesh axis runs over, the one named last changes fastest.
Arguments:
- kx: float32 [8, 128, 4096], P(None, 'region', 'tile'), may hold values from 0.05 to 0.24
- ky: float32 [8, 128, 4096], P(None, 'region', 'tile'), may hold values from 0.05 to 0.24
- mask: int32 [8, 128, 4096], P(None, 'region', 'tile'), may hold values 0 or 1
- obs_owner: int32 [131072, 1], P(('region', 'tile')), may hold values from 0 to 31; in each aligned block of 512 rows (0 to 511, 512 to 1023, ...) at most 32 rows name the same one
- obs_row: int32 [131072], P(('region', 'tile')), may hold values from 0 to 14
- obs_col: int32 [131072], P(('region', 'tile')), may hold values from 0 to 126
- obs_weight: float32 [131072, 128], P(('region', 'tile')), may hold values from -1 to 1
- innovation: float32 [131072], P(('region', 'tile')), may hold values from -6 to 6
- inverse_var: float32 [131072], P(('region', 'tile')), may hold values from 0.5 to 4
Outputs:
- control: float32 [4, 8, 128, 4096], P(None, None, 'region', 'tile')
- residual: float32 [4, 8, 128, 4096], P(None, None, 'region', 'tile')
The draws below stay inside these ranges and needn't reach their ends.
Inputs may be any that keep to these rules, and one draw needn't show every extreme that they name: `obs_owner`: within the rows of one device no tile is named more than 32 times.
All inputs are finite; a program needn't handle non-finite values. No bound on the sum of `mask` on one device may be relied on, other than what follows from the above.
Results may differ from the reference program's by a relative error of at most 0.009.
Values sent between devices are 32-bit elements; how exact they have to be, the bound alone decides.
A program may use at most 64 MiB of HBM per device.

```python
import math
import jax
import jax.numpy as jnp
import numpy as np

FIELDS = 4
LEV = 8
BLOCK = 128
STEPS = 4
ITERS = 2
CX = 16
CY = 128
OBS_DEV = 512
CAP = 32
NX = 128
NY = 4096
NOBS = 131072
N_TILE = 32


def rates_between(key, lower, upper):
    spread_log = jax.random.uniform(key, (LEV, NX, NY), jnp.float32, math.log(lower), math.log(upper))
    return jnp.exp(spread_log)


def draw_kx(key, part):
    key = jax.random.fold_in(key, 11)
    return rates_between(key, 0.05, 0.24)


def draw_ky(key, part):
    key = jax.random.fold_in(key, 23)
    return rates_between(key, 0.05, 0.24)


def set_ends(drawn, key, smallest, largest):
    extent = drawn.shape
    index_at = [jax.random.randint(jax.random.fold_in(key, axis), (), 0, extent[axis]) for axis in range(len(extent))]
    drawn = drawn.at[tuple(index_at)].set(smallest)
    longest = extent.index(max(extent))
    index_at[longest] = (index_at[longest] + 1) % extent[longest]
    return drawn.at[tuple(index_at)].set(largest)


def block_scale(stream_key, dims, cuts, least, top_value):
    def one(axis_at, parts):
        steps = jax.random.uniform(jax.random.fold_in(jax.random.fold_in(stream_key, 6), axis_at), (parts,), jnp.float32, least / len(cuts), top_value / len(cuts))
        return jnp.repeat(jnp.exp(steps), dims[axis_at] // parts).reshape((-1,) + (1,) * (len(dims) - axis_at - 1))

    level = one(*cuts[0])
    for cut in cuts[1:]:
        level = level * one(*cut)
    return level


def routed_block(own_key, own, number, rows, number_of, top, most, lean):
    sequence = jax.random.permutation(own_key, number_of)
    packed, ordinary = shares(number_of, rows * top, most, lean, True), shares(number_of, rows * top, most, lean, False)
    places = jnp.arange(number_of)

    def named(tallies, turn):
        used = int((tallies > 0).sum())
        fixed = max(1, used // 4)
        passed = fixed + (places - fixed + turn * (used - fixed)) % max(1, number_of - fixed)
        return jnp.zeros((number_of,), jnp.int32).at[sequence[jnp.where(places < fixed, places, passed)]].set(jnp.asarray(tallies, jnp.int32))

    tallies = jnp.where(number % 4 == 0, named(packed, number // 4), named(ordinary, number - number // 4 - 1))
    mixed = jax.random.permutation(jax.random.fold_in(own, 3), number_of)
    source_of, receiver = mixed[0:number_of // 2 * 2:2], mixed[1:number_of // 2 * 2:2]
    margin = jnp.minimum(tallies[source_of] - 1, most - tallies[receiver]) // 2
    margin = jnp.where((source_of == sequence[0]) | (receiver == sequence[0]) | (tallies[receiver] == 0), 0, jnp.maximum(margin, 0))
    passed = jax.random.randint(jax.random.fold_in(own, 4), (number_of // 2,), 0, 1 << 20) % (margin + 1)
    tallies = tallies.at[source_of].add(-passed).at[receiver].add(passed)
    items = jnp.searchsorted(jnp.cumsum(tallies), jnp.arange(rows * top), side="right").astype(jnp.int32)
    table = items.reshape(top, rows).T
    table = table[jax.random.permutation(jax.random.fold_in(own, 1), rows)]
    turn = jax.random.randint(jax.random.fold_in(own, 2), (rows, 1), 0, top)
    return jnp.take_along_axis(table, (jnp.arange(top)[None, :] + turn) % top, axis=1)


def shares(number_of, total, bound, skew, full):
    loads = [(1 << 20) // math.isqrt(rank ** skew) + 1 for rank in range(1, number_of + 1)]
    largest = bound if full else min(bound, max(-(-total // number_of), total * loads[0] // sum(loads)))
    least = 1 if total - largest >= number_of - 1 else 0
    given, spare = [largest] + [least] * (number_of - 1), total - largest - least * (number_of - 1)
    while spare > 0:
        candidates = [i for i in range(1, number_of) if given[i] < largest] or [i for i in range(1, number_of) if given[i] < bound]
        whole, remaining = sum([loads[i] for i in candidates]), spare
        for i in candidates:
            extra = min(bound - given[i], max(1, remaining * loads[i] // whole), spare)
            given[i] = given[i] + extra
            spare = spare - extra
    return np.array(given)


def normal_values(rng, shape, scale, limit, shards=(), kind=jnp.bfloat16):
    drawn = jax.random.normal(rng, shape, jnp.float32) * scale
    if len(shards) > 0:
        drawn = block_scale(rng, shape, shards, -0.22, 0.18) * drawn
    return jnp.clip(drawn, min=-limit, max=limit).astype(kind)


def setup_inputs(seed: int = 0) -> dict:
    key_of = jax.random.split(jax.random.key(seed), 10)
    kx = draw_kx(jax.random.fold_in(key_of[9], 71), 0)
    ky = draw_ky(jax.random.fold_in(key_of[9], 71), 0)
    mask = set_ends((jax.random.randint(key_of[2], (LEV, NX, NY), 0, 8) < 7).astype(jnp.int32), jax.random.fold_in(key_of[2], 1), 0, 1)
    obs_owner_keys = jax.random.split(jax.random.fold_in(key_of[3], 1), NOBS // OBS_DEV)
    obs_owner_turns = jax.random.permutation(jax.random.fold_in(key_of[3], 3), NOBS // OBS_DEV)
    obs_owner = jax.vmap(lambda own, number: routed_block(jax.random.fold_in(key_of[3], 2), own, number, OBS_DEV, N_TILE, 1, CAP, 2))(obs_owner_keys, obs_owner_turns).reshape((NOBS, 1))
    obs_row = set_ends(jax.random.randint(key_of[4], (NOBS,), 0, CX - 1), jax.random.fold_in(key_of[4], 1), 0, (CX - 1) - 1).astype(jnp.int32)
    obs_col = set_ends(jax.random.randint(key_of[5], (NOBS,), 0, CY - 1), jax.random.fold_in(key_of[5], 1), 0, (CY - 1) - 1).astype(jnp.int32)
    obs_weight = normal_values(key_of[6], (NOBS, BLOCK), 32 ** -0.5, 1.0, ((0, 256),), jnp.float32)
    innovation = normal_values(key_of[7], (NOBS,), 1.0, 6.0, ((0, 256),), jnp.float32)
    inverse_var = jnp.clip(jnp.exp(math.log(4.0) - 2.0794415 * jax.random.uniform(key_of[8], (NOBS,), jnp.float32) ** block_scale(key_of[8], (NOBS,), ((0, 256),), -0.2, 0.2)), 0.5, 4.0)
    return dict(kx=kx, ky=ky, mask=mask, obs_owner=obs_owner, obs_row=obs_row, obs_col=obs_col, obs_weight=obs_weight, innovation=innovation, inverse_var=inverse_var)


def diffuse(field, wet, east, north):
    plain = field * wet
    centre = plain[..., 1:-1, 1:-1]
    flux = east[:, 1:-1, 1:-1] * (plain[..., 2:, 1:-1] - centre)
    flux = flux - east[:, :-2, 1:-1] * (centre - plain[..., :-2, 1:-1])
    flux = flux + north[:, 1:-1, 1:-1] * (plain[..., 1:-1, 2:] - centre)
    flux = flux - north[:, 1:-1, :-2] * (centre - plain[..., 1:-1, :-2])
    return wet[:, 1:-1, 1:-1] * (centre + flux)


def reference(kx, ky, mask, obs_owner, obs_row, obs_col, obs_weight, innovation, inverse_var):
    wet = mask.astype(jnp.float32)
    padded = jnp.pad(wet, ((0, 0), (1, 1), (1, 1)))
    east = kx * wet * padded[:, 2:, 1:-1]
    north = ky * wet * padded[:, 1:-1, 2:]
    frame = ((0, 0), (1, 1), (1, 1))
    wet_pad = jnp.pad(wet, frame)
    east_pad = jnp.pad(east, frame)
    north_pad = jnp.pad(north, frame)
    slices = FIELDS * LEV

    def spread(field):
        for step in range(STEPS):
            field = diffuse(jnp.pad(field, ((0, 0), (0, 0), (1, 1), (1, 1))), wet_pad, east_pad, north_pad)
        return field

    device = jnp.arange(NOBS, dtype=jnp.int32) // OBS_DEV
    region = device // N_TILE
    first = region * CX + obs_row
    second = obs_owner[:, 0] * CY + obs_col
    base = first * NY + second
    corners = base[:, None] + jnp.array([0, 1, NY, NY + 1], jnp.int32)[None, :]

    def observe(field):
        table = field.reshape(slices, NX * NY).T
        values = table[corners].reshape(NOBS, BLOCK)
        return jnp.sum(obs_weight * values, axis=1)

    def adjoint(weights):
        terms = (obs_weight * weights[:, None]).reshape(NOBS * 4, slices)
        table = jnp.zeros((NX * NY, slices), jnp.float32).at[corners.reshape(-1)].add(terms)
        return table.T.reshape(FIELDS, LEV, NX, NY)

    def hessian(direction):
        return direction + spread(adjoint(inverse_var * observe(spread(direction))))

    right_side = spread(adjoint(inverse_var * innovation))
    control = jnp.zeros_like(right_side)
    residual = right_side
    direction = right_side
    norm_now = jnp.sum(residual * residual)
    for step in range(ITERS):
        image = hessian(direction)
        alpha = norm_now / jnp.sum(direction * image)
        control = control + alpha * direction
        residual = residual - alpha * image
        norm_next = jnp.sum(residual * residual)
        direction = residual + (norm_next / norm_now) * direction
        norm_now = norm_next
    return control, residual
```

```python
import functools

import jax
import jax.numpy as jnp
from jax import lax
from jax.experimental import pallas as pl
from jax.experimental.pallas import tpu as pltpu
from jax.sharding import PartitionSpec as P

MESH = pl.DeviceIdType.MESH
F32 = jnp.float32
BF16 = jnp.bfloat16
CAP = 32
LANES = 128
GROUPS = 4
WIDE = 40
FRAME_ROWS = 25


def iota(shape, dim):
    return lax.broadcasted_iota(jnp.int32, shape, dim)


def split(x, parts):
    out = []
    for i in range(parts):
        part = x.astype(BF16)
        out.append(part)
        if i + 1 < parts:
            x = x - part.astype(F32)
    return out


def dot(a, b):
    return jnp.dot(a, b, preferred_element_type=F32)


def dot_nt(a, b):
    return lax.dot_general(a, b, (((1,), (1,)), ((), ())), preferred_element_type=F32)


def kernel(
    regions, tiles, kx_ref, ky_ref, mask_ref, owner_ref, row_ref, col_ref, innov_ref, var_ref, weight_ref,
    control_ref, residual_ref,
    dense, rows_in, left_in, right_in, packed, frame, coef, wsplit, wsend, wrecv, msend, mrecv, expanded,
    pick, pick_t, terms, var_b, z_b, acc, state16, fields, sums_send, sums_tile, sums_mid, sums_region,
    halo_send, halo_recv, w_send_sem, w_recv_sem, m_send_sem, m_recv_sem, t_send_sem, t_recv_sem, r_send_sem, r_recv_sem,
):
    reg, til = lax.axis_index("region"), lax.axis_index("tile")
    up, down = lax.rem(reg + regions - 1, regions), lax.rem(reg + 1, regions)
    left, right = lax.rem(til + tiles - 1, tiles), lax.rem(til + 1, tiles)
    count = owner_ref.shape[1]
    slots = tiles * CAP

    barrier = pltpu.get_barrier_semaphore()

    def greet_tile(i, _):
        pl.semaphore_signal(barrier, inc=1, device_id=(reg, lax.rem(til + i, tiles)), device_id_type=MESH)
        return 0

    def greet_region(i, _):
        pl.semaphore_signal(barrier, inc=1, device_id=(lax.rem(reg + i, regions), til), device_id_type=MESH)
        return 0

    lax.fori_loop(1, tiles, greet_tile, 0)
    lax.fori_loop(1, regions, greet_region, 0)
    for a in (up, down):
        for b in (left, right):
            pl.semaphore_signal(barrier, inc=1, device_id=(a, b), device_id_type=MESH)

    owner = owner_ref[...]
    marks = jnp.where(iota((tiles, count), 0) == owner, 1.0, 0.0)
    upper = jnp.where(iota((count, count), 0) < iota((count, count), 1), 1.0, 0.0).astype(BF16)
    before = dot(marks.astype(BF16), upper)
    slot = owner * CAP + jnp.sum(before * marks, axis=0, keepdims=True).astype(jnp.int32)
    for i, part in enumerate(split(weight_ref[...], 3)):
        wsplit[:, i * LANES:(i + 1) * LANES] = part
    meta_rows = [row_ref[...].astype(F32), col_ref[...].astype(F32)]
    meta_rows += [p.astype(F32) for p in split(innov_ref[...], 3) + split(var_ref[...], 3)]
    meta = jnp.zeros((8, count), F32)
    for i, line in enumerate(meta_rows):
        meta = jnp.where(iota((8, count), 0) == i, line, meta)
    meta = meta.astype(BF16)
    lane8 = iota((8, LANES), 1)
    for b in range(tiles // 4):
        chosen = jnp.where(iota((LANES, count), 0) + b * LANES == slot, 1.0, 0.0).astype(BF16)
        block = dot(chosen, wsplit[...])
        block = block[:, :LANES] + block[:, LANES:2 * LANES] + block[:, 2 * LANES:]
        wsend[4 * b:4 * b + 4] = block.reshape(4, CAP, LANES)
        facts = dot_nt(meta, chosen)
        place = jnp.broadcast_to(facts[0:1] * LANES + facts[1:2], (8, LANES))
        innov = jnp.broadcast_to(facts[2:3] + facts[3:4] + facts[4:5], (8, LANES))
        var = jnp.broadcast_to(facts[5:6] + facts[6:7] + facts[7:8], (8, LANES))
        for k in range(4):
            turned = [pltpu.roll(x, (i - k) * 32 % LANES, 1) for i, x in enumerate((place, innov, var))]
            line = jnp.where(lane8 < 32, turned[0], jnp.where(lane8 < 64, turned[1], jnp.where(lane8 < 96, turned[2], 0.0)))
            msend[4 * b + k] = line[0:1]

    pl.semaphore_wait(barrier, (tiles - 1) + (regions - 1) + 4)

    def peer(i):
        return lax.rem(til + i, tiles)

    def w_copy(i):
        return pltpu.make_async_remote_copy(
            src_ref=wsend.at[peer(i)], dst_ref=wrecv.at[til], send_sem=w_send_sem.at[i], recv_sem=w_recv_sem.at[i],
            device_id=(reg, peer(i)), device_id_type=MESH)

    def m_copy(i):
        return pltpu.make_async_remote_copy(
            src_ref=msend.at[peer(i)], dst_ref=mrecv.at[til], send_sem=m_send_sem.at[i], recv_sem=m_recv_sem.at[i],
            device_id=(reg, peer(i)), device_id_type=MESH)

    def each(lo, hi, act):
        def step(i, _):
            act(i)
            return 0
        lax.fori_loop(lo, hi, step, 0)

    each(1, tiles, lambda i: m_copy(i).start())
    each(1, tiles, lambda i: w_copy(i).start())
    wrecv[til] = wsend[til]
    mrecv[til] = msend[til]

    sub8 = iota((8, LANES), 0)

    def halo_copies(e):
        def copy(n, src, dst, device):
            return pltpu.make_async_remote_copy(
                src_ref=src, dst_ref=dst, send_sem=halo_send.at[e, n], recv_sem=halo_recv.at[e, n],
                device_id=device, device_id_type=MESH)
        return [
            copy(0, dense.at[e, pl.ds(0, 128)], rows_in.at[e, 1], (up, til)),
            copy(1, dense.at[e, pl.ds(384, 128)], rows_in.at[e, 0], (down, til)),
            copy(2, packed.at[e, pl.ds(0, 4)], left_in.at[e, pl.ds(1, 4)], (reg, right)),
            copy(3, packed.at[e, pl.ds(4, 4)], right_in.at[e, pl.ds(1, 4)], (reg, left)),
            copy(4, packed.at[e, 0], left_in.at[e, 5], (up, right)),
            copy(5, packed.at[e, 3], left_in.at[e, 0], (down, right)),
            copy(6, packed.at[e, 4], right_in.at[e, 5], (up, left)),
            copy(7, packed.at[e, 7], right_in.at[e, 0], (down, left)),
        ]

    def halo_start(e):
        for j in range(4):
            to_right = jnp.zeros((8, LANES), F32)
            to_left = jnp.zeros((8, LANES), F32)
            for b in range(4):
                base = (4 * j + b) * 32
                here = (lane8 >= 32 * b) & (lane8 < 32 * b + 32)
                to_right = jnp.where(here, pltpu.roll(dense[e, base + 24:base + 32, :], (b - 3) * 32 % LANES, 1), to_right)
                to_left = jnp.where(here, pltpu.roll(dense[e, base:base + 8, :], b * 32 % LANES, 1), to_left)
            packed[e, j] = to_right
            packed[e, 4 + j] = to_left
        for c in halo_copies(e):
            c.start()

    def halo_finish(e, out):
        for j in range(16):
            out[(4 + j) * WIDE + 8:(5 + j) * WIDE, :] = dense[e, j * 32:(j + 1) * 32, :]
        for c in halo_copies(e):
            c.wait()

    def build_frame(e, out):
        for j in range(4):
            out[j * WIDE + 8:(j + 1) * WIDE, :] = rows_in[e, 0, j * 32:(j + 1) * 32, :]
            out[(20 + j) * WIDE + 8:(21 + j) * WIDE, :] = rows_in[e, 1, j * 32:(j + 1) * 32, :]

        carry = jnp.zeros((8, LANES), F32)
        for k in range(24):
            j, b = k // 4, k % 4
            base = k * WIDE
            from_left = jnp.where(lane8 < 32, pltpu.roll(left_in[e, j], -b * 32 % LANES, 1), pltpu.roll(out[base + 32:base + 40, :], 32, 1))
            from_right = jnp.where(lane8 >= 96, pltpu.roll(right_in[e, j], (3 - b) * 32, 1), pltpu.roll(out[base + 8:base + 16, :], 96, 1))
            out[base:base + 8, :] = jnp.where(sub8 >= 4, from_left, carry)
            carry = from_right
        out[24 * WIDE:24 * WIDE + 8, :] = carry

    def to_cells(source, e):
        group_of_row = iota((LANES, LANES), 0) // 32
        group_of_lane = iota((LANES, LANES), 1) // 32
        fold = jnp.where(iota((32, LANES), 0) == iota((32, LANES), 1) % 32, 1.0, 0.0).astype(BF16)
        for r in range(16):
            line = source[pl.ds(r, 8, stride=16), :].astype(F32)
            many = jnp.where(group_of_row == group_of_lane, jnp.concatenate([line] * 16, axis=0), 0.0)
            total = jnp.zeros((32, LANES), F32)
            for part in split(many, 3):
                total = total + dot_nt(fold, part)
            dense[e, r * 32:(r + 1) * 32, :] = total

    for e, source in enumerate((mask_ref, kx_ref, ky_ref)):
        to_cells(source, e)
        halo_start(e)
    for e in range(3):
        halo_finish(e, coef.at[e])
        if e == 0:
            inside_up = jnp.where(reg > 0, 1.0, 0.0)
            inside_down = jnp.where(reg < regions - 1, 1.0, 0.0)
            inside_left = jnp.where(til > 0, 1.0, 0.0)
            inside_right = jnp.where(til < tiles - 1, 1.0, 0.0)
            rows_in[0, 0] = rows_in[0, 0] * inside_up
            rows_in[0, 1] = rows_in[0, 1] * inside_down
            left_in[0] = left_in[0] * inside_left
            right_in[0] = right_in[0] * inside_right
            for side in (left_in, right_in):
                side[0, 0] = side[0, 0] * inside_up
                side[0, 5] = side[0, 5] * inside_down
        build_frame(e, coef.at[e])

    def make_faces(k, _):
        base = pl.multiple_of(k * WIDE, 8)
        wet = coef[0, pl.ds(base, WIDE), :]
        coef[1, pl.ds(base, WIDE), :] = coef[1, pl.ds(base, WIDE), :] * wet * coef[0, pl.ds(base + WIDE, WIDE), :]
        coef[2, pl.ds(base, WIDE), :] = coef[2, pl.ds(base, WIDE), :] * wet * coef[0, pl.ds(base + 1, WIDE), :]
        return 0

    lax.fori_loop(0, 24, make_faces, 0)

    def make_centre(k, _):
        base = pl.multiple_of(k * WIDE, 8)
        faces = coef[1, pl.ds(base, WIDE), :] + coef[1, pl.ds(base - WIDE, WIDE), :]
        faces = faces + coef[2, pl.ds(base, WIDE), :] + coef[2, pl.ds(base - 1, WIDE), :]
        coef[0, pl.ds(base, WIDE), :] = coef[0, pl.ds(base, WIDE), :] - faces
        return 0

    lax.fori_loop(1, 24, make_centre, 0)

    def stencil(src, base):
        out = coef[0, pl.ds(base, WIDE), :] * frame[src, pl.ds(base, WIDE), :]
        out = out + coef[1, pl.ds(base, WIDE), :] * frame[src, pl.ds(base + WIDE, WIDE), :]
        out = out + coef[1, pl.ds(base - WIDE, WIDE), :] * frame[src, pl.ds(base - WIDE, WIDE), :]
        out = out + coef[2, pl.ds(base, WIDE), :] * frame[src, pl.ds(base + 1, WIDE), :]
        out = out + coef[2, pl.ds(base - 1, WIDE), :] * frame[src, pl.ds(base - 1, WIDE), :]
        return out

    def spread_finish(e, out):
        halo_finish(e, frame.at[0])
        build_frame(e, frame.at[0])
        for step in range(3):
            src, dst = step % 2, (step + 1) % 2

            def line(k, _):
                base = pl.multiple_of(k * WIDE, 8)
                frame[dst, pl.ds(base, WIDE), :] = stencil(src, base)
                return 0

            lax.fori_loop(step + 1, 24 - step, line, 0)

        def last(k, _):
            base = pl.multiple_of(k * WIDE, 8)
            out[pl.ds(pl.multiple_of((k - 4) * 32, 8), 32), :] = stencil(1, base)[8:, :]
            return 0

        lax.fori_loop(4, 20, last, 0)

    each(1, tiles, lambda i: m_copy(i).wait_recv())
    lane = iota((slots, LANES), 1)
    seat = iota((slots, LANES), 0) % CAP
    facts = jnp.broadcast_to(mrecv[...], (tiles, CAP, LANES)).reshape(slots, LANES)
    ones = jnp.ones((3 * LANES, LANES), BF16)

    def spread_lanes(kind):
        parts = split(jnp.where(lane == seat + 32 * kind, facts, 0.0), 3)
        return jnp.concatenate(parts, axis=1)

    place3 = spread_lanes(0)
    place_col = dot(place3, ones).astype(jnp.int32)
    place_row = dot_nt(jnp.ones((8, 3 * LANES), BF16), place3).astype(jnp.int32)[0:1]
    var_b[...] = dot(spread_lanes(2), ones)
    z_b[...] = var_b[...] * dot(spread_lanes(1), ones)

    def corner_of(place, c):
        row = (place >> 7) + c // 2
        col = (place & 127) + c % 2
        return row * 32 + (col & 31), col >> 5

    cells = pick.shape[2]
    for c in range(4):
        cell, _ = corner_of(place_col, c)
        for t in range(cells // LANES):
            pick[c, :, t * LANES:(t + 1) * LANES] = jnp.where(cell == lane + t * LANES, 1.0, 0.0).astype(BF16)
        cell, _ = corner_of(place_row, c)
        pick_t[:, c * slots:(c + 1) * slots] = jnp.where(iota((cells, slots), 0) == cell, 1.0, 0.0).astype(BF16)

    each(1, tiles, lambda i: w_copy(i).wait_recv())
    w3 = jnp.concatenate(split(wrecv[...].reshape(slots, LANES), 3), axis=1)
    for c in range(4):
        copy_lanes = jnp.where(iota((3 * LANES, LANES), 0) % LANES == c * 32 + iota((3 * LANES, LANES), 1) % 32, 1.0, 0.0).astype(BF16)
        _, group = corner_of(place_col, c)
        expanded[c] = jnp.where(group == lane // 32, dot(w3, copy_lanes), 0.0)

    def adjoint(e):
        def one(c, _):
            hi, lo = split(z_b[...] * expanded[c], 2)
            at = pl.ds(pl.multiple_of(c * slots, 128), slots)
            terms[at, :LANES] = hi
            terms[at, LANES:] = lo
            return 0
        lax.fori_loop(0, 4, one, 0)
        total = dot(pick_t[...], terms[...])
        dense[e] = total[:, :LANES] + total[:, LANES:]

    def observe(field):
        hi, lo = split(field, 2)
        state16[:, :LANES] = hi
        state16[:, LANES:] = lo
        acc[...] = jnp.zeros_like(acc)

        def one(c, _):
            values = dot(pick[c], state16[...])
            acc[...] += (values[:, :LANES] + values[:, LANES:]) * expanded[c]
            return 0

        lax.fori_loop(0, 4, one, 0)
        z_b[...] = var_b[...] * dot(jnp.concatenate(split(acc[...], 2), axis=1), ones[:2 * LANES])

    def t_copy(n, i):
        return pltpu.make_async_remote_copy(
            src_ref=sums_send.at[n], dst_ref=sums_tile.at[n, til], send_sem=t_send_sem.at[n, i], recv_sem=t_recv_sem.at[n, i],
            device_id=(reg, peer(i)), device_id_type=MESH)

    def r_copy(n, i):
        return pltpu.make_async_remote_copy(
            src_ref=sums_mid.at[n], dst_ref=sums_region.at[n, reg], send_sem=r_send_sem.at[n, i], recv_sem=r_recv_sem.at[n, i],
            device_id=(lax.rem(reg + i, regions), til), device_id_type=MESH)

    def sums_start(n, products):
        for i, x in enumerate(products):
            sums_send[n, i:i + 1, :] = jnp.sum(x, axis=0, keepdims=True)
        for i in range(len(products), 2):
            sums_send[n, i:i + 1, :] = jnp.zeros((1, LANES), F32)
        each(1, tiles, lambda i: t_copy(n, i).start())
        sums_tile[n, til] = sums_send[n]

    def sums_middle(n):
        each(1, tiles, lambda i: t_copy(n, i).wait())
        sums_mid[n] = jnp.sum(sums_tile[n], axis=0)
        each(1, regions, lambda i: r_copy(n, i).start())
        sums_region[n, reg] = sums_mid[n]

    def sums_finish(n):
        each(1, regions, lambda i: r_copy(n, i).wait())
        total = jnp.sum(sums_region[n], axis=0)
        return jnp.sum(total, axis=1, keepdims=True)

    adjoint(3)
    halo_start(3)
    spread_finish(3, dense.at[4])
    halo_start(4)
    fields[0] = dense[4]
    spread_finish(4, fields.at[1])
    observe(fields[1])
    adjoint(5)
    halo_start(5)
    spread_finish(5, fields.at[2])
    fields[2] = fields[0] + fields[2]
    dense[6] = fields[2]
    halo_start(6)
    sums_start(0, (fields[0] * fields[0], fields[0] * fields[2]))
    spread_finish(6, fields.at[3])
    sums_middle(0)
    found = sums_finish(0)
    norm_0 = found[0:1]
    alpha = norm_0 / found[1:2]
    fields[4] = fields[0] - alpha * fields[2]
    fields[1] = fields[1] - alpha * fields[3]
    sums_start(1, (fields[4] * fields[4],))
    observe(fields[1])
    sums_middle(1)
    adjoint(7)
    halo_start(7)
    norm_1 = sums_finish(1)[0:1]
    beta = norm_1 / norm_0
    spread_finish(7, fields.at[6])
    fields[5] = fields[4] + beta * fields[0]
    fields[6] = fields[4] + fields[6] + beta * fields[2]
    sums_start(2, (fields[5] * fields[6],))
    sums_middle(2)
    alpha_1 = norm_1 / sums_finish(2)[0:1]
    fields[0] = alpha * fields[0] + alpha_1 * fields[5]
    fields[4] = fields[4] - alpha_1 * fields[6]

    group_of_row = iota((LANES, LANES), 0) // 32
    group_of_lane = iota((LANES, LANES), 1) // 32
    slice_of = jnp.where(iota((32, LANES), 0) == iota((32, LANES), 1) % 32, 1.0, 0.0).astype(BF16)
    for at, out in ((0, control_ref), (4, residual_ref)):
        for r in range(16):
            line = fields[at, r * 32:(r + 1) * 32, :]
            many = jnp.where(group_of_row == group_of_lane, jnp.concatenate([line] * 4, axis=0), 0.0)
            total = jnp.zeros((32, LANES), F32)
            for part in split(many, 3):
                total = total + dot_nt(slice_of, part)
            out[pl.ds(r, 32, stride=16), :] = total

    each(1, tiles, lambda i: m_copy(i).wait_send())
    each(1, tiles, lambda i: w_copy(i).wait_send())


def body(regions, tiles, kx, ky, mask, obs_owner, obs_row, obs_col, obs_weight, innovation, inverse_var):
    levels, rows_x, cols_y = kx.shape
    count = obs_row.shape[0]
    slots = tiles * CAP
    cells = rows_x * cols_y // GROUPS
    line = (1, count)
    vmem = pl.BlockSpec(memory_space=pltpu.VMEM)
    out = jax.ShapeDtypeStruct((32 * rows_x, cols_y), F32)
    dma = pltpu.SemaphoreType.DMA
    control, residual = pl.pallas_call(
        functools.partial(kernel, regions, tiles),
        out_shape=(out, out),
        in_specs=[vmem] * 9,
        out_specs=(vmem, vmem),
        scratch_shapes=[
            pltpu.VMEM((8, cells, LANES), F32),
            pltpu.VMEM((8, 2, 128, LANES), F32),
            pltpu.VMEM((8, 6, 8, LANES), F32),
            pltpu.VMEM((8, 6, 8, LANES), F32),
            pltpu.VMEM((8, 8, 8, LANES), F32),
            pltpu.VMEM((2, FRAME_ROWS * WIDE, LANES), F32),
            pltpu.VMEM((3, FRAME_ROWS * WIDE, LANES), F32),
            pltpu.VMEM((count, 3 * LANES), BF16),
            pltpu.VMEM((tiles, CAP, LANES), F32),
            pltpu.VMEM((tiles, CAP, LANES), F32),
            pltpu.VMEM((tiles, 1, LANES), F32),
            pltpu.VMEM((tiles, 1, LANES), F32),
            pltpu.VMEM((4, slots, LANES), F32),
            pltpu.VMEM((4, slots, cells), BF16),
            pltpu.VMEM((cells, 4 * slots), BF16),
            pltpu.VMEM((4 * slots, 2 * LANES), BF16),
            pltpu.VMEM((slots, LANES), F32),
            pltpu.VMEM((slots, LANES), F32),
            pltpu.VMEM((slots, LANES), F32),
            pltpu.VMEM((cells, 2 * LANES), BF16),
            pltpu.VMEM((7, cells, LANES), F32),
            pltpu.VMEM((3, 2, LANES), F32),
            pltpu.VMEM((3, tiles, 2, LANES), F32),
            pltpu.VMEM((3, 2, LANES), F32),
            pltpu.VMEM((3, regions, 2, LANES), F32),
            dma((8, 8)), dma((8, 8)),
            dma((tiles,)), dma((tiles,)), dma((tiles,)), dma((tiles,)),
            dma((3, tiles)), dma((3, tiles)), dma((3, regions)), dma((3, regions)),
        ],
        compiler_params=pltpu.CompilerParams(collective_id=0, has_side_effects=True, vmem_limit_bytes=48 * 1024 * 1024),
    )(
        kx.reshape(levels * rows_x, cols_y), ky.reshape(levels * rows_x, cols_y), mask.reshape(levels * rows_x, cols_y),
        obs_owner.reshape(line), obs_row.reshape(line), obs_col.reshape(line),
        innovation.reshape(line), inverse_var.reshape(line), obs_weight,
    )
    shape = (32 // levels, levels, rows_x, cols_y)
    return control.reshape(shape), residual.reshape(shape)


def solution(mesh):
    return jax.shard_map(
        functools.partial(body, mesh.shape["region"], mesh.shape["tile"]),
        mesh=mesh,
        in_specs=(
            P(None, "region", "tile"),
            P(None, "region", "tile"),
            P(None, "region", "tile"),
            P(("region", "tile"), None),
            P(("region", "tile")),
            P(("region", "tile")),
            P(("region", "tile"), None),
            P(("region", "tile")),
            P(("region", "tile")),
        ),
        out_specs=(P(None, None, "region", "tile"), P(None, None, "region", "tile")),
        check_vma=False,
    )
```

```python
import functools

import jax
import jax.numpy as jnp
from jax import lax
from jax.experimental import pallas as pl
from jax.experimental.pallas import tpu as pltpu
from jax.sharding import PartitionSpec as P

MESH = pl.DeviceIdType.MESH
F32 = jnp.float32
BF16 = jnp.bfloat16
CAP = 32
LANES = 128
GROUPS = 4
HALO = 8
WIDE = HALO + 32 + HALO
TALL = HALO + 16 + HALO
FRAME = (TALL + 1) * WIDE
EXCHANGES = 6


def iota(shape, dim):
    return lax.broadcasted_iota(jnp.int32, shape, dim)


def split(x, parts):
    out = []
    for i in range(parts):
        part = x.astype(BF16)
        out.append(part)
        if i + 1 < parts:
            x = x - part.astype(F32)
    return out


def dot(a, b):
    return jnp.dot(a, b, preferred_element_type=F32)


def dot_nt(a, b):
    return lax.dot_general(a, b, (((1,), (1,)), ((), ())), preferred_element_type=F32)


def swap_blocks(four):
    lane = iota(four[0].shape, 1)
    low = lane < 64
    even = (lane // 32) % 2 == 0
    a, b, c, d = four
    a, c = jnp.where(low, a, pltpu.roll(c, 64, 1)), jnp.where(low, pltpu.roll(a, 64, 1), c)
    b, d = jnp.where(low, b, pltpu.roll(d, 64, 1)), jnp.where(low, pltpu.roll(b, 64, 1), d)
    a, b = jnp.where(even, a, pltpu.roll(b, 32, 1)), jnp.where(even, pltpu.roll(a, 96, 1), b)
    c, d = jnp.where(even, c, pltpu.roll(d, 32, 1)), jnp.where(even, pltpu.roll(c, 96, 1), d)
    return a, b, c, d


def kernel(
    regions, tiles, kx_any, ky_any, mask_any, owner_any, row_any, col_any, innov_any, var_any, weight_any,
    control_ref, residual_ref,
    kx_ref, ky_ref, mask_ref, owner_ref, row_ref, col_ref, innov_ref, var_ref, weight_ref,
    dense, rows_in, left_in, right_in, packed, frame_a, frame_b, coef, wsplit, wsend, wrecv, msend, mrecv, expanded,
    pick, pick_t, terms, var_b, z_b, q_b, acc, group_b, state16, fields, natural, sums_send, sums_region, sums_mid, sums_tile,
    in_sem, halo_send, halo_recv, w_send_sem, w_recv_sem, m_send_sem, m_recv_sem, r_send_sem, r_recv_sem, t_send_sem, t_recv_sem,
):
    reg, til = lax.axis_index("region"), lax.axis_index("tile")
    up, down = lax.rem(reg + regions - 1, regions), lax.rem(reg + 1, regions)
    left, right = lax.rem(til + tiles - 1, tiles), lax.rem(til + 1, tiles)
    count = owner_ref.shape[1]
    slots = tiles * CAP
    planes = tiles // 4
    late = []

    barrier = pltpu.get_barrier_semaphore()
    for i in range(1, tiles):
        pl.semaphore_signal(barrier, inc=1, device_id=(reg, lax.rem(til + i, tiles)), device_id_type=MESH)
    for i in range(1, regions):
        pl.semaphore_signal(barrier, inc=1, device_id=(lax.rem(reg + i, regions), til), device_id_type=MESH)
    for a in (up, down):
        for b in (left, right):
            pl.semaphore_signal(barrier, inc=1, device_id=(a, b), device_id_type=MESH)

    pairs = (
        (owner_any, owner_ref), (weight_any, weight_ref), (row_any, row_ref), (col_any, col_ref), (innov_any, innov_ref),
        (var_any, var_ref), (mask_any, mask_ref), (kx_any, kx_ref), (ky_any, ky_ref),
    )
    loads = [pltpu.make_async_copy(a, b, in_sem.at[i]) for i, (a, b) in enumerate(pairs)]
    for c in loads:
        c.start()
    for c in loads:
        c.wait()

    owner = owner_ref[...]
    marks = jnp.where(iota((tiles, count), 0) == owner, 1.0, 0.0)
    upper = jnp.where(iota((count, count), 0) < iota((count, count), 1), 1.0, 0.0).astype(BF16)
    before = dot(marks.astype(BF16), upper)
    slot = owner * CAP + jnp.sum(before * marks, axis=0, keepdims=True).astype(jnp.int32)
    for i, part in enumerate(split(weight_ref[...], 3)):
        wsplit[:, i * LANES:(i + 1) * LANES] = part
    meta_rows = [row_ref[...].astype(F32), col_ref[...].astype(F32)]
    meta_rows += [p.astype(F32) for p in split(innov_ref[...], 3) + split(var_ref[...], 3)]
    meta = jnp.zeros((8, count), F32)
    for i, line in enumerate(meta_rows):
        meta = jnp.where(iota((8, count), 0) == i, line, meta)
    meta = meta.astype(BF16)
    lane8 = iota((8, LANES), 1)

    def sort_plane(b, _):
        chosen = jnp.where(iota((LANES, count), 0) + b * LANES == slot, 1.0, 0.0).astype(BF16)
        block = dot(chosen, wsplit[...])
        block = block[:, :LANES] + block[:, LANES:2 * LANES] + block[:, 2 * LANES:]
        wsend[pl.ds(4 * b, 4)] = block.reshape(4, CAP, LANES)
        facts = dot_nt(meta, chosen)
        place = jnp.broadcast_to(facts[0:1] * LANES + facts[1:2], (8, LANES))
        innov = jnp.broadcast_to(facts[2:3] + facts[3:4] + facts[4:5], (8, LANES))
        var = jnp.broadcast_to(facts[5:6] + facts[6:7] + facts[7:8], (8, LANES))
        for k in range(4):
            turned = [pltpu.roll(x, (i - k) * 32 % LANES, 1) for i, x in enumerate((place, innov, var))]
            line = jnp.where(lane8 < 32, turned[0], jnp.where(lane8 < 64, turned[1], jnp.where(lane8 < 96, turned[2], 0.0)))
            msend[4 * b + k] = line[0:1]
        return 0

    lax.fori_loop(0, planes, sort_plane, 0)

    turns = sorted(range(planes), key=lambda i: (min(i, planes - i), i))
    plane, place_in = til // 4, lax.rem(til, 4)

    def sends(src, dst, send_sem, recv_sem):
        out = []
        for j, turn in enumerate(turns):
            for k in range(4):
                if j or k:
                    to = lax.rem(plane + turn, planes) * 4 + lax.rem(place_in + k, 4)
                    n = 4 * j + k
                    out.append(pltpu.make_async_remote_copy(
                        src_ref=src.at[to], dst_ref=dst.at[n], send_sem=send_sem.at[n], recv_sem=recv_sem.at[n],
                        device_id=(reg, to), device_id_type=MESH))
        return out

    m_copies = sends(msend, mrecv, m_send_sem, m_recv_sem)
    w_copies = sends(wsend, wrecv, w_send_sem, w_recv_sem)
    late.extend(m_copies + w_copies)
    pl.semaphore_wait(barrier, (tiles - 1) + (regions - 1) + 4)
    for c in m_copies + w_copies:
        c.start()
    wrecv[0] = wsend[til]
    mrecv[0] = msend[til]

    def halo_copies(e, deep):
        def copy(n, src, dst, device):
            return pltpu.make_async_remote_copy(
                src_ref=src, dst_ref=dst, send_sem=halo_send.at[e, n], recv_sem=halo_recv.at[e, n],
                device_id=device, device_id_type=MESH)
        size, packs = deep * 32, deep // 4
        return [
            copy(4, packed.at[e, pl.ds(0, packs)], left_in.at[e, pl.ds(6, packs)], (up, right)),
            copy(5, packed.at[e, pl.ds(4 - packs, packs)], left_in.at[e, pl.ds(2 - packs, packs)], (down, right)),
            copy(6, packed.at[e, pl.ds(4, packs)], right_in.at[e, pl.ds(6, packs)], (up, left)),
            copy(7, packed.at[e, pl.ds(8 - packs, packs)], right_in.at[e, pl.ds(2 - packs, packs)], (down, left)),
            copy(2, packed.at[e, pl.ds(0, 4)], left_in.at[e, pl.ds(2, 4)], (reg, right)),
            copy(3, packed.at[e, pl.ds(4, 4)], right_in.at[e, pl.ds(2, 4)], (reg, left)),
            copy(0, dense.at[e, pl.ds(0, size)], rows_in.at[e, 1, pl.ds(0, size)], (up, til)),
            copy(1, dense.at[e, pl.ds(512 - size, size)], rows_in.at[e, 0, pl.ds(256 - size, size)], (down, til)),
        ]

    def halo_start(e, deep=8):
        for j in range(4):
            first = swap_blocks([dense[e, (4 * j + b) * 32:(4 * j + b) * 32 + 8, :] for b in range(4)])
            last = swap_blocks([dense[e, (4 * j + b) * 32 + 24:(4 * j + b) * 32 + 32, :] for b in range(4)])
            packed[e, j] = last[3]
            packed[e, 4 + j] = first[0]
        copies = halo_copies(e, deep)
        late.extend(copies)
        for c in copies:
            c.start()
        return copies

    def build_frame(e, copies, out, deep=8):
        for j in range(16):
            out[(8 + j) * WIDE + 16:(9 + j) * WIDE, :] = dense[e, j * 32:(j + 1) * 32, :]
        for c in copies:
            c.wait_recv()
        if e == 0:
            inside_up = jnp.where(reg > 0, 1.0, 0.0)
            inside_down = jnp.where(reg < regions - 1, 1.0, 0.0)
            rows_in[0, 0] = rows_in[0, 0] * inside_up
            rows_in[0, 1] = rows_in[0, 1] * inside_down
            for side, inside in ((left_in, jnp.where(til > 0, 1.0, 0.0)), (right_in, jnp.where(til < tiles - 1, 1.0, 0.0))):
                for j in range(8):
                    side[0, j] = side[0, j] * (inside * inside_up if j < 2 else inside if j < 6 else inside * inside_down)
        for j in range(8 - deep, 8):
            out[j * WIDE + 16:(j + 1) * WIDE, :] = rows_in[e, 0, j * 32:(j + 1) * 32, :]
        for j in range(deep):
            out[(24 + j) * WIDE + 16:(25 + j) * WIDE, :] = rows_in[e, 1, j * 32:(j + 1) * 32, :]

        def four_rows(j, _):
            for b in range(4):
                base = pl.multiple_of((4 * j + b) * WIDE, 8)
                ends, starts = out[pl.ds(base + 40, 8), :], out[pl.ds(base + 16, 8), :]
                out[pl.ds(base + 8, 8), :] = jnp.where(
                    lane8 < 32, pltpu.roll(left_in[e, j], -b * 32 % LANES, 1), pltpu.roll(ends, 32, 1))
                out[pl.ds(base + WIDE, 8), :] = jnp.where(
                    lane8 >= 96, pltpu.roll(right_in[e, j], (3 - b) * 32, 1), pltpu.roll(starts, 96, 1))
            return 0

        lax.fori_loop(2 - deep // 4, 6 + deep // 4, four_rows, 0)

    def to_cells(source, e):
        def four_rows(j, _):
            lines = [source[pl.ds(4 * j + b, 8, stride=16), :].astype(F32) for b in range(4)]
            many = jnp.concatenate([x for x in lines for _ in range(4)], axis=0).T
            for b, x in enumerate(swap_blocks([many[32 * g:32 * g + 32] for g in range(4)])):
                dense[e, pl.ds(pl.multiple_of((4 * j + b) * 32, 32), 32), :] = x
            return 0
        lax.fori_loop(0, 4, four_rows, 0)

    def to_natural(field, out):
        def four_rows(j, _):
            lines = [field[pl.ds(pl.multiple_of((4 * j + b) * 32, 32), 32), :] for b in range(4)]
            many = jnp.concatenate(swap_blocks(lines), axis=0).T
            for b in range(4):
                out[pl.ds(4 * j + b, 32, stride=16), :] = many[32 * b:32 * b + 32]
            return 0
        lax.fori_loop(0, 4, four_rows, 0)

    waiting = []
    for e, source in enumerate((mask_ref, kx_ref, ky_ref)):
        to_cells(source, e)
        waiting.append(halo_start(e))
    for e in range(3):
        build_frame(e, waiting[e], coef.at[e])

    def make_faces(k, _):
        base = pl.multiple_of(k * WIDE, 8)
        wet = coef[0, pl.ds(base, WIDE), :]
        coef[1, pl.ds(base, WIDE), :] = coef[1, pl.ds(base, WIDE), :] * wet * coef[0, pl.ds(base + WIDE, WIDE), :]
        coef[2, pl.ds(base, WIDE), :] = coef[2, pl.ds(base, WIDE), :] * wet * coef[0, pl.ds(base + 1, WIDE), :]
        return 0

    lax.fori_loop(0, TALL, make_faces, 0)

    def make_centre(k, _):
        base = pl.multiple_of(k * WIDE, 8)
        faces = coef[1, pl.ds(base, WIDE), :] + coef[1, pl.ds(base - WIDE, WIDE), :]
        faces = faces + coef[2, pl.ds(base, WIDE), :] + coef[2, pl.ds(base - 1, WIDE), :]
        coef[0, pl.ds(base, WIDE), :] = coef[0, pl.ds(base, WIDE), :] - faces
        return 0

    lax.fori_loop(1, TALL, make_centre, 0)

    def diffuse(first, last):
        for s in range(first, last + 1):
            src, dst = (frame_a, frame_b) if (s - first) % 2 == 0 else (frame_b, frame_a)

            def line(k, carry):
                before, here, west = carry
                base = pl.multiple_of(k * WIDE, 8)
                after = src[pl.ds(base + WIDE, WIDE), :]
                east = coef[1, pl.ds(base, WIDE), :]
                out = coef[0, pl.ds(base, WIDE), :] * here + east * after + west * before
                out = out + coef[2, pl.ds(base, WIDE), :] * src[pl.ds(base + 1, WIDE), :]
                out = out + coef[2, pl.ds(base - 1, WIDE), :] * src[pl.ds(base - 1, WIDE), :]
                dst[pl.ds(base, WIDE), :] = out
                return here, after, east

            at = (s - 1) * WIDE
            lax.fori_loop(s, TALL + 1 - s, line, (src[at:at + WIDE, :], src[at + WIDE:at + 2 * WIDE, :], coef[1, at:at + WIDE, :]))

    def inner(out):
        for j in range(16):
            out[j * 32:(j + 1) * 32, :] = frame_a[(8 + j) * WIDE + 16:(9 + j) * WIDE, :]

    for c in m_copies:
        c.wait_recv()
    lane = iota((LANES, LANES), 1)
    seat = iota((LANES, LANES), 0) % CAP
    ones = jnp.ones((3 * LANES, LANES), BF16)
    cells = pick.shape[2]

    def corner_of(place, c):
        row = (place >> 7) + c // 2
        col = (place & 127) + c % 2
        return row * 32 + (col & 31), col >> 5

    def read_facts(j, _):
        at = pl.ds(pl.multiple_of(j * LANES, LANES), LANES)
        facts = jnp.broadcast_to(mrecv[pl.ds(4 * j, 4)], (4, CAP, LANES)).reshape(LANES, LANES)

        def spread_lanes(kind):
            return jnp.concatenate(split(jnp.where(lane == seat + 32 * kind, facts, 0.0), 3), axis=1)

        place3 = spread_lanes(0)
        place_col = dot(place3, ones).astype(jnp.int32)
        place_row = dot_nt(jnp.ones((8, 3 * LANES), BF16), place3).astype(jnp.int32)[0:1]
        var = dot(spread_lanes(2), ones)
        var_b[at, :] = var
        z_b[at, :] = var * dot(spread_lanes(1), ones)
        for c in range(4):
            cell, group = corner_of(place_col, c)
            group_b[c, at, :] = jnp.where(group == lane // 32, 1.0, 0.0)
            for t in range(cells // LANES):
                pick[c, at, t * LANES:(t + 1) * LANES] = jnp.where(cell == lane + t * LANES, 1.0, 0.0).astype(BF16)
            cell, _ = corner_of(place_row, c)
            there = pl.ds(pl.multiple_of((4 * j + c) * LANES, LANES), LANES)
            pick_t[:, there] = jnp.where(iota((cells, LANES), 0) == cell, 1.0, 0.0).astype(BF16)
        return 0

    lax.fori_loop(0, planes, read_facts, 0)

    def put_terms(j, c):
        at = pl.ds(pl.multiple_of(j * LANES, LANES), LANES)
        there = pl.ds(pl.multiple_of((4 * j + c) * LANES, LANES), LANES)
        hi, lo = split(z_b[at, :] * expanded[c, at, :], 2)
        terms[there, :LANES] = hi
        terms[there, LANES:] = lo

    copy_lanes = jnp.where(
        iota((3 * LANES, 4 * LANES), 0) % LANES == iota((3 * LANES, 4 * LANES), 1) // LANES * 32 + iota((3 * LANES, 4 * LANES), 1) % 32,
        1.0, 0.0).astype(BF16)
    total = jnp.zeros((cells, 2 * LANES), F32)
    for j in range(planes):
        for c in w_copies[max(4 * j - 1, 0):4 * j + 3]:
            c.wait_recv()
        wide = dot(jnp.concatenate(split(wrecv[4 * j:4 * j + 4].reshape(LANES, LANES), 3), axis=1), copy_lanes)
        at = slice(j * LANES, (j + 1) * LANES)
        for c in range(4):
            expanded[c, at, :] = wide[:, c * LANES:(c + 1) * LANES] * group_b[c, at, :]
            put_terms(j, c)
        there = slice(4 * j * LANES, 4 * (j + 1) * LANES)
        total = total + dot(pick_t[:, there], terms[there, :])
    dense[3] = total[:, :LANES] + total[:, LANES:]

    def adjoint(e):
        def one(j, _):
            for c in range(4):
                put_terms(j, c)
            return 0
        lax.fori_loop(0, planes, one, 0)
        total = dot(pick_t[...], terms[...])
        dense[e] = total[:, :LANES] + total[:, LANES:]

    def observe(field, n):
        hi, lo = split(field[...], 2)
        state16[:, :LANES] = hi
        state16[:, LANES:] = lo
        acc[...] = jnp.zeros_like(acc)

        def one(c, _):
            values = dot(pick[c], state16[...])
            acc[...] += (values[:, :LANES] + values[:, LANES:]) * expanded[c]
            return 0

        lax.fori_loop(0, 4, one, 0)
        q = dot(jnp.concatenate(split(acc[...], 2), axis=1), ones[:2 * LANES])
        q_b[n] = q
        z_b[...] = var_b[...] * q

    def r_copies(n):
        return [pltpu.make_async_remote_copy(
            src_ref=sums_send.at[n], dst_ref=sums_region.at[n, i], send_sem=r_send_sem.at[n, i], recv_sem=r_recv_sem.at[n, i],
            device_id=(lax.rem(reg + i, regions), til), device_id_type=MESH) for i in range(1, regions)]

    def t_copies(n):
        return [pltpu.make_async_remote_copy(
            src_ref=sums_mid.at[n], dst_ref=sums_tile.at[n, i], send_sem=t_send_sem.at[n, i], recv_sem=t_recv_sem.at[n, i],
            device_id=(reg, lax.rem(til + i, tiles)), device_id_type=MESH) for i in range(1, tiles)]

    def sums_start(n, sums):
        for i in range(4):
            sums_send[n, i:i + 1, :] = sums[i] if i < len(sums) else jnp.zeros((1, LANES), F32)
        copies = r_copies(n)
        late.extend(copies)
        for c in copies:
            c.start()
        sums_region[n, 0] = sums_send[n]
        return copies

    def sums_middle(n, copies):
        for c in copies:
            c.wait_recv()
        sums_mid[n] = jnp.sum(sums_region[n], axis=0)
        copies = t_copies(n)
        late.extend(copies)
        for c in copies:
            c.start()
        sums_tile[n, 0] = sums_mid[n]
        return copies

    def sums_finish(n, copies):
        for c in copies:
            c.wait_recv()
        return jnp.sum(jnp.sum(sums_tile[n], axis=0), axis=1, keepdims=True)

    def product(a, b):
        return jnp.sum(a * b, axis=0, keepdims=True)

    lane1 = iota((1, LANES), 1)

    def energy(a, b):
        return jnp.where(lane1 == 0, product(var_b[...] * q_b[a], q_b[b]), 0.0)

    copies = halo_start(3)
    build_frame(3, copies, frame_a)
    diffuse(1, 4)
    inner(fields.at[0])
    diffuse(5, 8)
    inner(fields.at[1])

    observe(fields.at[1], 0)
    summing = sums_start(0, (product(fields[0], fields[0]), energy(0, 0)))
    adjoint(4)
    copies = halo_start(4)
    summing = sums_middle(0, summing)
    to_natural(fields.at[0], natural.at[0])
    build_frame(4, copies, frame_a)
    diffuse(1, 4)
    inner(fields.at[2])
    diffuse(5, 8)
    inner(fields.at[4])
    found = sums_finish(0, summing)
    norm_0, energy_0 = found[0:1], found[1:2]
    alpha_0 = norm_0 / (norm_0 + energy_0)
    fields[4] = fields[1] - alpha_0 * (fields[1] + fields[4])

    observe(fields.at[4], 1)
    fields[2] = fields[0] + fields[2]
    fields[3] = fields[0] - alpha_0 * fields[2]
    summing = sums_start(1, (product(fields[3], fields[3]), product(fields[3], fields[0]), energy(1, 1), energy(1, 0)))
    adjoint(5)
    copies = halo_start(5, 4)
    summing = sums_middle(1, summing)
    to_natural(fields.at[2], natural.at[1])
    to_natural(fields.at[3], natural.at[2])
    build_frame(5, copies, frame_a, 4)
    diffuse(5, 8)
    inner(fields.at[5])
    to_natural(fields.at[5], natural.at[3])
    found = sums_finish(1, summing)
    norm_1 = found[0:1]
    beta = norm_1 / norm_0
    curve = norm_1 + 2.0 * beta * found[1:2] + beta * beta * norm_0 + found[2:3] + 2.0 * beta * found[3:4] + beta * beta * energy_0
    alpha_1 = norm_1 / curve
    control_ref[...] = (alpha_0 + alpha_1 * beta) * natural[0] + alpha_1 * natural[2]
    residual_ref[...] = natural[2] - alpha_1 * (natural[2] + natural[3] + beta * natural[1])

    for c in late:
        c.wait_send()


def body(regions, tiles, kx, ky, mask, obs_owner, obs_row, obs_col, obs_weight, innovation, inverse_var):
    levels, rows_x, cols_y = kx.shape
    count = obs_row.shape[0]
    slots = tiles * CAP
    cells = rows_x * cols_y // GROUPS
    line, flat = (1, count), (levels * rows_x, cols_y)
    out = jax.ShapeDtypeStruct((32 * rows_x, cols_y), F32)
    dma = pltpu.SemaphoreType.DMA
    args = (
        kx.reshape(flat), ky.reshape(flat), mask.reshape(flat), obs_owner.reshape(line), obs_row.reshape(line),
        obs_col.reshape(line), innovation.reshape(line), inverse_var.reshape(line), obs_weight,
    )
    control, residual = pl.pallas_call(
        functools.partial(kernel, regions, tiles),
        out_shape=(out, out),
        in_specs=[pl.BlockSpec(memory_space=pl.ANY)] * 9,
        out_specs=[pl.BlockSpec(memory_space=pltpu.VMEM)] * 2,
        scratch_shapes=[
            *[pltpu.VMEM(x.shape, x.dtype) for x in args],
            pltpu.VMEM((EXCHANGES, cells, LANES), F32),
            pltpu.VMEM((EXCHANGES, 2, 32 * HALO, LANES), F32),
            pltpu.VMEM((EXCHANGES, 8, 8, LANES), F32),
            pltpu.VMEM((EXCHANGES, 8, 8, LANES), F32),
            pltpu.VMEM((EXCHANGES, 8, 8, LANES), F32),
            pltpu.VMEM((FRAME, LANES), F32),
            pltpu.VMEM((FRAME, LANES), F32),
            pltpu.VMEM((3, FRAME, LANES), F32),
            pltpu.VMEM((count, 3 * LANES), BF16),
            pltpu.VMEM((tiles, CAP, LANES), F32),
            pltpu.VMEM((tiles, CAP, LANES), F32),
            pltpu.VMEM((tiles, 1, LANES), F32),
            pltpu.VMEM((tiles, 1, LANES), F32),
            pltpu.VMEM((4, slots, LANES), F32),
            pltpu.VMEM((4, slots, cells), BF16),
            pltpu.VMEM((cells, 4 * slots), BF16),
            pltpu.VMEM((4 * slots, 2 * LANES), BF16),
            pltpu.VMEM((slots, LANES), F32),
            pltpu.VMEM((slots, LANES), F32),
            pltpu.VMEM((2, slots, LANES), F32),
            pltpu.VMEM((slots, LANES), F32),
            pltpu.VMEM((4, slots, LANES), F32),
            pltpu.VMEM((cells, 2 * LANES), BF16),
            pltpu.VMEM((6, cells, LANES), F32),
            pltpu.VMEM((4, cells, LANES), F32),
            pltpu.VMEM((2, 4, LANES), F32),
            pltpu.VMEM((2, regions, 4, LANES), F32),
            pltpu.VMEM((2, 4, LANES), F32),
            pltpu.VMEM((2, tiles, 4, LANES), F32),
            dma((9,)), dma((EXCHANGES, 8)), dma((EXCHANGES, 8)),
            dma((tiles,)), dma((tiles,)), dma((tiles,)), dma((tiles,)),
            dma((2, regions)), dma((2, regions)), dma((2, tiles)), dma((2, tiles)),
        ],
        compiler_params=pltpu.CompilerParams(collective_id=0, has_side_effects=True, vmem_limit_bytes=48 * 1024 * 1024),
    )(*args)
    shape = (32 // levels, levels, rows_x, cols_y)
    return control.reshape(shape), residual.reshape(shape)


def solution(mesh):
    return jax.shard_map(
        functools.partial(body, mesh.shape["region"], mesh.shape["tile"]),
        mesh=mesh,
        in_specs=(
            P(None, "region", "tile"),
            P(None, "region", "tile"),
            P(None, "region", "tile"),
            P(("region", "tile"), None),
            P(("region", "tile")),
            P(("region", "tile")),
            P(("region", "tile"), None),
            P(("region", "tile")),
            P(("region", "tile")),
        ),
        out_specs=(P(None, None, "region", "tile"), P(None, None, "region", "tile")),
        check_vma=False,
    )
```

```python
import functools

import jax
import jax.numpy as jnp
from jax import lax
from jax.experimental import pallas as pl
from jax.experimental.pallas import tpu as pltpu
from jax.sharding import PartitionSpec as P

MESH = pl.DeviceIdType.MESH
F32 = jnp.float32
BF16 = jnp.bfloat16
CAP = 32
LANES = 128
GROUPS = 4
HALO = 8
WIDE = HALO + 32 + HALO
TALL = HALO + 16 + HALO
FRAME = (TALL + 1) * WIDE
EXCHANGES = 6


def iota(shape, dim):
    return lax.broadcasted_iota(jnp.int32, shape, dim)


def split(x, parts):
    out = []
    for i in range(parts):
        part = x.astype(BF16)
        out.append(part)
        if i + 1 < parts:
            x = x - part.astype(F32)
    return out


def dot(a, b):
    return jnp.dot(a, b, preferred_element_type=F32)


def dot_nt(a, b):
    return lax.dot_general(a, b, (((1,), (1,)), ((), ())), preferred_element_type=F32)


def swap_blocks(four):
    lane = iota(four[0].shape, 1)
    low = lane < 64
    even = (lane // 32) % 2 == 0
    a, b, c, d = four
    a, c = jnp.where(low, a, pltpu.roll(c, 64, 1)), jnp.where(low, pltpu.roll(a, 64, 1), c)
    b, d = jnp.where(low, b, pltpu.roll(d, 64, 1)), jnp.where(low, pltpu.roll(b, 64, 1), d)
    a, b = jnp.where(even, a, pltpu.roll(b, 32, 1)), jnp.where(even, pltpu.roll(a, 96, 1), b)
    c, d = jnp.where(even, c, pltpu.roll(d, 32, 1)), jnp.where(even, pltpu.roll(c, 96, 1), d)
    return a, b, c, d


def kernel(
    regions, tiles, kx_any, ky_any, mask_any, owner_any, row_any, col_any, innov_any, var_any, weight_any,
    control_ref, residual_ref,
    kx_ref, ky_ref, mask_ref, owner_ref, row_ref, col_ref, innov_ref, var_ref, weight_ref,
    dense, rows_in, left_in, right_in, packed, frame_a, frame_b, coef, wsplit, wsend, wrecv, msend, mrecv, expanded,
    pick, pick_t, terms, var_b, z_b, q_b, acc, group_b, state16, fields, natural, sums_send, sums_region, sums_mid, sums_tile,
    in_sem, halo_send, halo_recv, w_send_sem, w_recv_sem, m_send_sem, m_recv_sem, r_send_sem, r_recv_sem, t_send_sem, t_recv_sem,
):
    reg, til = lax.axis_index("region"), lax.axis_index("tile")
    up, down = lax.rem(reg + regions - 1, regions), lax.rem(reg + 1, regions)
    left, right = lax.rem(til + tiles - 1, tiles), lax.rem(til + 1, tiles)
    count = owner_ref.shape[1]
    slots = tiles * CAP
    planes = tiles // 4
    late = []

    barrier = pltpu.get_barrier_semaphore()
    for i in range(1, tiles):
        pl.semaphore_signal(barrier, inc=1, device_id=(reg, lax.rem(til + i, tiles)), device_id_type=MESH)
    for i in range(1, regions):
        pl.semaphore_signal(barrier, inc=1, device_id=(lax.rem(reg + i, regions), til), device_id_type=MESH)
    for a in (up, down):
        for b in (left, right):
            pl.semaphore_signal(barrier, inc=1, device_id=(a, b), device_id_type=MESH)

    pairs = (
        (mask_any, mask_ref), (kx_any, kx_ref), (ky_any, ky_ref), (owner_any, owner_ref), (row_any, row_ref), (col_any, col_ref),
        (innov_any, innov_ref), (var_any, var_ref), (weight_any, weight_ref),
    )
    loads = [pltpu.make_async_copy(a, b, in_sem.at[i]) for i, (a, b) in enumerate(pairs)]
    for c in loads:
        c.start()
    for c in loads:
        c.wait()
    lane8 = iota((8, LANES), 1)

    def halo_copies(e, deep, fields):
        def copy(n, src, dst, device):
            return pltpu.make_async_remote_copy(
                src_ref=src, dst_ref=dst, send_sem=halo_send.at[e, n], recv_sem=halo_recv.at[e, n],
                device_id=device, device_id_type=MESH)
        size, packs, at = deep * 32, deep // 4, pl.ds(e, fields)
        return [
            copy(4, packed.at[at, pl.ds(0, packs)], left_in.at[at, pl.ds(6, packs)], (up, right)),
            copy(5, packed.at[at, pl.ds(4 - packs, packs)], left_in.at[at, pl.ds(2 - packs, packs)], (down, right)),
            copy(6, packed.at[at, pl.ds(4, packs)], right_in.at[at, pl.ds(6, packs)], (up, left)),
            copy(7, packed.at[at, pl.ds(8 - packs, packs)], right_in.at[at, pl.ds(2 - packs, packs)], (down, left)),
            copy(2, packed.at[at, pl.ds(0, 4)], left_in.at[at, pl.ds(2, 4)], (reg, right)),
            copy(3, packed.at[at, pl.ds(4, 4)], right_in.at[at, pl.ds(2, 4)], (reg, left)),
            copy(0, dense.at[at, pl.ds(0, size)], rows_in.at[at, 1, pl.ds(0, size)], (up, til)),
            copy(1, dense.at[at, pl.ds(512 - size, size)], rows_in.at[at, 0, pl.ds(256 - size, size)], (down, til)),
        ]

    def halo_pack(e):
        for j in range(4):
            first = swap_blocks([dense[e, (4 * j + b) * 32:(4 * j + b) * 32 + 8, :] for b in range(4)])
            last = swap_blocks([dense[e, (4 * j + b) * 32 + 24:(4 * j + b) * 32 + 32, :] for b in range(4)])
            packed[e, j] = last[3]
            packed[e, 4 + j] = first[0]

    def halo_start(e, deep=8, fields=1):
        copies = halo_copies(e, deep, fields)
        late.extend(copies)
        for c in copies:
            c.start()
        return copies

    def frame_own(e, out):
        def four_rows(j, _):
            for b in range(4):
                row = 4 * j + b
                base = pl.multiple_of((row + 8) * WIDE, 8)
                own = dense[e, pl.ds(pl.multiple_of(row * 32, 32), 32), :]
                out[pl.ds(base + 16, 32), :] = own
                out[pl.ds(base + 8, 8), :] = pltpu.roll(own[24:], 32, 1)
                out[pl.ds(base + WIDE, 8), :] = pltpu.roll(own[:8], 96, 1)
            return 0
        lax.fori_loop(0, 4, four_rows, 0)

    def frame_halo(e, out, deep=8):
        if e == 0:
            inside_up = jnp.where(reg > 0, 1.0, 0.0)
            inside_down = jnp.where(reg < regions - 1, 1.0, 0.0)
            rows_in[0, 0] = rows_in[0, 0] * inside_up
            rows_in[0, 1] = rows_in[0, 1] * inside_down
            for side, inside in ((left_in, jnp.where(til > 0, 1.0, 0.0)), (right_in, jnp.where(til < tiles - 1, 1.0, 0.0))):
                for j in range(8):
                    side[0, j] = side[0, j] * (inside * inside_up if j < 2 else inside if j < 6 else inside * inside_down)

        def beside(j, b):
            return pltpu.roll(left_in[e, j], -b * 32 % LANES, 1), pltpu.roll(right_in[e, j], (3 - b) * 32, 1)

        def own_rows(j, _):
            for b in range(4):
                base = pl.multiple_of((4 * j + b) * WIDE, 8)
                start, end = beside(j, b)
                out[pl.ds(base + 8, 8), :] = jnp.where(lane8 < 32, start, out[pl.ds(base + 8, 8), :])
                out[pl.ds(base + WIDE, 8), :] = jnp.where(lane8 >= 96, end, out[pl.ds(base + WIDE, 8), :])
            return 0

        lax.fori_loop(2, 6, own_rows, 0)
        for side in range(2):
            def outer_rows(j, _):
                for b in range(4):
                    row = 4 * j + b
                    base = pl.multiple_of((row + 24 * side) * WIDE, 8)
                    came = rows_in[e, side, pl.ds(pl.multiple_of(row * 32, 32), 32), :]
                    start, end = beside(j + 6 * side, b)
                    out[pl.ds(base + 16, 32), :] = came
                    out[pl.ds(base + 8, 8), :] = jnp.where(lane8 < 32, start, pltpu.roll(came[24:], 32, 1))
                    out[pl.ds(base + WIDE, 8), :] = jnp.where(lane8 >= 96, end, pltpu.roll(came[:8], 96, 1))
                return 0
            lax.fori_loop(0 if side else 2 - deep // 4, deep // 4 if side else 2, outer_rows, 0)

    def build_frame(e, copies, out, deep=8):
        frame_own(e, out)
        for c in copies:
            c.wait_recv()
        frame_halo(e, out, deep)

    def to_cells(source, e):
        def four_rows(j, _):
            lines = [source[pl.ds(4 * j + b, 8, stride=16), :].astype(F32) for b in range(4)]
            many = jnp.concatenate([x for x in lines for _ in range(4)], axis=0).T
            for b, x in enumerate(swap_blocks([many[32 * g:32 * g + 32] for g in range(4)])):
                dense[e, pl.ds(pl.multiple_of((4 * j + b) * 32, 32), 32), :] = x
            return 0
        lax.fori_loop(0, 4, four_rows, 0)

    def to_natural(field, out):
        def four_rows(j, _):
            lines = [field[pl.ds(pl.multiple_of((4 * j + b) * 32, 32), 32), :] for b in range(4)]
            many = jnp.concatenate(swap_blocks(lines), axis=0).T
            for b in range(4):
                out[pl.ds(4 * j + b, 32, stride=16), :] = many[32 * b:32 * b + 32]
            return 0
        lax.fori_loop(0, 4, four_rows, 0)

    for e, source in enumerate((mask_ref, kx_ref, ky_ref)):
        to_cells(source, e)
        halo_pack(e)

    owner = owner_ref[...]
    marks = jnp.where(iota((tiles, count), 0) == owner, 1.0, 0.0)
    upper = jnp.where(iota((count, count), 0) < iota((count, count), 1), 1.0, 0.0).astype(BF16)
    before = dot(marks.astype(BF16), upper)
    slot = owner * CAP + jnp.sum(before * marks, axis=0, keepdims=True).astype(jnp.int32)
    for i, part in enumerate(split(weight_ref[...], 3)):
        wsplit[:, i * LANES:(i + 1) * LANES] = part
    meta_rows = [row_ref[...].astype(F32), col_ref[...].astype(F32)]
    meta_rows += [p.astype(F32) for p in split(innov_ref[...], 3) + split(var_ref[...], 3)]
    meta = jnp.zeros((8, count), F32)
    for i, line in enumerate(meta_rows):
        meta = jnp.where(iota((8, count), 0) == i, line, meta)
    meta = meta.astype(BF16)

    def sort_plane(b, _):
        chosen = jnp.where(iota((LANES, count), 0) + b * LANES == slot, 1.0, 0.0).astype(BF16)
        block = dot(chosen, wsplit[...])
        block = block[:, :LANES] + block[:, LANES:2 * LANES] + block[:, 2 * LANES:]
        wsend[pl.ds(4 * b, 4)] = block.reshape(4, CAP, LANES)
        facts = dot_nt(meta, chosen)
        place = jnp.broadcast_to(facts[0:1] * LANES + facts[1:2], (8, LANES))
        innov = jnp.broadcast_to(facts[2:3] + facts[3:4] + facts[4:5], (8, LANES))
        var = jnp.broadcast_to(facts[5:6] + facts[6:7] + facts[7:8], (8, LANES))
        for k in range(4):
            turned = [pltpu.roll(x, (i - k) * 32 % LANES, 1) for i, x in enumerate((place, innov, var))]
            line = jnp.where(lane8 < 32, turned[0], jnp.where(lane8 < 64, turned[1], jnp.where(lane8 < 96, turned[2], 0.0)))
            msend[4 * b + k] = line[0:1]
        return 0

    lax.fori_loop(0, planes, sort_plane, 0)

    turns = sorted(range(planes), key=lambda i: (min(i, planes - i), i))
    plane, place_in = til // 4, lax.rem(til, 4)

    def sends(src, dst, send_sem, recv_sem):
        out = []
        for j, turn in enumerate(turns):
            for k in range(4):
                if j or k:
                    to = lax.rem(plane + turn, planes) * 4 + lax.rem(place_in + k, 4)
                    n = 4 * j + k
                    out.append(pltpu.make_async_remote_copy(
                        src_ref=src.at[to], dst_ref=dst.at[n], send_sem=send_sem.at[n], recv_sem=recv_sem.at[n],
                        device_id=(reg, to), device_id_type=MESH))
        return out

    m_copies = sends(msend, mrecv, m_send_sem, m_recv_sem)
    w_copies = sends(wsend, wrecv, w_send_sem, w_recv_sem)
    late.extend(m_copies + w_copies)
    pl.semaphore_wait(barrier, (tiles - 1) + (regions - 1) + 4)
    copies = halo_start(0, 8, 3)
    for c in m_copies + w_copies:
        c.start()
    wrecv[0] = wsend[til]
    mrecv[0] = msend[til]

    for e in range(3):
        frame_own(e, coef.at[e])
    for c in copies:
        c.wait_recv()
    for e in range(3):
        frame_halo(e, coef.at[e])

    def make_faces(k, _):
        base = pl.multiple_of(k * WIDE, 8)
        wet = coef[0, pl.ds(base, WIDE), :]
        coef[1, pl.ds(base, WIDE), :] = coef[1, pl.ds(base, WIDE), :] * wet * coef[0, pl.ds(base + WIDE, WIDE), :]
        coef[2, pl.ds(base, WIDE), :] = coef[2, pl.ds(base, WIDE), :] * wet * coef[0, pl.ds(base + 1, WIDE), :]
        return 0

    lax.fori_loop(0, TALL, make_faces, 0)

    def make_centre(k, _):
        base = pl.multiple_of(k * WIDE, 8)
        faces = coef[1, pl.ds(base, WIDE), :] + coef[1, pl.ds(base - WIDE, WIDE), :]
        faces = faces + coef[2, pl.ds(base, WIDE), :] + coef[2, pl.ds(base - 1, WIDE), :]
        coef[0, pl.ds(base, WIDE), :] = coef[0, pl.ds(base, WIDE), :] - faces
        return 0

    lax.fori_loop(1, TALL, make_centre, 0)

    def diffuse(first, last):
        for s in range(first, last + 1):
            src, dst = (frame_a, frame_b) if (s - first) % 2 == 0 else (frame_b, frame_a)

            def line(k, carry):
                before, here, west = carry
                base = pl.multiple_of(k * WIDE, 8)
                after = src[pl.ds(base + WIDE, WIDE), :]
                east = coef[1, pl.ds(base, WIDE), :]
                out = coef[0, pl.ds(base, WIDE), :] * here + east * after + west * before
                out = out + coef[2, pl.ds(base, WIDE), :] * src[pl.ds(base + 1, WIDE), :]
                out = out + coef[2, pl.ds(base - 1, WIDE), :] * src[pl.ds(base - 1, WIDE), :]
                dst[pl.ds(base, WIDE), :] = out
                return here, after, east

            at = (s - 1) * WIDE
            lax.fori_loop(s, TALL + 1 - s, line, (src[at:at + WIDE, :], src[at + WIDE:at + 2 * WIDE, :], coef[1, at:at + WIDE, :]))

    def inner(out):
        for j in range(16):
            out[j * 32:(j + 1) * 32, :] = frame_a[(8 + j) * WIDE + 16:(9 + j) * WIDE, :]

    for c in m_copies:
        c.wait_recv()
    lane = iota((LANES, LANES), 1)
    seat = iota((LANES, LANES), 0) % CAP
    ones = jnp.ones((3 * LANES, LANES), BF16)
    cells = pick.shape[2]

    def corner_of(place, c):
        row = (place >> 7) + c // 2
        col = (place & 127) + c % 2
        return row * 32 + (col & 31), col >> 5

    def read_facts(j, _):
        at = pl.ds(pl.multiple_of(j * LANES, LANES), LANES)
        facts = jnp.broadcast_to(mrecv[pl.ds(4 * j, 4)], (4, CAP, LANES)).reshape(LANES, LANES)

        def spread_lanes(kind):
            return jnp.concatenate(split(jnp.where(lane == seat + 32 * kind, facts, 0.0), 3), axis=1)

        place3 = spread_lanes(0)
        place_col = dot(place3, ones).astype(jnp.int32)
        place_row = dot_nt(jnp.ones((8, 3 * LANES), BF16), place3).astype(jnp.int32)[0:1]
        var = dot(spread_lanes(2), ones)
        var_b[at, :] = var
        z_b[at, :] = var * dot(spread_lanes(1), ones)
        for c in range(4):
            cell, group = corner_of(place_col, c)
            group_b[c, at, :] = jnp.where(group == lane // 32, 1.0, 0.0)
            for t in range(cells // LANES):
                pick[c, at, t * LANES:(t + 1) * LANES] = jnp.where(cell == lane + t * LANES, 1.0, 0.0).astype(BF16)
            cell, _ = corner_of(place_row, c)
            there = pl.ds(pl.multiple_of((4 * j + c) * LANES, LANES), LANES)
            pick_t[:, there] = jnp.where(iota((cells, LANES), 0) == cell, 1.0, 0.0).astype(BF16)
        return 0

    lax.fori_loop(0, planes, read_facts, 0)

    def put_terms(j, c):
        at = pl.ds(pl.multiple_of(j * LANES, LANES), LANES)
        there = pl.ds(pl.multiple_of((4 * j + c) * LANES, LANES), LANES)
        hi, lo = split(z_b[at, :] * expanded[c, at, :], 2)
        terms[there, :LANES] = hi
        terms[there, LANES:] = lo

    copy_lanes = jnp.where(
        iota((3 * LANES, 4 * LANES), 0) % LANES == iota((3 * LANES, 4 * LANES), 1) // LANES * 32 + iota((3 * LANES, 4 * LANES), 1) % 32,
        1.0, 0.0).astype(BF16)
    def take_plane(j, first):
        for k in range(first, 4):
            n = 4 * j + k
            pltpu.make_async_remote_copy(
                src_ref=wsend.at[n], dst_ref=wrecv.at[n], send_sem=w_send_sem.at[n], recv_sem=w_recv_sem.at[n],
                device_id=(reg, left), device_id_type=MESH).wait_recv()
        wide = dot(jnp.concatenate(split(wrecv[pl.ds(4 * j, 4)].reshape(LANES, LANES), 3), axis=1), copy_lanes)
        at = pl.ds(pl.multiple_of(j * LANES, LANES), LANES)
        for c in range(4):
            expanded[c, at, :] = wide[:, c * LANES:(c + 1) * LANES] * group_b[c, at, :]
            put_terms(j, c)
        there = pl.ds(pl.multiple_of(4 * j * LANES, LANES), 4 * LANES)
        part = dot(pick_t[:, there], terms[there, :])
        return part[:, :LANES] + part[:, LANES:]

    dense[3] = take_plane(0, 1)

    def later_plane(j, _):
        dense[3] = dense[3] + take_plane(j, 0)
        return 0

    lax.fori_loop(1, planes, later_plane, 0)

    def adjoint(e):
        def one(j, _):
            for c in range(4):
                put_terms(j, c)
            return 0
        lax.fori_loop(0, planes, one, 0)
        total = dot(pick_t[...], terms[...])
        dense[e] = total[:, :LANES] + total[:, LANES:]

    def observe(field, n):
        hi, lo = split(field[...], 2)
        state16[:, :LANES] = hi
        state16[:, LANES:] = lo
        acc[...] = jnp.zeros_like(acc)

        def one(c, _):
            values = dot(pick[c], state16[...])
            acc[...] += (values[:, :LANES] + values[:, LANES:]) * expanded[c]
            return 0

        lax.fori_loop(0, 4, one, 0)
        q = dot(jnp.concatenate(split(acc[...], 2), axis=1), ones[:2 * LANES])
        q_b[n] = q
        z_b[...] = var_b[...] * q

    def r_copies(n):
        return [pltpu.make_async_remote_copy(
            src_ref=sums_send.at[n], dst_ref=sums_region.at[n, i], send_sem=r_send_sem.at[n, i], recv_sem=r_recv_sem.at[n, i],
            device_id=(lax.rem(reg + i, regions), til), device_id_type=MESH) for i in range(1, regions)]

    def t_copies(n):
        return [pltpu.make_async_remote_copy(
            src_ref=sums_mid.at[n], dst_ref=sums_tile.at[n, i], send_sem=t_send_sem.at[n, i], recv_sem=t_recv_sem.at[n, i],
            device_id=(reg, lax.rem(til + i, tiles)), device_id_type=MESH) for i in range(1, tiles)]

    def sums_start(n, sums):
        for i in range(4):
            sums_send[n, i:i + 1, :] = sums[i] if i < len(sums) else jnp.zeros((1, LANES), F32)
        copies = r_copies(n)
        late.extend(copies)
        for c in copies:
            c.start()
        sums_region[n, 0] = sums_send[n]
        return copies

    def sums_middle(n, copies):
        for c in copies:
            c.wait_recv()
        sums_mid[n] = jnp.sum(sums_region[n], axis=0)
        copies = t_copies(n)
        late.extend(copies)
        for c in copies:
            c.start()
        sums_tile[n, 0] = sums_mid[n]
        return copies

    def sums_finish(n, copies):
        for c in copies:
            c.wait_recv()
        return jnp.sum(jnp.sum(sums_tile[n], axis=0), axis=1, keepdims=True)

    def product(a, b):
        return jnp.sum(a * b, axis=0, keepdims=True)

    lane1 = iota((1, LANES), 1)

    def energy(a, b):
        return jnp.where(lane1 == 0, product(var_b[...] * q_b[a], q_b[b]), 0.0)

    halo_pack(3)
    copies = halo_start(3)
    build_frame(3, copies, frame_a)
    diffuse(1, 4)
    inner(fields.at[0])
    diffuse(5, 8)
    inner(fields.at[1])

    observe(fields.at[1], 0)
    summing = sums_start(0, (product(fields[0], fields[0]), energy(0, 0)))
    adjoint(4)
    halo_pack(4)
    copies = halo_start(4)
    summing = sums_middle(0, summing)
    to_natural(fields.at[0], natural.at[0])
    build_frame(4, copies, frame_a)
    diffuse(1, 4)
    inner(fields.at[2])
    diffuse(5, 8)
    inner(fields.at[4])
    found = sums_finish(0, summing)
    norm_0, energy_0 = found[0:1], found[1:2]
    alpha_0 = norm_0 / (norm_0 + energy_0)
    fields[4] = fields[1] - alpha_0 * (fields[1] + fields[4])

    observe(fields.at[4], 1)
    fields[2] = fields[0] + fields[2]
    fields[3] = fields[0] - alpha_0 * fields[2]
    summing = sums_start(1, (product(fields[3], fields[3]), product(fields[3], fields[0]), energy(1, 1), energy(1, 0)))
    adjoint(5)
    halo_pack(5)
    copies = halo_start(5, 4)
    summing = sums_middle(1, summing)
    to_natural(fields.at[2], natural.at[1])
    to_natural(fields.at[3], natural.at[2])
    build_frame(5, copies, frame_a, 4)
    diffuse(5, 8)
    inner(fields.at[5])
    to_natural(fields.at[5], natural.at[3])
    found = sums_finish(1, summing)
    norm_1 = found[0:1]
    beta = norm_1 / norm_0
    curve = norm_1 + 2.0 * beta * found[1:2] + beta * beta * norm_0 + found[2:3] + 2.0 * beta * found[3:4] + beta * beta * energy_0
    alpha_1 = norm_1 / curve
    control_ref[...] = (alpha_0 + alpha_1 * beta) * natural[0] + alpha_1 * natural[2]
    residual_ref[...] = natural[2] - alpha_1 * (natural[2] + natural[3] + beta * natural[1])

    for c in late:
        c.wait_send()


def body(regions, tiles, kx, ky, mask, obs_owner, obs_row, obs_col, obs_weight, innovation, inverse_var):
    levels, rows_x, cols_y = kx.shape
    count = obs_row.shape[0]
    slots = tiles * CAP
    cells = rows_x * cols_y // GROUPS
    line, flat = (1, count), (levels * rows_x, cols_y)
    out = jax.ShapeDtypeStruct((32 * rows_x, cols_y), F32)
    dma = pltpu.SemaphoreType.DMA
    args = (
        kx.reshape(flat), ky.reshape(flat), mask.reshape(flat), obs_owner.reshape(line), obs_row.reshape(line),
        obs_col.reshape(line), innovation.reshape(line), inverse_var.reshape(line), obs_weight,
    )
    control, residual = pl.pallas_call(
        functools.partial(kernel, regions, tiles),
        out_shape=(out, out),
        in_specs=[pl.BlockSpec(memory_space=pl.ANY)] * 9,
        out_specs=[pl.BlockSpec(memory_space=pltpu.VMEM)] * 2,
        scratch_shapes=[
            *[pltpu.VMEM(x.shape, x.dtype) for x in args],
            pltpu.VMEM((EXCHANGES, cells, LANES), F32),
            pltpu.VMEM((EXCHANGES, 2, 32 * HALO, LANES), F32),
            pltpu.VMEM((EXCHANGES, 8, 8, LANES), F32),
            pltpu.VMEM((EXCHANGES, 8, 8, LANES), F32),
            pltpu.VMEM((EXCHANGES, 8, 8, LANES), F32),
            pltpu.VMEM((FRAME, LANES), F32),
            pltpu.VMEM((FRAME, LANES), F32),
            pltpu.VMEM((3, FRAME, LANES), F32),
            pltpu.VMEM((count, 3 * LANES), BF16),
            pltpu.VMEM((tiles, CAP, LANES), F32),
            pltpu.VMEM((tiles, CAP, LANES), F32),
            pltpu.VMEM((tiles, 1, LANES), F32),
            pltpu.VMEM((tiles, 1, LANES), F32),
            pltpu.VMEM((4, slots, LANES), F32),
            pltpu.VMEM((4, slots, cells), BF16),
            pltpu.VMEM((cells, 4 * slots), BF16),
            pltpu.VMEM((4 * slots, 2 * LANES), BF16),
            pltpu.VMEM((slots, LANES), F32),
            pltpu.VMEM((slots, LANES), F32),
            pltpu.VMEM((2, slots, LANES), F32),
            pltpu.VMEM((slots, LANES), F32),
            pltpu.VMEM((4, slots, LANES), F32),
            pltpu.VMEM((cells, 2 * LANES), BF16),
            pltpu.VMEM((6, cells, LANES), F32),
            pltpu.VMEM((4, cells, LANES), F32),
            pltpu.VMEM((2, 4, LANES), F32),
            pltpu.VMEM((2, regions, 4, LANES), F32),
            pltpu.VMEM((2, 4, LANES), F32),
            pltpu.VMEM((2, tiles, 4, LANES), F32),
            dma((9,)), dma((EXCHANGES, 8)), dma((EXCHANGES, 8)),
            dma((tiles,)), dma((tiles,)), dma((tiles,)), dma((tiles,)),
            dma((2, regions)), dma((2, regions)), dma((2, tiles)), dma((2, tiles)),
        ],
        compiler_params=pltpu.CompilerParams(collective_id=0, has_side_effects=True, vmem_limit_bytes=60 * 1024 * 1024),
    )(*args)
    shape = (32 // levels, levels, rows_x, cols_y)
    return control.reshape(shape), residual.reshape(shape)


def solution(mesh):
    return jax.shard_map(
        functools.partial(body, mesh.shape["region"], mesh.shape["tile"]),
        mesh=mesh,
        in_specs=(
            P(None, "region", "tile"),
            P(None, "region", "tile"),
            P(None, "region", "tile"),
            P(("region", "tile"), None),
            P(("region", "tile")),
            P(("region", "tile")),
            P(("region", "tile"), None),
            P(("region", "tile")),
            P(("region", "tile")),
        ),
        out_specs=(P(None, None, "region", "tile"), P(None, None, "region", "tile")),
        check_vma=False,
    )
```

```python
import functools

import jax
import jax.numpy as jnp
from jax import lax
from jax.experimental import pallas as pl
from jax.experimental.pallas import tpu as pltpu
from jax.sharding import PartitionSpec as P

MESH = pl.DeviceIdType.MESH
F32 = jnp.float32
BF16 = jnp.bfloat16
CAP = 32
LANES = 128
GROUPS = 4
HALO = 8
WIDE = HALO + 32 + HALO
TALL = HALO + 16 + HALO
ROWS_AT_ONCE = 3
FRAME = (TALL + 3) * WIDE
EXCHANGES = 6


def iota(shape, dim):
    return lax.broadcasted_iota(jnp.int32, shape, dim)


def split(x, parts):
    out = []
    for i in range(parts):
        part = x.astype(BF16)
        out.append(part)
        if i + 1 < parts:
            x = x - part.astype(F32)
    return out


def dot(a, b):
    return jnp.dot(a, b, preferred_element_type=F32)


def dot_nt(a, b):
    return lax.dot_general(a, b, (((1,), (1,)), ((), ())), preferred_element_type=F32)


def swap_blocks(four):
    lane = iota(four[0].shape, 1)
    low = lane < 64
    even = (lane // 32) % 2 == 0
    a, b, c, d = four
    a, c = jnp.where(low, a, pltpu.roll(c, 64, 1)), jnp.where(low, pltpu.roll(a, 64, 1), c)
    b, d = jnp.where(low, b, pltpu.roll(d, 64, 1)), jnp.where(low, pltpu.roll(b, 64, 1), d)
    a, b = jnp.where(even, a, pltpu.roll(b, 32, 1)), jnp.where(even, pltpu.roll(a, 96, 1), b)
    c, d = jnp.where(even, c, pltpu.roll(d, 32, 1)), jnp.where(even, pltpu.roll(c, 96, 1), d)
    return a, b, c, d


def kernel(
    regions, tiles, kx_any, ky_any, mask_any, owner_any, row_any, col_any, innov_any, var_any, weight_any,
    control_ref, residual_ref,
    kx_ref, ky_ref, mask_ref, owner_ref, row_ref, col_ref, innov_ref, var_ref, weight_ref,
    dense, rows_in, left_in, right_in, packed, frame_a, frame_b, coef, wsplit, wsend, wrecv, msend, mrecv, expanded, expanded_0, coef_rows, coef_in,
    pick, pick_t, terms, var_b, z_b, q_b, acc, group_b, state16, fields, natural, sums_send, sums_region, sums_mid, sums_tile,
    in_sem, halo_send, halo_recv, w_send_sem, w_recv_sem, m_send_sem, m_recv_sem, r_send_sem, r_recv_sem, t_send_sem, t_recv_sem,
):
    reg, til = lax.axis_index("region"), lax.axis_index("tile")
    up, down = lax.rem(reg + regions - 1, regions), lax.rem(reg + 1, regions)
    left, right = lax.rem(til + tiles - 1, tiles), lax.rem(til + 1, tiles)
    count = owner_ref.shape[1]
    slots = tiles * CAP
    planes = tiles // 4
    late = []

    barrier = pltpu.get_barrier_semaphore()
    for i in sorted(range(1, tiles), key=lambda i: -min(i, tiles - i)):
        pl.semaphore_signal(barrier, inc=1, device_id=(reg, lax.rem(til + i, tiles)), device_id_type=MESH)
    for i in range(1, regions):
        pl.semaphore_signal(barrier, inc=1, device_id=(lax.rem(reg + i, regions), til), device_id_type=MESH)
    for a in (up, down):
        for b in (left, right):
            pl.semaphore_signal(barrier, inc=1, device_id=(a, b), device_id_type=MESH)

    pairs = (
        (mask_any, mask_ref), (kx_any, kx_ref), (ky_any, ky_ref), (owner_any, owner_ref), (row_any, row_ref), (col_any, col_ref),
        (innov_any, innov_ref), (var_any, var_ref), (weight_any, weight_ref),
    )
    loads = [pltpu.make_async_copy(a, b, in_sem.at[i]) for i, (a, b) in enumerate(pairs)]
    for c in loads:
        c.start()
    for c in loads:
        c.wait()
    lane8 = iota((8, LANES), 1)

    def halo_copies(e, deep, fields):
        def copy(n, src, dst, device):
            return pltpu.make_async_remote_copy(
                src_ref=src, dst_ref=dst, send_sem=halo_send.at[e, n], recv_sem=halo_recv.at[e, n],
                device_id=device, device_id_type=MESH)
        size, packs, at = deep * 32, deep // 4, pl.ds(e, fields)
        return [
            copy(4, packed.at[at, pl.ds(0, packs)], left_in.at[at, pl.ds(6, packs)], (up, right)),
            copy(5, packed.at[at, pl.ds(4 - packs, packs)], left_in.at[at, pl.ds(2 - packs, packs)], (down, right)),
            copy(6, packed.at[at, pl.ds(4, packs)], right_in.at[at, pl.ds(6, packs)], (up, left)),
            copy(7, packed.at[at, pl.ds(8 - packs, packs)], right_in.at[at, pl.ds(2 - packs, packs)], (down, left)),
            copy(2, packed.at[at, pl.ds(0, 4)], left_in.at[at, pl.ds(2, 4)], (reg, right)),
            copy(3, packed.at[at, pl.ds(4, 4)], right_in.at[at, pl.ds(2, 4)], (reg, left)),
            copy(0, coef_rows.at[pl.ds(0, 8)], coef_in.at[1], (up, til)) if e == 0 else
            copy(0, dense.at[e, pl.ds(0, size)], rows_in.at[e, 1, pl.ds(0, size)], (up, til)),
            copy(1, coef_rows.at[pl.ds(8, 8)], coef_in.at[0], (down, til)) if e == 0 else
            copy(1, dense.at[e, pl.ds(512 - size, size)], rows_in.at[e, 0, pl.ds(256 - size, size)], (down, til)),
        ]

    def halo_pack(e):
        for j in range(4):
            first = swap_blocks([dense[e, (4 * j + b) * 32:(4 * j + b) * 32 + 8, :] for b in range(4)])
            last = swap_blocks([dense[e, (4 * j + b) * 32 + 24:(4 * j + b) * 32 + 32, :] for b in range(4)])
            packed[e, j] = last[3]
            packed[e, 4 + j] = first[0]

    def halo_start(e, deep=8, fields=1):
        copies = halo_copies(e, deep, fields)
        late.extend(copies)
        for c in copies:
            c.start()
        return copies

    def frame_own(e, out):
        def four_rows(j, _):
            for b in range(4):
                row = 4 * j + b
                base = pl.multiple_of((row + 8) * WIDE, 8)
                own = dense[e, pl.ds(pl.multiple_of(row * 32, 32), 32), :]
                out[pl.ds(base + 16, 32), :] = own
                out[pl.ds(base + 8, 8), :] = pltpu.roll(own[24:], 32, 1)
                out[pl.ds(base + WIDE, 8), :] = pltpu.roll(own[:8], 96, 1)
            return 0
        lax.fori_loop(0, 4, four_rows, 0)

    def frame_halo(e, out, deep=8):
        if e == 0:
            inside_up = jnp.where(reg > 0, 1.0, 0.0)
            inside_down = jnp.where(reg < regions - 1, 1.0, 0.0)
            rows_in[0, 0] = rows_in[0, 0] * inside_up
            rows_in[0, 1] = rows_in[0, 1] * inside_down
            for side, inside in ((left_in, jnp.where(til > 0, 1.0, 0.0)), (right_in, jnp.where(til < tiles - 1, 1.0, 0.0))):
                for j in range(8):
                    side[0, j] = side[0, j] * (inside * inside_up if j < 2 else inside if j < 6 else inside * inside_down)

        def beside(j, b):
            return pltpu.roll(left_in[e, j], -b * 32 % LANES, 1), pltpu.roll(right_in[e, j], (3 - b) * 32, 1)

        def own_rows(j, _):
            for b in range(4):
                base = pl.multiple_of((4 * j + b) * WIDE, 8)
                start, end = beside(j, b)
                out[pl.ds(base + 8, 8), :] = jnp.where(lane8 < 32, start, out[pl.ds(base + 8, 8), :])
                out[pl.ds(base + WIDE, 8), :] = jnp.where(lane8 >= 96, end, out[pl.ds(base + WIDE, 8), :])
            return 0

        lax.fori_loop(2, 6, own_rows, 0)
        for side in range(2):
            def outer_rows(j, _):
                for b in range(4):
                    row = 4 * j + b
                    base = pl.multiple_of((row + 24 * side) * WIDE, 8)
                    came = rows_in[e, side, pl.ds(pl.multiple_of(row * 32, 32), 32), :]
                    start, end = beside(j + 6 * side, b)
                    out[pl.ds(base + 16, 32), :] = came
                    out[pl.ds(base + 8, 8), :] = jnp.where(lane8 < 32, start, pltpu.roll(came[24:], 32, 1))
                    out[pl.ds(base + WIDE, 8), :] = jnp.where(lane8 >= 96, end, pltpu.roll(came[:8], 96, 1))
                return 0
            lax.fori_loop(0 if side else 2 - deep // 4, deep // 4 if side else 2, outer_rows, 0)

    def build_frame(e, copies, out, deep=8):
        frame_own(e, out)
        drain()
        for c in copies:
            c.wait_recv()
        frame_halo(e, out, deep)

    def to_cells(line, out, rows):
        def four_rows(j, _):
            lines = [line(4 * j + b) for b in range(4)]
            many = jnp.concatenate([x for x in lines for _ in range(4)], axis=0).T
            for b, x in enumerate(swap_blocks([many[32 * g:32 * g + 32] for g in range(4)])):
                out[pl.ds(pl.multiple_of((4 * j + b) * 32, 32), 32), :] = x
            return 0
        lax.fori_loop(0, rows // 4, four_rows, 0)

    def to_natural(field, out):
        def four_rows(j, _):
            lines = [field[pl.ds(pl.multiple_of((4 * j + b) * 32, 32), 32), :] for b in range(4)]
            many = jnp.concatenate(swap_blocks(lines), axis=0).T
            for b in range(4):
                out[pl.ds(4 * j + b, 32, stride=16), :] = many[32 * b:32 * b + 32]
            return 0
        lax.fori_loop(0, 4, four_rows, 0)

    def stage(r, _):
        for e, source in enumerate((mask_ref, kx_ref, ky_ref)):
            coef_rows[r, 8 * e:8 * e + 8, :] = source[pl.ds(r, 8, stride=16), :].astype(F32)
        return 0

    lax.fori_loop(0, 16, stage, 0)
    for e in range(3):
        to_cells(lambda r: coef_rows[r, 8 * e:8 * e + 8, :], dense.at[e], 16)
        halo_pack(e)

    owner = owner_ref[...]
    marks = jnp.where(iota((tiles, count), 0) == owner, 1.0, 0.0)
    upper = jnp.where(iota((count, count), 0) < iota((count, count), 1), 1.0, 0.0).astype(BF16)
    before = dot(marks.astype(BF16), upper)
    slot = owner * CAP + jnp.sum(before * marks, axis=0, keepdims=True).astype(jnp.int32)
    for i, part in enumerate(split(weight_ref[...], 3)):
        wsplit[:, i * LANES:(i + 1) * LANES] = part
    meta_rows = [row_ref[...].astype(F32), col_ref[...].astype(F32)]
    meta_rows += [p.astype(F32) for p in split(innov_ref[...], 3) + split(var_ref[...], 3)]
    meta = jnp.zeros((8, count), F32)
    for i, line in enumerate(meta_rows):
        meta = jnp.where(iota((8, count), 0) == i, line, meta)
    meta = meta.astype(BF16)

    def sort_plane(b, _):
        chosen = jnp.where(iota((LANES, count), 0) + b * LANES == slot, 1.0, 0.0).astype(BF16)
        block = dot(chosen, wsplit[...])
        block = block[:, :LANES] + block[:, LANES:2 * LANES] + block[:, 2 * LANES:]
        wsend[pl.ds(4 * b, 4)] = block.reshape(4, CAP, LANES)
        facts = dot_nt(meta, chosen)
        place = jnp.broadcast_to(facts[0:1] * LANES + facts[1:2], (8, LANES))
        innov = jnp.broadcast_to(facts[2:3] + facts[3:4] + facts[4:5], (8, LANES))
        var = jnp.broadcast_to(facts[5:6] + facts[6:7] + facts[7:8], (8, LANES))
        for k in range(4):
            turned = [pltpu.roll(x, (i - k) * 32 % LANES, 1) for i, x in enumerate((place, innov, var))]
            line = jnp.where(lane8 < 32, turned[0], jnp.where(lane8 < 64, turned[1], jnp.where(lane8 < 96, turned[2], 0.0)))
            msend[4 * b + k] = line[0:1]
        return 0

    lax.fori_loop(0, planes, sort_plane, 0)

    turns = sorted(range(planes), key=lambda i: (min(i, planes - i), i))
    plane, place_in = til // 4, lax.rem(til, 4)

    def sends(src, dst, send_sem, recv_sem):
        out = []
        for j, turn in enumerate(turns):
            for k in range(4):
                if j or k:
                    to = lax.rem(plane + turn, planes) * 4 + lax.rem(place_in + k, 4)
                    n = 4 * j + k
                    out.append(pltpu.make_async_remote_copy(
                        src_ref=src.at[to], dst_ref=dst.at[n], send_sem=send_sem.at[n], recv_sem=recv_sem.at[n],
                        device_id=(reg, to), device_id_type=MESH))
        return out

    def both_ways(copies):
        order = list(range(3))
        for j in range(1, planes, 2):
            order += [4 * i + k - 1 for k in range(4) for i in (j, j + 1) if i < planes]
        return [copies[i] for i in order]

    m_copies = sends(msend, mrecv, m_send_sem, m_recv_sem)
    w_copies = sends(wsend, wrecv, w_send_sem, w_recv_sem)
    late.extend(m_copies + w_copies)
    def drain():
        for c in late:
            c.wait_send()
        late.clear()

    pl.semaphore_wait(barrier, (tiles - 1) + (regions - 1) + 4)
    copies = halo_start(0, 8, 3)
    for c in both_ways(m_copies) + both_ways(w_copies):
        c.start()
    wrecv[0] = wsend[til]
    mrecv[0] = msend[til]

    for e in range(3):
        frame_own(e, coef.at[e])
    for c in copies:
        c.wait_recv()
    for e in range(3):
        for side in range(2):
            to_cells(lambda r: coef_in[side, r, 8 * e:8 * e + 8, :], rows_in.at[e, side], 8)
        frame_halo(e, coef.at[e])

    def make_faces(k, _):
        base = pl.multiple_of(k * WIDE, 8)
        wet = coef[0, pl.ds(base, WIDE), :]
        coef[1, pl.ds(base, WIDE), :] = coef[1, pl.ds(base, WIDE), :] * wet * coef[0, pl.ds(base + WIDE, WIDE), :]
        coef[2, pl.ds(base, WIDE), :] = coef[2, pl.ds(base, WIDE), :] * wet * coef[0, pl.ds(base + 1, WIDE), :]
        return 0

    lax.fori_loop(0, TALL, make_faces, 0)

    def make_centre(k, _):
        base = pl.multiple_of(k * WIDE, 8)
        faces = coef[1, pl.ds(base, WIDE), :] + coef[1, pl.ds(base - WIDE, WIDE), :]
        faces = faces + coef[2, pl.ds(base, WIDE), :] + coef[2, pl.ds(base - 1, WIDE), :]
        coef[0, pl.ds(base, WIDE), :] = coef[0, pl.ds(base, WIDE), :] - faces
        return 0

    lax.fori_loop(1, TALL, make_centre, 0)

    def diffuse(first, last):
        for s in range(first, last + 1):
            src, dst = (frame_a, frame_b) if (s - first) % 2 == 0 else (frame_b, frame_a)

            def lines(i, carry):
                before, here, west = carry
                base = pl.multiple_of((s + ROWS_AT_ONCE * i) * WIDE, 8)
                for u in range(ROWS_AT_ONCE):
                    at = base + u * WIDE
                    after = src[pl.ds(at + WIDE, WIDE), :]
                    east = coef[1, pl.ds(at, WIDE), :]
                    out = (coef[0, pl.ds(at, WIDE), :] * here + east * after) + west * before
                    dst[pl.ds(at, WIDE), :] = out + (
                        coef[2, pl.ds(at, WIDE), :] * src[pl.ds(at + 1, WIDE), :]
                        + coef[2, pl.ds(at - 1, WIDE), :] * src[pl.ds(at - 1, WIDE), :])
                    before, here, west = here, after, east
                return before, here, west

            at = (s - 1) * WIDE
            rows = 16 if s == HALO else TALL + 1 - 2 * s
            lax.fori_loop(
                0, -(-rows // ROWS_AT_ONCE), lines, (src[at:at + WIDE, :], src[at + WIDE:at + 2 * WIDE, :], coef[1, at:at + WIDE, :]))

    def inner(out):
        for j in range(16):
            out[j * 32:(j + 1) * 32, :] = frame_a[(8 + j) * WIDE + 16:(9 + j) * WIDE, :]

    for c in m_copies:
        c.wait_recv()
    lane = iota((LANES, LANES), 1)
    seat = iota((LANES, LANES), 0) % CAP
    ones = jnp.ones((3 * LANES, LANES), BF16)
    cells = pick_t.shape[0]

    def corner_of(place, c):
        row = (place >> 7) + c // 2
        col = (place & 127) + c % 2
        return row * 32 + (col & 31), col >> 5

    def read_facts(j, _):
        at = pl.ds(pl.multiple_of(j * LANES, LANES), LANES)
        facts = jnp.broadcast_to(mrecv[pl.ds(4 * j, 4)], (4, CAP, LANES)).reshape(LANES, LANES)

        def spread_lanes(kind):
            return jnp.concatenate(split(jnp.where(lane == seat + 32 * kind, facts, 0.0), 3), axis=1)

        place3 = spread_lanes(0)
        place_col = dot(place3, ones).astype(jnp.int32)
        place_row = dot_nt(jnp.ones((8, 3 * LANES), BF16), place3).astype(jnp.int32)[0:1]
        var = dot(spread_lanes(2), ones)
        var_b[at, :] = var
        z_b[at, :] = var * dot(spread_lanes(1), ones)
        for c in range(4):
            cell, group = corner_of(place_col, c)
            group_b[c, at, :] = jnp.where(group == lane // 32, 1.0, 0.0)
            if c == 0:
                for t in range(cells // LANES):
                    hit = jnp.where(cell == lane + t * LANES, 1.0, 0.0).astype(BF16)
                    pick[at, t * LANES:(t + 1) * LANES] = hit
                    pick[at, cells + t * LANES:cells + (t + 1) * LANES] = hit
            cell, _ = corner_of(place_row, c)
            there = pl.ds(pl.multiple_of((4 * j + c) * LANES, LANES), LANES)
            pick_t[:, there] = jnp.where(iota((cells, LANES), 0) == cell, 1.0, 0.0).astype(BF16)
        return 0

    lax.fori_loop(0, planes, read_facts, 0)

    def put_terms(j, c):
        at = pl.ds(pl.multiple_of(j * LANES, LANES), LANES)
        there = pl.ds(pl.multiple_of((4 * j + c) * LANES, LANES), LANES)
        hi, lo = split(z_b[at, :] * expanded[c, at, :], 2)
        terms[there, :LANES] = hi
        terms[there, LANES:] = lo

    copy_lanes = jnp.where(
        iota((3 * LANES, 4 * LANES), 0) % LANES == iota((3 * LANES, 4 * LANES), 1) // LANES * 32 + iota((3 * LANES, 4 * LANES), 1) % 32,
        1.0, 0.0).astype(BF16)
    def take_plane(j, first):
        for k in range(first, 4):
            n = 4 * j + k
            pltpu.make_async_remote_copy(
                src_ref=wsend.at[n], dst_ref=wrecv.at[n], send_sem=w_send_sem.at[n], recv_sem=w_recv_sem.at[n],
                device_id=(reg, left), device_id_type=MESH).wait_recv()
        wide = dot(jnp.concatenate(split(wrecv[pl.ds(4 * j, 4)].reshape(LANES, LANES), 3), axis=1), copy_lanes)
        at = pl.ds(pl.multiple_of(j * LANES, LANES), LANES)
        for c in range(4):
            expanded[c, at, :] = wide[:, c * LANES:(c + 1) * LANES] * group_b[c, at, :]
            expanded_0[c, at, :] = wide[:, c * LANES:(c + 1) * LANES] * group_b[0, at, :]
            put_terms(j, c)
        there = pl.ds(pl.multiple_of(4 * j * LANES, LANES), 4 * LANES)
        part = dot(pick_t[:, there], terms[there, :])
        return part[:, :LANES] + part[:, LANES:]

    state16[...] = jnp.zeros_like(state16)
    dense[3] = take_plane(0, 1)

    def later_plane(j, _):
        dense[3] = dense[3] + take_plane(j, 0)
        return 0

    lax.fori_loop(1, planes, later_plane, 0)

    def adjoint(e):
        def one(j, _):
            for c in range(4):
                put_terms(j, c)
            return 0
        lax.fori_loop(0, planes, one, 0)
        total = dot(pick_t[...], terms[...])
        dense[e] = total[:, :LANES] + total[:, LANES:]

    def observe(field, n):
        def corners(r, _):
            at = pl.multiple_of(r * 32, 32)
            here = field[pl.ds(at, 32), :]
            past = jnp.broadcast_to(pltpu.roll(here[:8], 96, 1)[0:1], (32, LANES))
            beside = jnp.where(iota((32, LANES), 0) == 31, past, field[pl.ds(at + 1, 32), :])
            above = pl.multiple_of(jnp.maximum(at - 32, 0), 32)
            for c, value in enumerate((here, beside)):
                for h, part in enumerate(split(value, 2)):
                    state16[pl.ds(h * cells + at, 32), c * LANES:(c + 1) * LANES] = part
                    state16[pl.ds(h * cells + above, 32), (2 + c) * LANES:(3 + c) * LANES] = part
            return 0

        lax.fori_loop(0, 16, corners, 0)
        acc[...] = jnp.zeros_like(acc)

        def one(i, _):
            values = dot(pick[...], state16[:, pl.ds(pl.multiple_of(i * 2 * LANES, LANES), 2 * LANES)])
            acc[...] += values[:, :LANES] * expanded_0[2 * i] + values[:, LANES:] * expanded_0[2 * i + 1]
            return 0

        lax.fori_loop(0, 2, one, 0)
        q = jnp.broadcast_to(jnp.sum(acc[...], axis=1, keepdims=True), acc.shape)
        q_b[n] = q
        z_b[...] = var_b[...] * q

    def r_copies(n):
        return [pltpu.make_async_remote_copy(
            src_ref=sums_send.at[n], dst_ref=sums_region.at[n, i], send_sem=r_send_sem.at[n, i], recv_sem=r_recv_sem.at[n, i],
            device_id=(lax.rem(reg + i, regions), til), device_id_type=MESH) for i in range(1, regions)]

    def t_copies(n):
        return [pltpu.make_async_remote_copy(
            src_ref=sums_mid.at[n], dst_ref=sums_tile.at[n, i], send_sem=t_send_sem.at[n, i], recv_sem=t_recv_sem.at[n, i],
            device_id=(reg, lax.rem(til + i, tiles)), device_id_type=MESH) for i in range(1, tiles)]

    def sums_start(n, sums):
        for i in range(4):
            sums_send[n, i:i + 1, :] = sums[i] if i < len(sums) else jnp.zeros((1, LANES), F32)
        copies = r_copies(n)
        late.extend(copies)
        for c in copies:
            c.start()
        sums_region[n, 0] = sums_send[n]
        return copies

    def sums_middle(n, copies):
        for c in copies:
            c.wait_recv()
        sums_mid[n] = jnp.sum(sums_region[n], axis=0)
        copies = t_copies(n)
        late.extend(copies)
        for c in copies:
            c.start()
        sums_tile[n, 0] = sums_mid[n]
        return copies

    def sums_finish(n, copies):
        for c in copies:
            c.wait_recv()
        return jnp.sum(jnp.sum(sums_tile[n], axis=0), axis=1, keepdims=True)

    def product(a, b):
        return jnp.sum(a * b, axis=0, keepdims=True)

    lane1 = iota((1, LANES), 1)

    def energy(a, b):
        return jnp.where(lane1 == 0, product(var_b[...] * q_b[a], q_b[b]), 0.0)

    halo_pack(3)
    copies = halo_start(3)
    build_frame(3, copies, frame_a)
    diffuse(1, 4)
    inner(fields.at[0])
    diffuse(5, 8)
    inner(fields.at[1])

    observe(fields.at[1], 0)
    summing = sums_start(0, (product(fields[0, :512, :], fields[0, :512, :]), energy(0, 0)))
    adjoint(4)
    halo_pack(4)
    copies = halo_start(4)
    summing = sums_middle(0, summing)
    to_natural(fields.at[0], natural.at[0])
    build_frame(4, copies, frame_a)
    diffuse(1, 4)
    inner(fields.at[2])
    diffuse(5, 8)
    inner(fields.at[4])
    found = sums_finish(0, summing)
    norm_0, energy_0 = found[0:1], found[1:2]
    alpha_0 = norm_0 / (norm_0 + energy_0)
    fields[4, :512, :] = fields[1, :512, :] - alpha_0 * (fields[1, :512, :] + fields[4, :512, :])

    observe(fields.at[4], 1)
    fields[2, :512, :] = fields[0, :512, :] + fields[2, :512, :]
    fields[3, :512, :] = fields[0, :512, :] - alpha_0 * fields[2, :512, :]
    summing = sums_start(1, (product(fields[3, :512, :], fields[3, :512, :]), product(fields[3, :512, :], fields[0, :512, :]), energy(1, 1), energy(1, 0)))
    adjoint(5)
    halo_pack(5)
    copies = halo_start(5, 4)
    summing = sums_middle(1, summing)
    to_natural(fields.at[2], natural.at[1])
    to_natural(fields.at[3], natural.at[2])
    build_frame(5, copies, frame_a, 4)
    diffuse(5, 8)
    inner(fields.at[5])
    to_natural(fields.at[5], natural.at[3])
    drain()
    found = sums_finish(1, summing)
    norm_1 = found[0:1]
    beta = norm_1 / norm_0
    curve = norm_1 + 2.0 * beta * found[1:2] + beta * beta * norm_0 + found[2:3] + 2.0 * beta * found[3:4] + beta * beta * energy_0
    alpha_1 = norm_1 / curve
    control_ref[...] = (alpha_0 + alpha_1 * beta) * natural[0] + alpha_1 * natural[2]
    residual_ref[...] = natural[2] - alpha_1 * (natural[2] + natural[3] + beta * natural[1])


def hand_over(control, residual, control_out, residual_out, sem):
    copies = [pltpu.make_async_copy(control, control_out, sem.at[0]), pltpu.make_async_copy(residual, residual_out, sem.at[1])]
    for c in copies:
        c.start()
    for c in copies:
        c.wait()


def body(regions, tiles, kx, ky, mask, obs_owner, obs_row, obs_col, obs_weight, innovation, inverse_var):
    levels, rows_x, cols_y = kx.shape
    count = obs_row.shape[0]
    slots = tiles * CAP
    cells = rows_x * cols_y // GROUPS
    line, flat = (1, count), (levels * rows_x, cols_y)
    out = jax.ShapeDtypeStruct((32 * rows_x, cols_y), F32)
    dma = pltpu.SemaphoreType.DMA
    args = (
        kx.reshape(flat), ky.reshape(flat), mask.reshape(flat), obs_owner.reshape(line), obs_row.reshape(line),
        obs_col.reshape(line), innovation.reshape(line), inverse_var.reshape(line), obs_weight,
    )
    control, residual = pl.pallas_call(
        functools.partial(kernel, regions, tiles),
        out_shape=(out, out),
        in_specs=[pl.BlockSpec(memory_space=pl.ANY)] * 9,
        out_specs=[pl.BlockSpec(memory_space=pltpu.VMEM)] * 2,
        scratch_shapes=[
            *[pltpu.VMEM(x.shape, x.dtype) for x in args],
            pltpu.VMEM((EXCHANGES, cells, LANES), F32),
            pltpu.VMEM((EXCHANGES, 2, 32 * HALO, LANES), F32),
            pltpu.VMEM((EXCHANGES, 8, 8, LANES), F32),
            pltpu.VMEM((EXCHANGES, 8, 8, LANES), F32),
            pltpu.VMEM((EXCHANGES, 8, 8, LANES), F32),
            pltpu.VMEM((FRAME, LANES), F32),
            pltpu.VMEM((FRAME, LANES), F32),
            pltpu.VMEM((3, FRAME, LANES), F32),
            pltpu.VMEM((count, 3 * LANES), BF16),
            pltpu.VMEM((tiles, CAP, LANES), F32),
            pltpu.VMEM((tiles, CAP, LANES), F32),
            pltpu.VMEM((tiles, 1, LANES), F32),
            pltpu.VMEM((tiles, 1, LANES), F32),
            pltpu.VMEM((4, slots, LANES), F32),
            pltpu.VMEM((4, slots, LANES), F32),
            pltpu.VMEM((16, 24, LANES), F32),
            pltpu.VMEM((2, HALO, 24, LANES), F32),
            pltpu.VMEM((slots, 2 * cells), BF16),
            pltpu.VMEM((cells, 4 * slots), BF16),
            pltpu.VMEM((4 * slots, 2 * LANES), BF16),
            pltpu.VMEM((slots, LANES), F32),
            pltpu.VMEM((slots, LANES), F32),
            pltpu.VMEM((2, slots, LANES), F32),
            pltpu.VMEM((slots, LANES), F32),
            pltpu.VMEM((4, slots, LANES), F32),
            pltpu.VMEM((2 * cells, 4 * LANES), BF16),
            pltpu.VMEM((6, cells + 8, LANES), F32),
            pltpu.VMEM((4, cells, LANES), F32),
            pltpu.VMEM((2, 4, LANES), F32),
            pltpu.VMEM((2, regions, 4, LANES), F32),
            pltpu.VMEM((2, 4, LANES), F32),
            pltpu.VMEM((2, tiles, 4, LANES), F32),
            dma((9,)), dma((EXCHANGES, 8)), dma((EXCHANGES, 8)),
            dma((tiles,)), dma((tiles,)), dma((tiles,)), dma((tiles,)),
            dma((2, regions)), dma((2, regions)), dma((2, tiles)), dma((2, tiles)),
        ],
        compiler_params=pltpu.CompilerParams(collective_id=0, has_side_effects=True, vmem_limit_bytes=60 * 1024 * 1024),
    )(*args)
    control, residual = pl.pallas_call(
        hand_over,
        out_shape=(out, out),
        in_specs=[pl.BlockSpec(memory_space=pl.ANY)] * 2,
        out_specs=[pl.BlockSpec(memory_space=pl.ANY)] * 2,
        scratch_shapes=[dma((2,))],
        compiler_params=pltpu.CompilerParams(vmem_limit_bytes=60 * 1024 * 1024),
    )(control, residual)
    shape = (32 // levels, levels, rows_x, cols_y)
    return control.reshape(shape), residual.reshape(shape)


def solution(mesh):
    return jax.shard_map(
        functools.partial(body, mesh.shape["region"], mesh.shape["tile"]),
        mesh=mesh,
        in_specs=(
            P(None, "region", "tile"),
            P(None, "region", "tile"),
            P(None, "region", "tile"),
            P(("region", "tile"), None),
            P(("region", "tile")),
            P(("region", "tile")),
            P(("region", "tile"), None),
            P(("region", "tile")),
            P(("region", "tile")),
        ),
        out_specs=(P(None, None, "region", "tile"), P(None, None, "region", "tile")),
        check_vma=False,
    )
```

```python
import functools

import jax
import jax.numpy as jnp
from jax import lax
from jax.experimental import pallas as pl
from jax.experimental.pallas import tpu as pltpu
from jax.sharding import PartitionSpec as P

MESH = pl.DeviceIdType.MESH
F32 = jnp.float32
BF16 = jnp.bfloat16
CAP = 32
LANES = 128
GROUPS = 4
HALO = 8
WIDE = HALO + 32 + HALO
TALL = HALO + 16 + HALO
ROWS_AT_ONCE = 3
FRAME = (TALL + 3) * WIDE
EXCHANGES = 6


def iota(shape, dim):
    return lax.broadcasted_iota(jnp.int32, shape, dim)


def split(x, parts):
    out = []
    for i in range(parts):
        part = x.astype(BF16)
        out.append(part)
        if i + 1 < parts:
            x = x - part.astype(F32)
    return out


def dot(a, b):
    return jnp.dot(a, b, preferred_element_type=F32)


def dot_nt(a, b):
    return lax.dot_general(a, b, (((1,), (1,)), ((), ())), preferred_element_type=F32)


def swap_blocks(four):
    lane = iota(four[0].shape, 1)
    low = lane < 64
    even = (lane // 32) % 2 == 0
    a, b, c, d = four
    a, c = jnp.where(low, a, pltpu.roll(c, 64, 1)), jnp.where(low, pltpu.roll(a, 64, 1), c)
    b, d = jnp.where(low, b, pltpu.roll(d, 64, 1)), jnp.where(low, pltpu.roll(b, 64, 1), d)
    a, b = jnp.where(even, a, pltpu.roll(b, 32, 1)), jnp.where(even, pltpu.roll(a, 96, 1), b)
    c, d = jnp.where(even, c, pltpu.roll(d, 32, 1)), jnp.where(even, pltpu.roll(c, 96, 1), d)
    return a, b, c, d


def kernel(
    regions, tiles, kx_any, ky_any, mask_any, owner_any, row_any, col_any, innov_any, var_any, weight_any,
    control_ref, residual_ref,
    kx_ref, ky_ref, mask_ref, owner_ref, row_ref, col_ref, innov_ref, var_ref, weight_ref,
    dense, rows_in, left_in, right_in, packed, frame_a, frame_b, coef, wsplit, wsend, wrecv, msend, mrecv, expanded, expanded_0, coef_rows, coef_in,
    pick, pick_t, terms, var_b, z_b, q_b, acc, group_b, state16, fields, natural, sums_send, sums_region, sums_mid, sums_tile,
    in_sem, halo_send, halo_recv, w_send_sem, w_recv_sem, m_sem, r_sem, t_sem,
):
    reg, til = lax.axis_index("region"), lax.axis_index("tile")
    up, down = lax.rem(reg + regions - 1, regions), lax.rem(reg + 1, regions)
    left, right = lax.rem(til + tiles - 1, tiles), lax.rem(til + 1, tiles)
    count = owner_ref.shape[1]
    slots = tiles * CAP
    planes = tiles // 4
    late = []

    def wait_all(ref, sem):
        pltpu.make_async_copy(ref, ref, sem).wait()

    barrier = pltpu.get_barrier_semaphore()
    for i in sorted(range(1, tiles), key=lambda i: -min(i, tiles - i)):
        pl.semaphore_signal(barrier, inc=1, device_id=(reg, lax.rem(til + i, tiles)), device_id_type=MESH)
    for i in range(1, regions):
        pl.semaphore_signal(barrier, inc=1, device_id=(lax.rem(reg + i, regions), til), device_id_type=MESH)
    for a in (up, down):
        for b in (left, right):
            pl.semaphore_signal(barrier, inc=1, device_id=(a, b), device_id_type=MESH)

    pairs = (
        (owner_any, owner_ref), (row_any, row_ref), (col_any, col_ref), (innov_any, innov_ref), (var_any, var_ref),
        (weight_any, weight_ref), (mask_any, mask_ref), (kx_any, kx_ref), (ky_any, ky_ref),
    )
    loads = [pltpu.make_async_copy(a, b, in_sem.at[i]) for i, (a, b) in enumerate(pairs)]
    for c in loads:
        c.start()
    for c in loads[:6]:
        c.wait()
    lane8 = iota((8, LANES), 1)

    def halo_copies(e, deep, fields):
        def copy(src, dst, device):
            return pltpu.make_async_remote_copy(
                src_ref=src, dst_ref=dst, send_sem=halo_send.at[e], recv_sem=halo_recv.at[e],
                device_id=device, device_id_type=MESH)
        size, packs, at = deep * 32, deep // 4, pl.ds(e, fields)
        return [
            copy(packed.at[at, pl.ds(0, packs)], left_in.at[at, pl.ds(6, packs)], (up, right)),
            copy(packed.at[at, pl.ds(4 - packs, packs)], left_in.at[at, pl.ds(2 - packs, packs)], (down, right)),
            copy(packed.at[at, pl.ds(4, packs)], right_in.at[at, pl.ds(6, packs)], (up, left)),
            copy(packed.at[at, pl.ds(8 - packs, packs)], right_in.at[at, pl.ds(2 - packs, packs)], (down, left)),
            copy(packed.at[at, pl.ds(0, 4)], left_in.at[at, pl.ds(2, 4)], (reg, right)),
            copy(packed.at[at, pl.ds(4, 4)], right_in.at[at, pl.ds(2, 4)], (reg, left)),
            copy(coef_rows.at[pl.ds(0, 8)], coef_in.at[1], (up, til)) if e == 0 else
            copy(dense.at[e, pl.ds(0, size)], rows_in.at[e, 1, pl.ds(0, size)], (up, til)),
            copy(coef_rows.at[pl.ds(8, 8)], coef_in.at[0], (down, til)) if e == 0 else
            copy(dense.at[e, pl.ds(512 - size, size)], rows_in.at[e, 0, pl.ds(256 - size, size)], (down, til)),
        ]

    def halo_pack(e):
        for j in range(4):
            first = swap_blocks([dense[e, (4 * j + b) * 32:(4 * j + b) * 32 + 8, :] for b in range(4)])
            last = swap_blocks([dense[e, (4 * j + b) * 32 + 24:(4 * j + b) * 32 + 32, :] for b in range(4)])
            packed[e, j] = last[3]
            packed[e, 4 + j] = first[0]

    def halo_start(e, deep=8, fields=1):
        for c in halo_copies(e, deep, fields):
            c.start()
        amount = frame_b.at[pl.ds(0, 768 if e == 0 else 72 * deep + 64)]
        late.append(lambda: wait_all(amount, halo_send.at[e]))
        return lambda: wait_all(amount, halo_recv.at[e])

    def frame_own(e, out):
        def four_rows(j, _):
            for b in range(4):
                row = 4 * j + b
                base = pl.multiple_of((row + 8) * WIDE, 8)
                own = dense[e, pl.ds(pl.multiple_of(row * 32, 32), 32), :]
                out[pl.ds(base + 16, 32), :] = own
                out[pl.ds(base + 8, 8), :] = pltpu.roll(own[24:], 32, 1)
                out[pl.ds(base + WIDE, 8), :] = pltpu.roll(own[:8], 96, 1)
            return 0
        lax.fori_loop(0, 4, four_rows, 0)

    def frame_halo(e, out, deep=8):
        if e == 0:
            inside_up = jnp.where(reg > 0, 1.0, 0.0)
            inside_down = jnp.where(reg < regions - 1, 1.0, 0.0)
            rows_in[0, 0] = rows_in[0, 0] * inside_up
            rows_in[0, 1] = rows_in[0, 1] * inside_down
            for side, inside in ((left_in, jnp.where(til > 0, 1.0, 0.0)), (right_in, jnp.where(til < tiles - 1, 1.0, 0.0))):
                for j in range(8):
                    side[0, j] = side[0, j] * (inside * inside_up if j < 2 else inside if j < 6 else inside * inside_down)

        def beside(j, b):
            return pltpu.roll(left_in[e, j], -b * 32 % LANES, 1), pltpu.roll(right_in[e, j], (3 - b) * 32, 1)

        def own_rows(j, _):
            for b in range(4):
                base = pl.multiple_of((4 * j + b) * WIDE, 8)
                start, end = beside(j, b)
                out[pl.ds(base + 8, 8), :] = jnp.where(lane8 < 32, start, out[pl.ds(base + 8, 8), :])
                out[pl.ds(base + WIDE, 8), :] = jnp.where(lane8 >= 96, end, out[pl.ds(base + WIDE, 8), :])
            return 0

        lax.fori_loop(2, 6, own_rows, 0)
        for side in range(2):
            def outer_rows(j, _):
                for b in range(4):
                    row = 4 * j + b
                    base = pl.multiple_of((row + 24 * side) * WIDE, 8)
                    came = rows_in[e, side, pl.ds(pl.multiple_of(row * 32, 32), 32), :]
                    start, end = beside(j + 6 * side, b)
                    out[pl.ds(base + 16, 32), :] = came
                    out[pl.ds(base + 8, 8), :] = jnp.where(lane8 < 32, start, pltpu.roll(came[24:], 32, 1))
                    out[pl.ds(base + WIDE, 8), :] = jnp.where(lane8 >= 96, end, pltpu.roll(came[:8], 96, 1))
                return 0
            lax.fori_loop(0 if side else 2 - deep // 4, deep // 4 if side else 2, outer_rows, 0)

    def build_frame(e, arrive, out, deep=8):
        frame_own(e, out)
        drain()
        arrive()
        frame_halo(e, out, deep)

    def to_cells(line, out, rows):
        def four_rows(j, _):
            lines = [line(4 * j + b) for b in range(4)]
            many = jnp.concatenate([x for x in lines for _ in range(4)], axis=0).T
            for b, x in enumerate(swap_blocks([many[32 * g:32 * g + 32] for g in range(4)])):
                out[pl.ds(pl.multiple_of((4 * j + b) * 32, 32), 32), :] = x
            return 0
        lax.fori_loop(0, rows // 4, four_rows, 0)

    def to_natural(field, out):
        def four_rows(j, _):
            lines = [field[pl.ds(pl.multiple_of((4 * j + b) * 32, 32), 32), :] for b in range(4)]
            many = jnp.concatenate(swap_blocks(lines), axis=0).T
            for b in range(4):
                out[pl.ds(4 * j + b, 32, stride=16), :] = many[32 * b:32 * b + 32]
            return 0
        lax.fori_loop(0, 4, four_rows, 0)

    owner = owner_ref[...]
    marks = jnp.where(iota((tiles, count), 0) == owner, 1.0, 0.0)
    upper = jnp.where(iota((count, count), 0) < iota((count, count), 1), 1.0, 0.0).astype(BF16)
    before = dot(marks.astype(BF16), upper)
    slot = owner * CAP + jnp.sum(before * marks, axis=0, keepdims=True).astype(jnp.int32)
    for i, part in enumerate(split(weight_ref[...], 3)):
        wsplit[:, i * LANES:(i + 1) * LANES] = part
    meta_rows = [row_ref[...].astype(F32), col_ref[...].astype(F32)]
    meta_rows += [p.astype(F32) for p in split(innov_ref[...], 3) + split(var_ref[...], 3)]
    meta = jnp.zeros((8, count), F32)
    for i, line in enumerate(meta_rows):
        meta = jnp.where(iota((8, count), 0) == i, line, meta)
    meta = meta.astype(BF16)

    def sort_plane(b, _):
        chosen = jnp.where(iota((LANES, count), 0) + b * LANES == slot, 1.0, 0.0).astype(BF16)
        block = dot(chosen, wsplit[...])
        block = block[:, :LANES] + block[:, LANES:2 * LANES] + block[:, 2 * LANES:]
        wsend[pl.ds(4 * b, 4)] = block.reshape(4, CAP, LANES)
        facts = dot_nt(meta, chosen)
        place = jnp.broadcast_to(facts[0:1] * LANES + facts[1:2], (8, LANES))
        innov = jnp.broadcast_to(facts[2:3] + facts[3:4] + facts[4:5], (8, LANES))
        var = jnp.broadcast_to(facts[5:6] + facts[6:7] + facts[7:8], (8, LANES))
        for k in range(4):
            turned = [pltpu.roll(x, (i - k) * 32 % LANES, 1) for i, x in enumerate((place, innov, var))]
            line = jnp.where(lane8 < 32, turned[0], jnp.where(lane8 < 64, turned[1], jnp.where(lane8 < 96, turned[2], 0.0)))
            msend[4 * b + k] = line[0:1]
        return 0

    lax.fori_loop(0, planes, sort_plane, 0)

    turns = sorted(range(planes), key=lambda i: (min(i, planes - i), i))
    plane, place_in = til // 4, lax.rem(til, 4)

    def sends(src, dst, send_sem, recv_sem, together):
        out = []
        for j, turn in enumerate(turns):
            for k in range(4):
                if j or k:
                    to = lax.rem(plane + turn, planes) * 4 + lax.rem(place_in + k, 4)
                    n = 4 * j + k
                    out.append(pltpu.make_async_remote_copy(
                        src_ref=src.at[to], dst_ref=dst.at[n], send_sem=send_sem, recv_sem=recv_sem.at[n // together],
                        device_id=(reg, to), device_id_type=MESH))
        return out

    def both_ways(copies):
        order = list(range(3))
        for j in range(1, planes, 2):
            order += [4 * i + k - 1 for k in range(4) for i in (j, j + 1) if i < planes]
        return [copies[i] for i in order]

    m_copies = sends(msend, mrecv, m_sem.at[0], m_sem.at[pl.ds(1, 1)], tiles)
    w_copies = sends(wsend, wrecv, w_send_sem.at[0], w_recv_sem, 4)
    late.append(lambda: wait_all(msend.at[pl.ds(1, tiles - 1)], m_sem.at[0]))
    late.append(lambda: wait_all(wsend.at[pl.ds(1, tiles - 1)], w_send_sem.at[0]))
    def drain():
        for wait in late:
            wait()
        late.clear()

    pl.semaphore_wait(barrier, (tiles - 1) + (regions - 1) + 4)
    for c in both_ways(m_copies) + both_ways(w_copies):
        c.start()
    wrecv[0] = wsend[til]
    mrecv[0] = msend[til]

    for c in loads[6:]:
        c.wait()

    def stage(r, _):
        for e, source in enumerate((mask_ref, kx_ref, ky_ref)):
            coef_rows[r, 8 * e:8 * e + 8, :] = source[pl.ds(r, 8, stride=16), :].astype(F32)
        return 0

    lax.fori_loop(0, 16, stage, 0)
    for e in range(3):
        to_cells(lambda r: coef_rows[r, 8 * e:8 * e + 8, :], dense.at[e], 16)
        halo_pack(e)
    coef_arrive = halo_start(0, 8, 3)

    def diffuse(first, last):
        for s in range(first, last + 1):
            src, dst = (frame_a, frame_b) if (s - first) % 2 == 0 else (frame_b, frame_a)

            def lines(i, carry):
                before, here, west = carry
                base = pl.multiple_of((s + ROWS_AT_ONCE * i) * WIDE, 8)
                for u in range(ROWS_AT_ONCE):
                    at = base + u * WIDE
                    after = src[pl.ds(at + WIDE, WIDE), :]
                    east = coef[1, pl.ds(at, WIDE), :]
                    out = (coef[0, pl.ds(at, WIDE), :] * here + east * after) + west * before
                    dst[pl.ds(at, WIDE), :] = out + (
                        coef[2, pl.ds(at, WIDE), :] * src[pl.ds(at + 1, WIDE), :]
                        + coef[2, pl.ds(at - 1, WIDE), :] * src[pl.ds(at - 1, WIDE), :])
                    before, here, west = here, after, east
                return before, here, west

            at = (s - 1) * WIDE
            rows = 16 if s == HALO else TALL + 1 - 2 * s
            lax.fori_loop(
                0, -(-rows // ROWS_AT_ONCE), lines, (src[at:at + WIDE, :], src[at + WIDE:at + 2 * WIDE, :], coef[1, at:at + WIDE, :]))

    def inner(out):
        for j in range(16):
            out[j * 32:(j + 1) * 32, :] = frame_a[(8 + j) * WIDE + 16:(9 + j) * WIDE, :]

    wait_all(mrecv.at[pl.ds(1, tiles - 1)], m_sem.at[1])
    lane = iota((LANES, LANES), 1)
    seat = iota((LANES, LANES), 0) % CAP
    ones = jnp.ones((3 * LANES, LANES), BF16)
    cells = pick_t.shape[0]

    def corner_of(place, c):
        row = (place >> 7) + c // 2
        col = (place & 127) + c % 2
        return row * 32 + (col & 31), col >> 5

    def read_facts(j, _):
        at = pl.ds(pl.multiple_of(j * LANES, LANES), LANES)
        facts = jnp.broadcast_to(mrecv[pl.ds(4 * j, 4)], (4, CAP, LANES)).reshape(LANES, LANES)

        def spread_lanes(kind):
            return jnp.concatenate(split(jnp.where(lane == seat + 32 * kind, facts, 0.0), 3), axis=1)

        place3 = spread_lanes(0)
        place_col = dot(place3, ones).astype(jnp.int32)
        place_row = dot_nt(jnp.ones((8, 3 * LANES), BF16), place3).astype(jnp.int32)[0:1]
        var = dot(spread_lanes(2), ones)
        var_b[at, :] = var
        z_b[at, :] = var * dot(spread_lanes(1), ones)
        for c in range(4):
            cell, group = corner_of(place_col, c)
            group_b[c, at, :] = jnp.where(group == lane // 32, 1.0, 0.0)
            if c == 0:
                for t in range(cells // LANES):
                    hit = jnp.where(cell == lane + t * LANES, 1.0, 0.0).astype(BF16)
                    pick[at, t * LANES:(t + 1) * LANES] = hit
                    pick[at, cells + t * LANES:cells + (t + 1) * LANES] = hit
            cell, _ = corner_of(place_row, c)
            there = pl.ds(pl.multiple_of((4 * j + c) * LANES, LANES), LANES)
            pick_t[:, there] = jnp.where(iota((cells, LANES), 0) == cell, 1.0, 0.0).astype(BF16)
        return 0

    lax.fori_loop(0, planes, read_facts, 0)

    def put_terms(j, c):
        at = pl.ds(pl.multiple_of(j * LANES, LANES), LANES)
        there = pl.ds(pl.multiple_of((4 * j + c) * LANES, LANES), LANES)
        hi, lo = split(z_b[at, :] * expanded[c, at, :], 2)
        terms[there, :LANES] = hi
        terms[there, LANES:] = lo

    copy_lanes = jnp.where(
        iota((3 * LANES, 4 * LANES), 0) % LANES == iota((3 * LANES, 4 * LANES), 1) // LANES * 32 + iota((3 * LANES, 4 * LANES), 1) % 32,
        1.0, 0.0).astype(BF16)
    def take_plane(j, first):
        wait_all(wrecv.at[pl.ds(4 * j + first, 4 - first)], w_recv_sem.at[j])
        wide = dot(jnp.concatenate(split(wrecv[pl.ds(4 * j, 4)].reshape(LANES, LANES), 3), axis=1), copy_lanes)
        at = pl.ds(pl.multiple_of(j * LANES, LANES), LANES)
        for c in range(4):
            expanded[c, at, :] = wide[:, c * LANES:(c + 1) * LANES] * group_b[c, at, :]
            expanded_0[c, at, :] = wide[:, c * LANES:(c + 1) * LANES] * group_b[0, at, :]
            put_terms(j, c)
        there = pl.ds(pl.multiple_of(4 * j * LANES, LANES), 4 * LANES)
        part = dot(pick_t[:, there], terms[there, :])
        return part[:, :LANES] + part[:, LANES:]

    state16[...] = jnp.zeros_like(state16)
    dense[3] = take_plane(0, 1)

    def later_plane(j, _):
        dense[3] = dense[3] + take_plane(j, 0)
        return 0

    lax.fori_loop(1, planes, later_plane, 0)

    def adjoint(e):
        def one(j, _):
            for c in range(4):
                put_terms(j, c)
            return 0
        lax.fori_loop(0, planes, one, 0)
        total = dot(pick_t[...], terms[...])
        dense[e] = total[:, :LANES] + total[:, LANES:]

    def observe(field, n):
        def corners(r, _):
            at = pl.multiple_of(r * 32, 32)
            here = field[pl.ds(at, 32), :]
            past = jnp.broadcast_to(pltpu.roll(here[:8], 96, 1)[0:1], (32, LANES))
            beside = jnp.where(iota((32, LANES), 0) == 31, past, field[pl.ds(at + 1, 32), :])
            above = pl.multiple_of(jnp.maximum(at - 32, 0), 32)
            for c, value in enumerate((here, beside)):
                for h, part in enumerate(split(value, 2)):
                    state16[pl.ds(h * cells + at, 32), c * LANES:(c + 1) * LANES] = part
                    state16[pl.ds(h * cells + above, 32), (2 + c) * LANES:(3 + c) * LANES] = part
            return 0

        lax.fori_loop(0, 16, corners, 0)
        acc[...] = jnp.zeros_like(acc)

        def one(i, _):
            values = dot(pick[...], state16[:, pl.ds(pl.multiple_of(i * 2 * LANES, LANES), 2 * LANES)])
            acc[...] += values[:, :LANES] * expanded_0[2 * i] + values[:, LANES:] * expanded_0[2 * i + 1]
            return 0

        lax.fori_loop(0, 2, one, 0)
        q = jnp.broadcast_to(jnp.sum(acc[...], axis=1, keepdims=True), acc.shape)
        q_b[n] = q
        z_b[...] = var_b[...] * q

    def r_copies(n):
        return [pltpu.make_async_remote_copy(
            src_ref=sums_send.at[n], dst_ref=sums_region.at[n, i], send_sem=r_sem.at[n, 0], recv_sem=r_sem.at[n, 1],
            device_id=(lax.rem(reg + i, regions), til), device_id_type=MESH) for i in range(1, regions)]

    def t_copies(n):
        return [pltpu.make_async_remote_copy(
            src_ref=sums_mid.at[n], dst_ref=sums_tile.at[n, i], send_sem=t_sem.at[n, 0], recv_sem=t_sem.at[n, 1],
            device_id=(reg, lax.rem(til + i, tiles)), device_id_type=MESH) for i in range(1, tiles)]

    def sums_start(n, sums):
        for i in range(4):
            sums_send[n, i:i + 1, :] = sums[i] if i < len(sums) else jnp.zeros((1, LANES), F32)
        for c in r_copies(n):
            c.start()
        late.append(lambda: wait_all(sums_region.at[n, pl.ds(1, regions - 1)], r_sem.at[n, 0]))
        sums_region[n, 0] = sums_send[n]

    def sums_middle(n):
        wait_all(sums_region.at[n, pl.ds(1, regions - 1)], r_sem.at[n, 1])
        sums_mid[n] = jnp.sum(sums_region[n], axis=0)
        for c in t_copies(n):
            c.start()
        late.append(lambda: wait_all(sums_tile.at[n, pl.ds(1, tiles - 1)], t_sem.at[n, 0]))
        sums_tile[n, 0] = sums_mid[n]

    def sums_finish(n):
        wait_all(sums_tile.at[n, pl.ds(1, tiles - 1)], t_sem.at[n, 1])
        return jnp.sum(jnp.sum(sums_tile[n], axis=0), axis=1, keepdims=True)

    def product(a, b):
        return jnp.sum(a * b, axis=0, keepdims=True)

    lane1 = iota((1, LANES), 1)

    def energy(a, b):
        return jnp.where(lane1 == 0, product(var_b[...] * q_b[a], q_b[b]), 0.0)

    halo_pack(3)
    arrive = halo_start(3)

    for e in range(3):
        frame_own(e, coef.at[e])
    coef_arrive()
    for e in range(3):
        for side in range(2):
            to_cells(lambda r: coef_in[side, r, 8 * e:8 * e + 8, :], rows_in.at[e, side], 8)
        frame_halo(e, coef.at[e])

    def make_faces(k, _):
        base = pl.multiple_of(k * WIDE, 8)
        wet = coef[0, pl.ds(base, WIDE), :]
        coef[1, pl.ds(base, WIDE), :] = coef[1, pl.ds(base, WIDE), :] * wet * coef[0, pl.ds(base + WIDE, WIDE), :]
        coef[2, pl.ds(base, WIDE), :] = coef[2, pl.ds(base, WIDE), :] * wet * coef[0, pl.ds(base + 1, WIDE), :]
        return 0

    lax.fori_loop(0, TALL, make_faces, 0)

    def make_centre(k, _):
        base = pl.multiple_of(k * WIDE, 8)
        faces = coef[1, pl.ds(base, WIDE), :] + coef[1, pl.ds(base - WIDE, WIDE), :]
        faces = faces + coef[2, pl.ds(base, WIDE), :] + coef[2, pl.ds(base - 1, WIDE), :]
        coef[0, pl.ds(base, WIDE), :] = coef[0, pl.ds(base, WIDE), :] - faces
        return 0

    lax.fori_loop(1, TALL, make_centre, 0)

    build_frame(3, arrive, frame_a)
    diffuse(1, 4)
    inner(fields.at[0])
    diffuse(5, 8)
    inner(fields.at[1])

    observe(fields.at[1], 0)
    sums_start(0, (product(fields[0, :512, :], fields[0, :512, :]), energy(0, 0)))
    adjoint(4)
    halo_pack(4)
    arrive = halo_start(4)
    sums_middle(0)
    to_natural(fields.at[0], natural.at[0])
    build_frame(4, arrive, frame_a)
    diffuse(1, 4)
    inner(fields.at[2])
    diffuse(5, 8)
    inner(fields.at[4])
    found = sums_finish(0)
    norm_0, energy_0 = found[0:1], found[1:2]
    alpha_0 = norm_0 / (norm_0 + energy_0)
    fields[4, :512, :] = fields[1, :512, :] - alpha_0 * (fields[1, :512, :] + fields[4, :512, :])

    observe(fields.at[4], 1)
    fields[2, :512, :] = fields[0, :512, :] + fields[2, :512, :]
    fields[3, :512, :] = fields[0, :512, :] - alpha_0 * fields[2, :512, :]
    sums_start(1, (product(fields[3, :512, :], fields[3, :512, :]), product(fields[3, :512, :], fields[0, :512, :]), energy(1, 1), energy(1, 0)))
    adjoint(5)
    halo_pack(5)
    arrive = halo_start(5, 4)
    sums_middle(1)
    to_natural(fields.at[2], natural.at[1])
    to_natural(fields.at[3], natural.at[2])
    build_frame(5, arrive, frame_a, 4)
    diffuse(5, 8)
    inner(fields.at[5])
    to_natural(fields.at[5], natural.at[3])
    drain()
    found = sums_finish(1)
    norm_1 = found[0:1]
    beta = norm_1 / norm_0
    curve = norm_1 + 2.0 * beta * found[1:2] + beta * beta * norm_0 + found[2:3] + 2.0 * beta * found[3:4] + beta * beta * energy_0
    alpha_1 = norm_1 / curve
    control_ref[...] = (alpha_0 + alpha_1 * beta) * natural[0] + alpha_1 * natural[2]
    residual_ref[...] = natural[2] - alpha_1 * (natural[2] + natural[3] + beta * natural[1])


def hand_over(control, residual, control_out, residual_out):
    control_out[...] = control[...]
    residual_out[...] = residual[...]


def body(regions, tiles, kx, ky, mask, obs_owner, obs_row, obs_col, obs_weight, innovation, inverse_var):
    levels, rows_x, cols_y = kx.shape
    count = obs_row.shape[0]
    slots = tiles * CAP
    cells = rows_x * cols_y // GROUPS
    line, flat = (1, count), (levels * rows_x, cols_y)
    out = jax.ShapeDtypeStruct((32 * rows_x, cols_y), F32)
    dma = pltpu.SemaphoreType.DMA
    args = (
        kx.reshape(flat), ky.reshape(flat), mask.reshape(flat), obs_owner.reshape(line), obs_row.reshape(line),
        obs_col.reshape(line), innovation.reshape(line), inverse_var.reshape(line), obs_weight,
    )
    control, residual = pl.pallas_call(
        functools.partial(kernel, regions, tiles),
        out_shape=(out, out),
        in_specs=[pl.BlockSpec(memory_space=pl.ANY)] * 9,
        out_specs=[pl.BlockSpec(memory_space=pltpu.VMEM)] * 2,
        scratch_shapes=[
            *[pltpu.VMEM(x.shape, x.dtype) for x in args],
            pltpu.VMEM((EXCHANGES, cells, LANES), F32),
            pltpu.VMEM((EXCHANGES, 2, 32 * HALO, LANES), F32),
            pltpu.VMEM((EXCHANGES, 8, 8, LANES), F32),
            pltpu.VMEM((EXCHANGES, 8, 8, LANES), F32),
            pltpu.VMEM((EXCHANGES, 8, 8, LANES), F32),
            pltpu.VMEM((FRAME, LANES), F32),
            pltpu.VMEM((FRAME, LANES), F32),
            pltpu.VMEM((3, FRAME, LANES), F32),
            pltpu.VMEM((count, 3 * LANES), BF16),
            pltpu.VMEM((tiles, CAP, LANES), F32),
            pltpu.VMEM((tiles, CAP, LANES), F32),
            pltpu.VMEM((tiles, 1, LANES), F32),
            pltpu.VMEM((tiles, 1, LANES), F32),
            pltpu.VMEM((4, slots, LANES), F32),
            pltpu.VMEM((4, slots, LANES), F32),
            pltpu.VMEM((16, 24, LANES), F32),
            pltpu.VMEM((2, HALO, 24, LANES), F32),
            pltpu.VMEM((slots, 2 * cells), BF16),
            pltpu.VMEM((cells, 4 * slots), BF16),
            pltpu.VMEM((4 * slots, 2 * LANES), BF16),
            pltpu.VMEM((slots, LANES), F32),
            pltpu.VMEM((slots, LANES), F32),
            pltpu.VMEM((2, slots, LANES), F32),
            pltpu.VMEM((slots, LANES), F32),
            pltpu.VMEM((4, slots, LANES), F32),
            pltpu.VMEM((2 * cells, 4 * LANES), BF16),
            pltpu.VMEM((6, cells + 8, LANES), F32),
            pltpu.VMEM((4, cells, LANES), F32),
            pltpu.VMEM((2, 4, LANES), F32),
            pltpu.VMEM((2, regions, 4, LANES), F32),
            pltpu.VMEM((2, 4, LANES), F32),
            pltpu.VMEM((2, tiles, 4, LANES), F32),
            dma((9,)), dma((EXCHANGES,)), dma((EXCHANGES,)), dma((1,)), dma((tiles // 4,)), dma((2,)), dma((2, 2)), dma((2, 2)),
        ],
        compiler_params=pltpu.CompilerParams(collective_id=0, has_side_effects=True, vmem_limit_bytes=60 * 1024 * 1024),
    )(*args)
    control, residual = pl.pallas_call(
        hand_over,
        out_shape=(out, out),
        in_specs=[pl.BlockSpec(memory_space=pltpu.VMEM)] * 2,
        out_specs=[pl.BlockSpec(memory_space=pltpu.VMEM)] * 2,
        compiler_params=pltpu.CompilerParams(vmem_limit_bytes=60 * 1024 * 1024),
    )(control, residual)
    shape = (32 // levels, levels, rows_x, cols_y)
    return control.reshape(shape), residual.reshape(shape)


def solution(mesh):
    return jax.shard_map(
        functools.partial(body, mesh.shape["region"], mesh.shape["tile"]),
        mesh=mesh,
        in_specs=(
            P(None, "region", "tile"),
            P(None, "region", "tile"),
            P(None, "region", "tile"),
            P(("region", "tile"), None),
            P(("region", "tile")),
            P(("region", "tile")),
            P(("region", "tile"), None),
            P(("region", "tile")),
            P(("region", "tile")),
        ),
        out_specs=(P(None, None, "region", "tile"), P(None, None, "region", "tile")),
        check_vma=False,
    )
```

```python
import functools

import jax
import jax.numpy as jnp
from jax import lax
from jax.experimental import pallas as pl
from jax.experimental.pallas import tpu as pltpu
from jax.sharding import PartitionSpec as P

MESH = pl.DeviceIdType.MESH
F32 = jnp.float32
BF16 = jnp.bfloat16
CAP = 32
LANES = 128
GROUPS = 4
HALO = 8
WIDE = HALO + 32 + HALO
TALL = HALO + 16 + HALO
ROWS_AT_ONCE = 3
FRAME = (TALL + 3) * WIDE
EXCHANGES = 6


def iota(shape, dim):
    return lax.broadcasted_iota(jnp.int32, shape, dim)


def split(x, parts):
    out = []
    for i in range(parts):
        part = x.astype(BF16)
        out.append(part)
        if i + 1 < parts:
            x = x - part.astype(F32)
    return out


def dot(a, b):
    return jnp.dot(a, b, preferred_element_type=F32)


def dot_nt(a, b):
    return lax.dot_general(a, b, (((1,), (1,)), ((), ())), preferred_element_type=F32)


def swap_blocks(four):
    lane = iota(four[0].shape, 1)
    low = lane < 64
    even = (lane // 32) % 2 == 0
    a, b, c, d = four
    a, c = jnp.where(low, a, pltpu.roll(c, 64, 1)), jnp.where(low, pltpu.roll(a, 64, 1), c)
    b, d = jnp.where(low, b, pltpu.roll(d, 64, 1)), jnp.where(low, pltpu.roll(b, 64, 1), d)
    a, b = jnp.where(even, a, pltpu.roll(b, 32, 1)), jnp.where(even, pltpu.roll(a, 96, 1), b)
    c, d = jnp.where(even, c, pltpu.roll(d, 32, 1)), jnp.where(even, pltpu.roll(c, 96, 1), d)
    return a, b, c, d


def kernel(
    regions, tiles, kx_any, ky_any, mask_any, owner_any, row_any, col_any, innov_any, var_any, weight_any,
    control_ref, residual_ref,
    kx_ref, ky_ref, mask_ref, owner_ref, row_ref, col_ref, innov_ref, var_ref, weight_ref,
    dense, rows_in, left_in, right_in, packed, frame_a, frame_b, coef, wsplit, wsend, wrecv, msend, mrecv, expanded, expanded_0, coef_rows, coef_in,
    pick, pick_t, terms, var_b, z_b, q_b, acc, group_b, state16, fields, natural, sums_send, sums_region, sums_mid, sums_tile,
    in_sem, halo_send, halo_recv, w_send_sem, w_recv_sem, m_sem, r_sem, t_sem,
):
    reg, til = lax.axis_index("region"), lax.axis_index("tile")
    up, down = lax.rem(reg + regions - 1, regions), lax.rem(reg + 1, regions)
    left, right = lax.rem(til + tiles - 1, tiles), lax.rem(til + 1, tiles)
    count = owner_ref.shape[1]
    slots = tiles * CAP
    planes = tiles // 4
    late = []

    def wait_all(ref, sem):
        pltpu.make_async_copy(ref, ref, sem).wait()

    barrier = pltpu.get_barrier_semaphore()
    for i in sorted(range(1, tiles), key=lambda i: -min(i, tiles - i)):
        pl.semaphore_signal(barrier, inc=1, device_id=(reg, lax.rem(til + i, tiles)), device_id_type=MESH)
    for i in range(1, regions):
        pl.semaphore_signal(barrier, inc=1, device_id=(lax.rem(reg + i, regions), til), device_id_type=MESH)
    for a in (up, down):
        for b in (left, right):
            pl.semaphore_signal(barrier, inc=1, device_id=(a, b), device_id_type=MESH)

    pairs = (
        (owner_any, owner_ref), (row_any, row_ref), (col_any, col_ref), (innov_any, innov_ref), (var_any, var_ref),
        (weight_any, weight_ref), (mask_any, mask_ref), (kx_any, kx_ref), (ky_any, ky_ref),
    )
    loads = [pltpu.make_async_copy(a, b, in_sem.at[i]) for i, (a, b) in enumerate(pairs)]
    for c in loads:
        c.start()
    for c in loads[:5]:
        c.wait()
    lane8 = iota((8, LANES), 1)

    def halo_copies(e, deep, fields):
        def copy(src, dst, device):
            return pltpu.make_async_remote_copy(
                src_ref=src, dst_ref=dst, send_sem=halo_send.at[e], recv_sem=halo_recv.at[e],
                device_id=device, device_id_type=MESH)
        size, packs, at = deep * 32, deep // 4, pl.ds(e, fields)
        return [
            copy(packed.at[at, pl.ds(0, packs)], left_in.at[at, pl.ds(6, packs)], (up, right)),
            copy(packed.at[at, pl.ds(4 - packs, packs)], left_in.at[at, pl.ds(2 - packs, packs)], (down, right)),
            copy(packed.at[at, pl.ds(4, packs)], right_in.at[at, pl.ds(6, packs)], (up, left)),
            copy(packed.at[at, pl.ds(8 - packs, packs)], right_in.at[at, pl.ds(2 - packs, packs)], (down, left)),
            copy(packed.at[at, pl.ds(0, 4)], left_in.at[at, pl.ds(2, 4)], (reg, right)),
            copy(packed.at[at, pl.ds(4, 4)], right_in.at[at, pl.ds(2, 4)], (reg, left)),
            copy(coef_rows.at[pl.ds(0, 8)], coef_in.at[1], (up, til)) if e == 0 else
            copy(dense.at[e, pl.ds(0, size)], rows_in.at[e, 1, pl.ds(0, size)], (up, til)),
            copy(coef_rows.at[pl.ds(8, 8)], coef_in.at[0], (down, til)) if e == 0 else
            copy(dense.at[e, pl.ds(512 - size, size)], rows_in.at[e, 0, pl.ds(256 - size, size)], (down, til)),
        ]

    def halo_pack(e):
        for j in range(4):
            first = swap_blocks([dense[e, (4 * j + b) * 32:(4 * j + b) * 32 + 8, :] for b in range(4)])
            last = swap_blocks([dense[e, (4 * j + b) * 32 + 24:(4 * j + b) * 32 + 32, :] for b in range(4)])
            packed[e, j] = last[3]
            packed[e, 4 + j] = first[0]

    def halo_start(e, deep=8, fields=1):
        for c in halo_copies(e, deep, fields):
            c.start()
        amount = frame_b.at[pl.ds(0, 768 if e == 0 else 72 * deep + 64)]
        late.append(lambda: wait_all(amount, halo_send.at[e]))
        return lambda: wait_all(amount, halo_recv.at[e])

    def frame_own(e, out):
        def four_rows(j, _):
            for b in range(4):
                row = 4 * j + b
                base = pl.multiple_of((row + 8) * WIDE, 8)
                own = dense[e, pl.ds(pl.multiple_of(row * 32, 32), 32), :]
                out[pl.ds(base + 16, 32), :] = own
                out[pl.ds(base + 8, 8), :] = pltpu.roll(own[24:], 32, 1)
                out[pl.ds(base + WIDE, 8), :] = pltpu.roll(own[:8], 96, 1)
            return 0
        lax.fori_loop(0, 4, four_rows, 0)

    def frame_halo(e, out, deep=8):
        if e == 0:
            inside_up = jnp.where(reg > 0, 1.0, 0.0)
            inside_down = jnp.where(reg < regions - 1, 1.0, 0.0)
            rows_in[0, 0] = rows_in[0, 0] * inside_up
            rows_in[0, 1] = rows_in[0, 1] * inside_down
            for side, inside in ((left_in, jnp.where(til > 0, 1.0, 0.0)), (right_in, jnp.where(til < tiles - 1, 1.0, 0.0))):
                for j in range(8):
                    side[0, j] = side[0, j] * (inside * inside_up if j < 2 else inside if j < 6 else inside * inside_down)

        def beside(j, b):
            return pltpu.roll(left_in[e, j], -b * 32 % LANES, 1), pltpu.roll(right_in[e, j], (3 - b) * 32, 1)

        def own_rows(j, _):
            for b in range(4):
                base = pl.multiple_of((4 * j + b) * WIDE, 8)
                start, end = beside(j, b)
                out[pl.ds(base + 8, 8), :] = jnp.where(lane8 < 32, start, out[pl.ds(base + 8, 8), :])
                out[pl.ds(base + WIDE, 8), :] = jnp.where(lane8 >= 96, end, out[pl.ds(base + WIDE, 8), :])
            return 0

        lax.fori_loop(2, 6, own_rows, 0)
        for side in range(2):
            def outer_rows(j, _):
                for b in range(4):
                    row = 4 * j + b
                    base = pl.multiple_of((row + 24 * side) * WIDE, 8)
                    came = rows_in[e, side, pl.ds(pl.multiple_of(row * 32, 32), 32), :]
                    start, end = beside(j + 6 * side, b)
                    out[pl.ds(base + 16, 32), :] = came
                    out[pl.ds(base + 8, 8), :] = jnp.where(lane8 < 32, start, pltpu.roll(came[24:], 32, 1))
                    out[pl.ds(base + WIDE, 8), :] = jnp.where(lane8 >= 96, end, pltpu.roll(came[:8], 96, 1))
                return 0
            lax.fori_loop(0 if side else 2 - deep // 4, deep // 4 if side else 2, outer_rows, 0)

    def build_frame(e, arrive, out, deep=8, meanwhile=lambda: None):
        frame_own(e, out)
        drain()
        meanwhile()
        arrive()
        frame_halo(e, out, deep)

    def to_cells(line, out, rows):
        def four_rows(j, _):
            lines = [line(4 * j + b) for b in range(4)]
            many = jnp.concatenate([x for x in lines for _ in range(4)], axis=0).T
            for b, x in enumerate(swap_blocks([many[32 * g:32 * g + 32] for g in range(4)])):
                out[pl.ds(pl.multiple_of((4 * j + b) * 32, 32), 32), :] = x
            return 0
        lax.fori_loop(0, rows // 4, four_rows, 0)

    def to_natural(field, out):
        def four_rows(j, _):
            lines = [field[pl.ds(pl.multiple_of((4 * j + b) * 32, 32), 32), :] for b in range(4)]
            many = jnp.concatenate(swap_blocks(lines), axis=0).T
            for b in range(4):
                out[pl.ds(4 * j + b, 32, stride=16), :] = many[32 * b:32 * b + 32]
            return 0
        lax.fori_loop(0, 4, four_rows, 0)

    owner = owner_ref[...]
    marks = jnp.where(iota((tiles, count), 0) == owner, 1.0, 0.0)
    upper = jnp.where(iota((count, count), 0) < iota((count, count), 1), 1.0, 0.0).astype(BF16)
    before = dot(marks.astype(BF16), upper)
    slot = owner * CAP + jnp.sum(before * marks, axis=0, keepdims=True).astype(jnp.int32)
    meta_rows = [row_ref[...].astype(F32), col_ref[...].astype(F32)]
    meta_rows += [p.astype(F32) for p in split(innov_ref[...], 3) + split(var_ref[...], 3)]
    meta = jnp.zeros((8, count), F32)
    for i, line in enumerate(meta_rows):
        meta = jnp.where(iota((8, count), 0) == i, line, meta)
    meta = meta.astype(BF16)

    def choose(b, _):
        chosen = jnp.where(iota((LANES, count), 0) + b * LANES == slot, 1.0, 0.0).astype(BF16)
        pick[pl.ds(pl.multiple_of(b * LANES, LANES), LANES), :count] = chosen
        return 0

    lax.fori_loop(0, planes, choose, 0)
    facts = dot_nt(meta, pick[:, :count])
    place = facts[0:1] * LANES + facts[1:2]
    innov = facts[2:3] + facts[3:4] + facts[4:5]
    var = facts[5:6] + facts[6:7] + facts[7:8]
    for b in range(planes):
        at = slice(b * LANES, (b + 1) * LANES)
        three = [jnp.broadcast_to(x[:, at], (8, LANES)) for x in (place, innov, var)]
        for k in range(4):
            turned = [pltpu.roll(x, (i - k) * 32 % LANES, 1) for i, x in enumerate(three)]
            line = jnp.where(lane8 < 32, turned[0], jnp.where(lane8 < 64, turned[1], jnp.where(lane8 < 96, turned[2], 0.0)))
            msend[4 * b + k] = line[0:1]
    loads[5].wait()
    for i, part in enumerate(split(weight_ref[...], 3)):
        wsplit[:, i * LANES:(i + 1) * LANES] = part
    block = dot(pick[:, :count], wsplit[...])
    wsend[...] = (block[:, :LANES] + block[:, LANES:2 * LANES] + block[:, 2 * LANES:]).reshape(tiles, CAP, LANES)

    turns = sorted(range(planes), key=lambda i: (min(i, planes - i), i))
    plane, place_in = til // 4, lax.rem(til, 4)

    def sends(src, dst, send_sem, recv_sem, together):
        out = []
        for j, turn in enumerate(turns):
            for k in range(4):
                if j or k:
                    to = lax.rem(plane + turn, planes) * 4 + lax.rem(place_in + k, 4)
                    n = 4 * j + k
                    out.append(pltpu.make_async_remote_copy(
                        src_ref=src.at[to], dst_ref=dst.at[n], send_sem=send_sem, recv_sem=recv_sem.at[n // together],
                        device_id=(reg, to), device_id_type=MESH))
        return out

    def both_ways(copies):
        order = list(range(3))
        for j in range(1, planes, 2):
            order += [4 * i + k - 1 for k in range(4) for i in (j, j + 1) if i < planes]
        return [copies[i] for i in order]

    m_copies = sends(msend, mrecv, m_sem.at[0], m_sem.at[pl.ds(1, 1)], tiles)
    w_copies = sends(wsend, wrecv, w_send_sem.at[0], w_recv_sem, 4)
    late.append(lambda: wait_all(msend.at[pl.ds(1, tiles - 1)], m_sem.at[0]))
    late.append(lambda: wait_all(wsend.at[pl.ds(1, tiles - 1)], w_send_sem.at[0]))
    def drain():
        for wait in late:
            wait()
        late.clear()

    pl.semaphore_wait(barrier, (tiles - 1) + (regions - 1) + 4)
    for c in both_ways(m_copies) + both_ways(w_copies):
        c.start()
    wrecv[0] = wsend[til]
    mrecv[0] = msend[til]

    for c in loads[6:]:
        c.wait()

    def stage(r, _):
        for e, source in enumerate((mask_ref, kx_ref, ky_ref)):
            coef_rows[r, 8 * e:8 * e + 8, :] = source[pl.ds(r, 8, stride=16), :].astype(F32)
        return 0

    lax.fori_loop(0, 16, stage, 0)
    for e in range(3):
        to_cells(lambda r: coef_rows[r, 8 * e:8 * e + 8, :], dense.at[e], 16)
        halo_pack(e)
    coef_arrive = halo_start(0, 8, 3)

    def diffuse(first, last):
        for s in range(first, last + 1):
            src, dst = (frame_a, frame_b) if (s - first) % 2 == 0 else (frame_b, frame_a)

            def lines(i, carry):
                before, here, west = carry
                base = pl.multiple_of((s + ROWS_AT_ONCE * i) * WIDE, 8)
                for u in range(ROWS_AT_ONCE):
                    at = base + u * WIDE
                    after = src[pl.ds(at + WIDE, WIDE), :]
                    east = coef[1, pl.ds(at, WIDE), :]
                    out = (coef[0, pl.ds(at, WIDE), :] * here + east * after) + west * before
                    dst[pl.ds(at, WIDE), :] = out + (
                        coef[2, pl.ds(at, WIDE), :] * src[pl.ds(at + 1, WIDE), :]
                        + coef[2, pl.ds(at - 1, WIDE), :] * src[pl.ds(at - 1, WIDE), :])
                    before, here, west = here, after, east
                return before, here, west

            at = (s - 1) * WIDE
            rows = 16 if s == HALO else TALL + 1 - 2 * s
            lax.fori_loop(
                0, -(-rows // ROWS_AT_ONCE), lines, (src[at:at + WIDE, :], src[at + WIDE:at + 2 * WIDE, :], coef[1, at:at + WIDE, :]))

    def inner(out):
        for j in range(16):
            out[j * 32:(j + 1) * 32, :] = frame_a[(8 + j) * WIDE + 16:(9 + j) * WIDE, :]

    wait_all(mrecv.at[pl.ds(1, tiles - 1)], m_sem.at[1])
    lane = iota((LANES, LANES), 1)
    seat = iota((LANES, LANES), 0) % CAP
    ones = jnp.ones((3 * LANES, LANES), BF16)
    cells = pick_t.shape[0]

    def corner_of(place, c):
        row = (place >> 7) + c // 2
        col = (place & 127) + c % 2
        return row * 32 + (col & 31), col >> 5

    def read_facts(j, _):
        at = pl.ds(pl.multiple_of(j * LANES, LANES), LANES)
        facts = jnp.broadcast_to(mrecv[pl.ds(4 * j, 4)], (4, CAP, LANES)).reshape(LANES, LANES)

        def spread_lanes(kind):
            return jnp.concatenate(split(jnp.where(lane == seat + 32 * kind, facts, 0.0), 3), axis=1)

        place3 = spread_lanes(0)
        place_col = dot(place3, ones).astype(jnp.int32)
        place_row = dot_nt(jnp.ones((8, 3 * LANES), BF16), place3).astype(jnp.int32)[0:1]
        var = dot(spread_lanes(2), ones)
        var_b[at, :] = var
        z_b[at, :] = var * dot(spread_lanes(1), ones)
        for c in range(4):
            cell, group = corner_of(place_col, c)
            group_b[c, at, :] = jnp.where(group == lane // 32, 1.0, 0.0)
            if c == 0:
                for t in range(cells // LANES):
                    hit = jnp.where(cell == lane + t * LANES, 1.0, 0.0).astype(BF16)
                    pick[at, t * LANES:(t + 1) * LANES] = hit
                    pick[at, cells + t * LANES:cells + (t + 1) * LANES] = hit
            cell, _ = corner_of(place_row, c)
            there = pl.ds(pl.multiple_of((4 * j + c) * LANES, LANES), LANES)
            pick_t[:, there] = jnp.where(iota((cells, LANES), 0) == cell, 1.0, 0.0).astype(BF16)
        return 0

    lax.fori_loop(0, planes, read_facts, 0)

    def put_terms(j, c):
        at = pl.ds(pl.multiple_of(j * LANES, LANES), LANES)
        there = pl.ds(pl.multiple_of((4 * j + c) * LANES, LANES), LANES)
        hi, lo = split(z_b[at, :] * expanded[c, at, :], 2)
        terms[there, :LANES] = hi
        terms[there, LANES:] = lo

    for e in range(3):
        frame_own(e, coef.at[e])

    copy_lanes = jnp.where(
        iota((3 * LANES, 4 * LANES), 0) % LANES == iota((3 * LANES, 4 * LANES), 1) // LANES * 32 + iota((3 * LANES, 4 * LANES), 1) % 32,
        1.0, 0.0).astype(BF16)
    def take_plane(j, first):
        wait_all(wrecv.at[pl.ds(4 * j + first, 4 - first)], w_recv_sem.at[j])
        wide = dot(jnp.concatenate(split(wrecv[pl.ds(4 * j, 4)].reshape(LANES, LANES), 3), axis=1), copy_lanes)
        at = pl.ds(pl.multiple_of(j * LANES, LANES), LANES)
        for c in range(4):
            expanded[c, at, :] = wide[:, c * LANES:(c + 1) * LANES] * group_b[c, at, :]
            expanded_0[c, at, :] = wide[:, c * LANES:(c + 1) * LANES] * group_b[0, at, :]
            put_terms(j, c)
        there = pl.ds(pl.multiple_of(4 * j * LANES, LANES), 4 * LANES)
        part = dot(pick_t[:, there], terms[there, :])
        return part[:, :LANES] + part[:, LANES:]

    state16[...] = jnp.zeros_like(state16)
    dense[3] = take_plane(0, 1)

    def later_plane(j, _):
        dense[3] = dense[3] + take_plane(j, 0)
        return 0

    lax.fori_loop(1, planes, later_plane, 0)

    def adjoint(e):
        def one(j, _):
            for c in range(4):
                put_terms(j, c)
            return 0
        lax.fori_loop(0, planes, one, 0)
        total = dot(pick_t[...], terms[...])
        dense[e] = total[:, :LANES] + total[:, LANES:]

    def observe(field, n):
        def corners(r, _):
            at = pl.multiple_of(r * 32, 32)
            here = field[pl.ds(at, 32), :]
            past = jnp.broadcast_to(pltpu.roll(here[:8], 96, 1)[0:1], (32, LANES))
            beside = jnp.where(iota((32, LANES), 0) == 31, past, field[pl.ds(at + 1, 32), :])
            above = pl.multiple_of(jnp.maximum(at - 32, 0), 32)
            for c, value in enumerate((here, beside)):
                for h, part in enumerate(split(value, 2)):
                    state16[pl.ds(h * cells + at, 32), c * LANES:(c + 1) * LANES] = part
                    state16[pl.ds(h * cells + above, 32), (2 + c) * LANES:(3 + c) * LANES] = part
            return 0

        lax.fori_loop(0, 16, corners, 0)
        acc[...] = jnp.zeros_like(acc)

        def one(i, _):
            values = dot(pick[...], state16[:, pl.ds(pl.multiple_of(i * 2 * LANES, LANES), 2 * LANES)])
            acc[...] += values[:, :LANES] * expanded_0[2 * i] + values[:, LANES:] * expanded_0[2 * i + 1]
            return 0

        lax.fori_loop(0, 2, one, 0)
        q = jnp.broadcast_to(jnp.sum(acc[...], axis=1, keepdims=True), acc.shape)
        q_b[n] = q

    def sums_start(n, sums):
        for i in range(4):
            sums_send[n, i:i + 1, :] = sums[i] if i < len(sums) else jnp.zeros((1, LANES), F32)
        for i in sorted(range(1, tiles), key=lambda i: -min(i, tiles - i)):
            pltpu.make_async_remote_copy(
                src_ref=sums_send.at[n], dst_ref=sums_tile.at[n, i], send_sem=t_sem.at[n, 0], recv_sem=t_sem.at[n, 1],
                device_id=(reg, lax.rem(til + i, tiles)), device_id_type=MESH).start()
        late.append(lambda: wait_all(sums_tile.at[n, pl.ds(1, tiles - 1)], t_sem.at[n, 0]))
        sums_tile[n, 0] = sums_send[n]

    def sums_middle(n):
        wait_all(sums_tile.at[n, pl.ds(1, tiles - 1)], t_sem.at[n, 1])
        sums_mid[n] = jnp.sum(sums_tile[n], axis=0)
        for i in sorted(range(1, regions), key=lambda i: -min(i, regions - i)):
            pltpu.make_async_remote_copy(
                src_ref=sums_mid.at[n], dst_ref=sums_region.at[n, i], send_sem=r_sem.at[n, 0], recv_sem=r_sem.at[n, 1],
                device_id=(lax.rem(reg + i, regions), til), device_id_type=MESH).start()
        late.append(lambda: wait_all(sums_region.at[n, pl.ds(1, regions - 1)], r_sem.at[n, 0]))
        sums_region[n, 0] = sums_mid[n]

    def sums_finish(n):
        wait_all(sums_region.at[n, pl.ds(1, regions - 1)], r_sem.at[n, 1])
        return jnp.sum(jnp.sum(sums_region[n], axis=0), axis=1, keepdims=True)

    def product(a, b):
        return jnp.sum(a * b, axis=0, keepdims=True)

    lane1 = iota((1, LANES), 1)

    def energy(a, b):
        return jnp.where(lane1 == 0, product(var_b[...] * q_b[a], q_b[b]), 0.0)

    halo_pack(3)
    arrive = halo_start(3)

    coef_arrive()
    for e in range(3):
        for side in range(2):
            to_cells(lambda r: coef_in[side, r, 8 * e:8 * e + 8, :], rows_in.at[e, side], 8)
        frame_halo(e, coef.at[e])

    def make_faces(k, _):
        base = pl.multiple_of(k * WIDE, 8)
        wet = coef[0, pl.ds(base, WIDE), :]
        coef[1, pl.ds(base, WIDE), :] = coef[1, pl.ds(base, WIDE), :] * wet * coef[0, pl.ds(base + WIDE, WIDE), :]
        coef[2, pl.ds(base, WIDE), :] = coef[2, pl.ds(base, WIDE), :] * wet * coef[0, pl.ds(base + 1, WIDE), :]
        return 0

    lax.fori_loop(0, TALL, make_faces, 0)

    def make_centre(k, _):
        base = pl.multiple_of(k * WIDE, 8)
        faces = coef[1, pl.ds(base, WIDE), :] + coef[1, pl.ds(base - WIDE, WIDE), :]
        faces = faces + coef[2, pl.ds(base, WIDE), :] + coef[2, pl.ds(base - 1, WIDE), :]
        coef[0, pl.ds(base, WIDE), :] = coef[0, pl.ds(base, WIDE), :] - faces
        return 0

    lax.fori_loop(1, TALL, make_centre, 0)

    build_frame(3, arrive, frame_a)
    diffuse(1, 4)
    inner(fields.at[0])
    diffuse(5, 8)
    inner(fields.at[1])

    norm = product(fields[0, :512, :], fields[0, :512, :])
    observe(fields.at[1], 0)
    sums_start(0, (norm, energy(0, 0)))
    z_b[...] = var_b[...] * q_b[0]
    adjoint(4)
    halo_pack(4)
    arrive = halo_start(4)
    to_natural(fields.at[0], natural.at[0])
    build_frame(4, arrive, frame_a, 8, lambda: sums_middle(0))
    diffuse(1, 4)
    inner(fields.at[2])
    diffuse(5, 8)
    inner(fields.at[4])
    observe(fields.at[4], 1)
    fields[2, :512, :] = fields[0, :512, :] + fields[2, :512, :]
    found = sums_finish(0)
    norm_0, energy_0 = found[0:1], found[1:2]
    alpha_0 = norm_0 / (norm_0 + energy_0)
    q_b[1] = q_b[0] - alpha_0 * (q_b[0] + q_b[1])
    fields[3, :512, :] = fields[0, :512, :] - alpha_0 * fields[2, :512, :]
    sums_start(1, (
        product(fields[3, :512, :], fields[3, :512, :]), product(fields[3, :512, :], fields[0, :512, :]), energy(1, 1), energy(1, 0)))
    z_b[...] = var_b[...] * q_b[1]
    adjoint(5)
    halo_pack(5)
    arrive = halo_start(5, 4)
    to_natural(fields.at[2], natural.at[1])
    to_natural(fields.at[3], natural.at[2])
    build_frame(5, arrive, frame_a, 4, lambda: sums_middle(1))
    diffuse(5, 8)
    inner(fields.at[5])
    to_natural(fields.at[5], natural.at[3])
    drain()
    found = sums_finish(1)
    norm_1 = found[0:1]
    beta = norm_1 / norm_0
    curve = norm_1 + 2.0 * beta * found[1:2] + beta * beta * norm_0 + found[2:3] + 2.0 * beta * found[3:4] + beta * beta * energy_0
    alpha_1 = norm_1 / curve
    control_ref[...] = (alpha_0 + alpha_1 * beta) * natural[0] + alpha_1 * natural[2]
    residual_ref[...] = natural[2] - alpha_1 * (natural[2] + natural[3] + beta * natural[1])


def hand_over(control, residual, control_out, residual_out):
    control_out[...] = control[...]
    residual_out[...] = residual[...]


def body(regions, tiles, kx, ky, mask, obs_owner, obs_row, obs_col, obs_weight, innovation, inverse_var):
    levels, rows_x, cols_y = kx.shape
    count = obs_row.shape[0]
    slots = tiles * CAP
    cells = rows_x * cols_y // GROUPS
    line, flat = (1, count), (levels * rows_x, cols_y)
    out = jax.ShapeDtypeStruct((32 * rows_x, cols_y), F32)
    dma = pltpu.SemaphoreType.DMA
    args = (
        kx.reshape(flat), ky.reshape(flat), mask.reshape(flat), obs_owner.reshape(line), obs_row.reshape(line),
        obs_col.reshape(line), innovation.reshape(line), inverse_var.reshape(line), obs_weight,
    )
    control, residual = pl.pallas_call(
        functools.partial(kernel, regions, tiles),
        out_shape=(out, out),
        in_specs=[pl.BlockSpec(memory_space=pl.ANY)] * 9,
        out_specs=[pl.BlockSpec(memory_space=pltpu.VMEM)] * 2,
        scratch_shapes=[
            *[pltpu.VMEM(x.shape, x.dtype) for x in args],
            pltpu.VMEM((EXCHANGES, cells, LANES), F32),
            pltpu.VMEM((EXCHANGES, 2, 32 * HALO, LANES), F32),
            pltpu.VMEM((EXCHANGES, 8, 8, LANES), F32),
            pltpu.VMEM((EXCHANGES, 8, 8, LANES), F32),
            pltpu.VMEM((EXCHANGES, 8, 8, LANES), F32),
            pltpu.VMEM((FRAME, LANES), F32),
            pltpu.VMEM((FRAME, LANES), F32),
            pltpu.VMEM((3, FRAME, LANES), F32),
            pltpu.VMEM((count, 3 * LANES), BF16),
            pltpu.VMEM((tiles, CAP, LANES), F32),
            pltpu.VMEM((tiles, CAP, LANES), F32),
            pltpu.VMEM((tiles, 1, LANES), F32),
            pltpu.VMEM((tiles, 1, LANES), F32),
            pltpu.VMEM((4, slots, LANES), F32),
            pltpu.VMEM((4, slots, LANES), F32),
            pltpu.VMEM((16, 24, LANES), F32),
            pltpu.VMEM((2, HALO, 24, LANES), F32),
            pltpu.VMEM((slots, 2 * cells), BF16),
            pltpu.VMEM((cells, 4 * slots), BF16),
            pltpu.VMEM((4 * slots, 2 * LANES), BF16),
            pltpu.VMEM((slots, LANES), F32),
            pltpu.VMEM((slots, LANES), F32),
            pltpu.VMEM((2, slots, LANES), F32),
            pltpu.VMEM((slots, LANES), F32),
            pltpu.VMEM((4, slots, LANES), F32),
            pltpu.VMEM((2 * cells, 4 * LANES), BF16),
            pltpu.VMEM((6, cells + 8, LANES), F32),
            pltpu.VMEM((4, cells, LANES), F32),
            pltpu.VMEM((2, 4, LANES), F32),
            pltpu.VMEM((2, regions, 4, LANES), F32),
            pltpu.VMEM((2, 4, LANES), F32),
            pltpu.VMEM((2, tiles, 4, LANES), F32),
            dma((9,)), dma((EXCHANGES,)), dma((EXCHANGES,)), dma((1,)), dma((tiles // 4,)), dma((2,)), dma((2, 2)), dma((2, 2)),
        ],
        compiler_params=pltpu.CompilerParams(collective_id=0, has_side_effects=True, vmem_limit_bytes=60 * 1024 * 1024),
    )(*args)
    control, residual = pl.pallas_call(
        hand_over,
        out_shape=(out, out),
        in_specs=[pl.BlockSpec(memory_space=pltpu.VMEM)] * 2,
        out_specs=[pl.BlockSpec(memory_space=pltpu.VMEM)] * 2,
        compiler_params=pltpu.CompilerParams(vmem_limit_bytes=60 * 1024 * 1024),
    )(control, residual)
    shape = (32 // levels, levels, rows_x, cols_y)
    return control.reshape(shape), residual.reshape(shape)


def solution(mesh):
    return jax.shard_map(
        functools.partial(body, mesh.shape["region"], mesh.shape["tile"]),
        mesh=mesh,
        in_specs=(
            P(None, "region", "tile"),
            P(None, "region", "tile"),
            P(None, "region", "tile"),
            P(("region", "tile"), None),
            P(("region", "tile")),
            P(("region", "tile")),
            P(("region", "tile"), None),
            P(("region", "tile")),
            P(("region", "tile")),
        ),
        out_specs=(P(None, None, "region", "tile"), P(None, None, "region", "tile")),
        check_vma=False,
    )
```

```python
import functools

import jax
import jax.numpy as jnp
from jax import lax
from jax.experimental import pallas as pl
from jax.experimental.pallas import tpu as pltpu
from jax.sharding import PartitionSpec as P

MESH = pl.DeviceIdType.MESH
F32 = jnp.float32
BF16 = jnp.bfloat16
CAP = 32
LANES = 128
GROUPS = 4
HALO = 8
WIDE = HALO + 32 + HALO
TALL = HALO + 16 + HALO
ROWS_AT_ONCE = 3
FRAME = (TALL + 3) * WIDE
EXCHANGES = 6


def iota(shape, dim):
    return lax.broadcasted_iota(jnp.int32, shape, dim)


def split(x, parts):
    out = []
    for i in range(parts):
        part = x.astype(BF16)
        out.append(part)
        if i + 1 < parts:
            x = x - part.astype(F32)
    return out


def dot(a, b):
    return jnp.dot(a, b, preferred_element_type=F32)


def dot_nt(a, b):
    return lax.dot_general(a, b, (((1,), (1,)), ((), ())), preferred_element_type=F32)


def swap_blocks(four):
    lane = iota(four[0].shape, 1)
    low = lane < 64
    even = (lane // 32) % 2 == 0
    a, b, c, d = four
    a, c = jnp.where(low, a, pltpu.roll(c, 64, 1)), jnp.where(low, pltpu.roll(a, 64, 1), c)
    b, d = jnp.where(low, b, pltpu.roll(d, 64, 1)), jnp.where(low, pltpu.roll(b, 64, 1), d)
    a, b = jnp.where(even, a, pltpu.roll(b, 32, 1)), jnp.where(even, pltpu.roll(a, 96, 1), b)
    c, d = jnp.where(even, c, pltpu.roll(d, 32, 1)), jnp.where(even, pltpu.roll(c, 96, 1), d)
    return a, b, c, d


def kernel(
    regions, tiles, kx_any, ky_any, mask_any, owner_any, row_any, col_any, innov_any, var_any, weight_any,
    natural_out, factor_out,
    kx_ref, ky_ref, mask_ref, owner_ref, row_ref, col_ref, innov_ref, var_ref, weight_ref,
    dense, rows_in, left_in, right_in, packed, frame_a, frame_b, coef, wsplit, wsend, wrecv, msend, mrecv, expanded, expanded_0, coef_rows, coef_in,
    pick, pick_t, terms, var_b, z_b, q_b, acc, group_b, state16, fields, natural, sums_send, sums_region, sums_mid, sums_tile,
    in_sem, out_sem, halo_send, halo_recv, w_send_sem, w_recv_sem, m_sem, r_sem, t_sem,
):
    reg, til = lax.axis_index("region"), lax.axis_index("tile")
    up, down = lax.rem(reg + regions - 1, regions), lax.rem(reg + 1, regions)
    left, right = lax.rem(til + tiles - 1, tiles), lax.rem(til + 1, tiles)
    count = owner_ref.shape[1]
    slots = tiles * CAP
    planes = tiles // 4
    late = []

    def wait_all(ref, sem):
        pltpu.make_async_copy(ref, ref, sem).wait()

    barrier = pltpu.get_barrier_semaphore()
    for i in sorted(range(1, tiles), key=lambda i: -min(i, tiles - i)):
        pl.semaphore_signal(barrier, inc=1, device_id=(reg, lax.rem(til + i, tiles)), device_id_type=MESH)
    for i in range(1, regions):
        pl.semaphore_signal(barrier, inc=1, device_id=(lax.rem(reg + i, regions), til), device_id_type=MESH)
    for a in (up, down):
        for b in (left, right):
            pl.semaphore_signal(barrier, inc=1, device_id=(a, b), device_id_type=MESH)

    pairs = (
        (owner_any, owner_ref), (row_any, row_ref), (col_any, col_ref), (innov_any, innov_ref), (var_any, var_ref),
        (weight_any, weight_ref), (mask_any, mask_ref), (kx_any, kx_ref), (ky_any, ky_ref),
    )
    loads = [pltpu.make_async_copy(a, b, in_sem.at[i]) for i, (a, b) in enumerate(pairs)]
    for c in loads:
        c.start()
    for c in loads[:5]:
        c.wait()
    lane8 = iota((8, LANES), 1)

    def halo_copies(e, deep, fields):
        def copy(src, dst, device):
            return pltpu.make_async_remote_copy(
                src_ref=src, dst_ref=dst, send_sem=halo_send.at[e], recv_sem=halo_recv.at[e],
                device_id=device, device_id_type=MESH)
        size, packs, at = deep * 32, deep // 4, pl.ds(e, fields)
        return [
            copy(packed.at[at, pl.ds(0, packs)], left_in.at[at, pl.ds(6, packs)], (up, right)),
            copy(packed.at[at, pl.ds(4 - packs, packs)], left_in.at[at, pl.ds(2 - packs, packs)], (down, right)),
            copy(packed.at[at, pl.ds(4, packs)], right_in.at[at, pl.ds(6, packs)], (up, left)),
            copy(packed.at[at, pl.ds(8 - packs, packs)], right_in.at[at, pl.ds(2 - packs, packs)], (down, left)),
            copy(packed.at[at, pl.ds(0, 4)], left_in.at[at, pl.ds(2, 4)], (reg, right)),
            copy(packed.at[at, pl.ds(4, 4)], right_in.at[at, pl.ds(2, 4)], (reg, left)),
            copy(coef_rows.at[pl.ds(0, 8)], coef_in.at[1], (up, til)) if e == 0 else
            copy(dense.at[e, pl.ds(0, size)], rows_in.at[e, 1, pl.ds(0, size)], (up, til)),
            copy(coef_rows.at[pl.ds(8, 8)], coef_in.at[0], (down, til)) if e == 0 else
            copy(dense.at[e, pl.ds(512 - size, size)], rows_in.at[e, 0, pl.ds(256 - size, size)], (down, til)),
        ]

    def halo_pack(e):
        for j in range(4):
            first = swap_blocks([dense[e, (4 * j + b) * 32:(4 * j + b) * 32 + 8, :] for b in range(4)])
            last = swap_blocks([dense[e, (4 * j + b) * 32 + 24:(4 * j + b) * 32 + 32, :] for b in range(4)])
            packed[e, j] = last[3]
            packed[e, 4 + j] = first[0]

    def halo_start(e, deep=8, fields=1):
        for c in halo_copies(e, deep, fields):
            c.start()
        amount = frame_b.at[pl.ds(0, 768 if e == 0 else 72 * deep + 64)]
        late.append(lambda: wait_all(amount, halo_send.at[e]))
        return lambda: wait_all(amount, halo_recv.at[e])

    def frame_own(e, out):
        def four_rows(j, _):
            for b in range(4):
                row = 4 * j + b
                base = pl.multiple_of((row + 8) * WIDE, 8)
                own = dense[e, pl.ds(pl.multiple_of(row * 32, 32), 32), :]
                out[pl.ds(base + 16, 32), :] = own
                out[pl.ds(base + 8, 8), :] = pltpu.roll(own[24:], 32, 1)
                out[pl.ds(base + WIDE, 8), :] = pltpu.roll(own[:8], 96, 1)
            return 0
        lax.fori_loop(0, 4, four_rows, 0)

    def frame_halo(e, out, deep=8):
        if e == 0:
            inside_up = jnp.where(reg > 0, 1.0, 0.0)
            inside_down = jnp.where(reg < regions - 1, 1.0, 0.0)
            rows_in[0, 0] = rows_in[0, 0] * inside_up
            rows_in[0, 1] = rows_in[0, 1] * inside_down
            for side, inside in ((left_in, jnp.where(til > 0, 1.0, 0.0)), (right_in, jnp.where(til < tiles - 1, 1.0, 0.0))):
                for j in range(8):
                    side[0, j] = side[0, j] * (inside * inside_up if j < 2 else inside if j < 6 else inside * inside_down)

        def beside(j, b):
            return pltpu.roll(left_in[e, j], -b * 32 % LANES, 1), pltpu.roll(right_in[e, j], (3 - b) * 32, 1)

        def own_rows(j, _):
            for b in range(4):
                base = pl.multiple_of((4 * j + b) * WIDE, 8)
                start, end = beside(j, b)
                out[pl.ds(base + 8, 8), :] = jnp.where(lane8 < 32, start, out[pl.ds(base + 8, 8), :])
                out[pl.ds(base + WIDE, 8), :] = jnp.where(lane8 >= 96, end, out[pl.ds(base + WIDE, 8), :])
            return 0

        lax.fori_loop(2, 6, own_rows, 0)
        for side in range(2):
            def outer_rows(j, _):
                for b in range(4):
                    row = 4 * j + b
                    base = pl.multiple_of((row + 24 * side) * WIDE, 8)
                    came = rows_in[e, side, pl.ds(pl.multiple_of(row * 32, 32), 32), :]
                    start, end = beside(j + 6 * side, b)
                    out[pl.ds(base + 16, 32), :] = came
                    out[pl.ds(base + 8, 8), :] = jnp.where(lane8 < 32, start, pltpu.roll(came[24:], 32, 1))
                    out[pl.ds(base + WIDE, 8), :] = jnp.where(lane8 >= 96, end, pltpu.roll(came[:8], 96, 1))
                return 0
            lax.fori_loop(0 if side else 2 - deep // 4, deep // 4 if side else 2, outer_rows, 0)

    def build_frame(e, arrive, out, deep=8, meanwhile=lambda: None):
        frame_own(e, out)
        drain()
        meanwhile()
        arrive()
        frame_halo(e, out, deep)

    def to_cells(line, out, rows):
        def four_rows(j, _):
            lines = [line(4 * j + b) for b in range(4)]
            many = jnp.concatenate([x for x in lines for _ in range(4)], axis=0).T
            for b, x in enumerate(swap_blocks([many[32 * g:32 * g + 32] for g in range(4)])):
                out[pl.ds(pl.multiple_of((4 * j + b) * 32, 32), 32), :] = x
            return 0
        lax.fori_loop(0, rows // 4, four_rows, 0)

    def to_natural(field, out):
        def four_rows(j, _):
            lines = [field[pl.ds(pl.multiple_of((4 * j + b) * 32, 32), 32), :] for b in range(4)]
            many = jnp.concatenate(swap_blocks(lines), axis=0).T
            for b in range(4):
                out[pl.ds(4 * j + b, 32, stride=16), :] = many[32 * b:32 * b + 32]
            return 0
        lax.fori_loop(0, 4, four_rows, 0)

    owner = owner_ref[...]
    marks = jnp.where(iota((tiles, count), 0) == owner, 1.0, 0.0)
    upper = jnp.where(iota((count, count), 0) < iota((count, count), 1), 1.0, 0.0).astype(BF16)
    before = dot(marks.astype(BF16), upper)
    slot = owner * CAP + jnp.sum(before * marks, axis=0, keepdims=True).astype(jnp.int32)
    meta_rows = [row_ref[...].astype(F32), col_ref[...].astype(F32)]
    meta_rows += [p.astype(F32) for p in split(innov_ref[...], 3) + split(var_ref[...], 3)]
    meta = jnp.zeros((8, count), F32)
    for i, line in enumerate(meta_rows):
        meta = jnp.where(iota((8, count), 0) == i, line, meta)
    meta = meta.astype(BF16)

    def choose(b, _):
        chosen = jnp.where(iota((LANES, count), 0) + b * LANES == slot, 1.0, 0.0).astype(BF16)
        pick[pl.ds(pl.multiple_of(b * LANES, LANES), LANES), :count] = chosen
        return 0

    lax.fori_loop(0, planes, choose, 0)
    facts = dot_nt(meta, pick[:, :count])
    place = facts[0:1] * LANES + facts[1:2]
    innov = facts[2:3] + facts[3:4] + facts[4:5]
    var = facts[5:6] + facts[6:7] + facts[7:8]
    for b in range(planes):
        at = slice(b * LANES, (b + 1) * LANES)
        three = [jnp.broadcast_to(x[:, at], (8, LANES)) for x in (place, innov, var)]
        for k in range(4):
            turned = [pltpu.roll(x, (i - k) * 32 % LANES, 1) for i, x in enumerate(three)]
            line = jnp.where(lane8 < 32, turned[0], jnp.where(lane8 < 64, turned[1], jnp.where(lane8 < 96, turned[2], 0.0)))
            msend[4 * b + k] = line[0:1]
    loads[5].wait()
    for i, part in enumerate(split(weight_ref[...], 3)):
        wsplit[:, i * LANES:(i + 1) * LANES] = part
    block = dot(pick[:, :count], wsplit[...])
    wsend[...] = (block[:, :LANES] + block[:, LANES:2 * LANES] + block[:, 2 * LANES:]).reshape(tiles, CAP, LANES)

    turns = sorted(range(planes), key=lambda i: (min(i, planes - i), i))
    plane, place_in = til // 4, lax.rem(til, 4)

    def sends(src, dst, send_sem, recv_sem, together):
        out = []
        for j, turn in enumerate(turns):
            for k in range(4):
                if j or k:
                    to = lax.rem(plane + turn, planes) * 4 + lax.rem(place_in + k, 4)
                    n = 4 * j + k
                    out.append(pltpu.make_async_remote_copy(
                        src_ref=src.at[to], dst_ref=dst.at[n], send_sem=send_sem, recv_sem=recv_sem.at[n // together],
                        device_id=(reg, to), device_id_type=MESH))
        return out

    def both_ways(copies):
        order = list(range(3))
        for j in range(1, planes, 2):
            order += [4 * i + k - 1 for k in range(4) for i in (j, j + 1) if i < planes]
        return [copies[i] for i in order]

    m_copies = sends(msend, mrecv, m_sem.at[0], m_sem.at[pl.ds(1, 1)], tiles)
    w_copies = sends(wsend, wrecv, w_send_sem.at[0], w_recv_sem, 4)
    late.append(lambda: wait_all(msend.at[pl.ds(1, tiles - 1)], m_sem.at[0]))
    late.append(lambda: wait_all(wsend.at[pl.ds(1, tiles - 1)], w_send_sem.at[0]))
    def drain():
        for wait in late:
            wait()
        late.clear()

    pl.semaphore_wait(barrier, (tiles - 1) + (regions - 1) + 4)
    for c in both_ways(m_copies) + both_ways(w_copies):
        c.start()
    wrecv[0] = wsend[til]
    mrecv[0] = msend[til]

    for c in loads[6:]:
        c.wait()

    def stage(r, _):
        for e, source in enumerate((mask_ref, kx_ref, ky_ref)):
            coef_rows[r, 8 * e:8 * e + 8, :] = source[pl.ds(r, 8, stride=16), :].astype(F32)
        return 0

    lax.fori_loop(0, 16, stage, 0)
    for e in range(3):
        to_cells(lambda r: coef_rows[r, 8 * e:8 * e + 8, :], dense.at[e], 16)
        halo_pack(e)
    coef_arrive = halo_start(0, 8, 3)

    def diffuse(first, last):
        for s in range(first, last + 1):
            src, dst = (frame_a, frame_b) if (s - first) % 2 == 0 else (frame_b, frame_a)

            def lines(i, carry):
                before, here, west = carry
                base = pl.multiple_of((s + ROWS_AT_ONCE * i) * WIDE, 8)
                for u in range(ROWS_AT_ONCE):
                    at = base + u * WIDE
                    after = src[pl.ds(at + WIDE, WIDE), :]
                    east = coef[1, pl.ds(at, WIDE), :]
                    out = (coef[0, pl.ds(at, WIDE), :] * here + east * after) + west * before
                    dst[pl.ds(at, WIDE), :] = out + (
                        coef[2, pl.ds(at, WIDE), :] * src[pl.ds(at + 1, WIDE), :]
                        + coef[2, pl.ds(at - 1, WIDE), :] * src[pl.ds(at - 1, WIDE), :])
                    before, here, west = here, after, east
                return before, here, west

            at = (s - 1) * WIDE
            rows = 16 if s == HALO else TALL + 1 - 2 * s
            lax.fori_loop(
                0, -(-rows // ROWS_AT_ONCE), lines, (src[at:at + WIDE, :], src[at + WIDE:at + 2 * WIDE, :], coef[1, at:at + WIDE, :]))

    def inner(out):
        for j in range(16):
            out[j * 32:(j + 1) * 32, :] = frame_a[(8 + j) * WIDE + 16:(9 + j) * WIDE, :]

    wait_all(mrecv.at[pl.ds(1, tiles - 1)], m_sem.at[1])
    lane = iota((LANES, LANES), 1)
    seat = iota((LANES, LANES), 0) % CAP
    ones = jnp.ones((3 * LANES, LANES), BF16)
    cells = pick_t.shape[0]

    def corner_of(place, c):
        row = (place >> 7) + c // 2
        col = (place & 127) + c % 2
        return row * 32 + (col & 31), col >> 5

    def read_facts(j, _):
        at = pl.ds(pl.multiple_of(j * LANES, LANES), LANES)
        facts = jnp.broadcast_to(mrecv[pl.ds(4 * j, 4)], (4, CAP, LANES)).reshape(LANES, LANES)

        def spread_lanes(kind):
            return jnp.concatenate(split(jnp.where(lane == seat + 32 * kind, facts, 0.0), 3), axis=1)

        place3 = spread_lanes(0)
        place_col = dot(place3, ones).astype(jnp.int32)
        place_row = dot_nt(jnp.ones((8, 3 * LANES), BF16), place3).astype(jnp.int32)[0:1]
        var = dot(spread_lanes(2), ones)
        var_b[at, :] = var
        z_b[at, :] = var * dot(spread_lanes(1), ones)
        for c in range(4):
            cell, group = corner_of(place_col, c)
            group_b[c, at, :] = jnp.where(group == lane // 32, 1.0, 0.0)
            if c == 0:
                for t in range(cells // LANES):
                    hit = jnp.where(cell == lane + t * LANES, 1.0, 0.0).astype(BF16)
                    pick[at, t * LANES:(t + 1) * LANES] = hit
                    pick[at, cells + t * LANES:cells + (t + 1) * LANES] = hit
            cell, _ = corner_of(place_row, c)
            there = pl.ds(pl.multiple_of((4 * j + c) * LANES, LANES), LANES)
            pick_t[:, there] = jnp.where(iota((cells, LANES), 0) == cell, 1.0, 0.0).astype(BF16)
        return 0

    lax.fori_loop(0, planes, read_facts, 0)

    def put_terms(j, c):
        at = pl.ds(pl.multiple_of(j * LANES, LANES), LANES)
        there = pl.ds(pl.multiple_of((4 * j + c) * LANES, LANES), LANES)
        hi, lo = split(z_b[at, :] * expanded[c, at, :], 2)
        terms[there, :LANES] = hi
        terms[there, LANES:] = lo

    for e in range(3):
        frame_own(e, coef.at[e])

    copy_lanes = jnp.where(
        iota((3 * LANES, 4 * LANES), 0) % LANES == iota((3 * LANES, 4 * LANES), 1) // LANES * 32 + iota((3 * LANES, 4 * LANES), 1) % 32,
        1.0, 0.0).astype(BF16)
    def take_plane(j, first):
        wait_all(wrecv.at[pl.ds(4 * j + first, 4 - first)], w_recv_sem.at[j])
        wide = dot(jnp.concatenate(split(wrecv[pl.ds(4 * j, 4)].reshape(LANES, LANES), 3), axis=1), copy_lanes)
        at = pl.ds(pl.multiple_of(j * LANES, LANES), LANES)
        for c in range(4):
            expanded[c, at, :] = wide[:, c * LANES:(c + 1) * LANES] * group_b[c, at, :]
            expanded_0[c, at, :] = wide[:, c * LANES:(c + 1) * LANES] * group_b[0, at, :]
            put_terms(j, c)
        there = pl.ds(pl.multiple_of(4 * j * LANES, LANES), 4 * LANES)
        part = dot(pick_t[:, there], terms[there, :])
        return part[:, :LANES] + part[:, LANES:]

    state16[...] = jnp.zeros_like(state16)
    dense[3] = take_plane(0, 1)

    def later_plane(j, _):
        dense[3] = dense[3] + take_plane(j, 0)
        return 0

    lax.fori_loop(1, planes, later_plane, 0)

    def adjoint(e):
        def one(j, _):
            for c in range(4):
                put_terms(j, c)
            return 0
        lax.fori_loop(0, planes, one, 0)
        total = dot(pick_t[...], terms[...])
        dense[e] = total[:, :LANES] + total[:, LANES:]

    def observe(field, n):
        def corners(r, _):
            at = pl.multiple_of(r * 32, 32)
            here = field[pl.ds(at, 32), :]
            past = jnp.broadcast_to(pltpu.roll(here[:8], 96, 1)[0:1], (32, LANES))
            beside = jnp.where(iota((32, LANES), 0) == 31, past, field[pl.ds(at + 1, 32), :])
            above = pl.multiple_of(jnp.maximum(at - 32, 0), 32)
            for c, value in enumerate((here, beside)):
                for h, part in enumerate(split(value, 2)):
                    state16[pl.ds(h * cells + at, 32), c * LANES:(c + 1) * LANES] = part
                    state16[pl.ds(h * cells + above, 32), (2 + c) * LANES:(3 + c) * LANES] = part
            return 0

        lax.fori_loop(0, 16, corners, 0)
        acc[...] = jnp.zeros_like(acc)

        def one(i, _):
            values = dot(pick[...], state16[:, pl.ds(pl.multiple_of(i * 2 * LANES, LANES), 2 * LANES)])
            acc[...] += values[:, :LANES] * expanded_0[2 * i] + values[:, LANES:] * expanded_0[2 * i + 1]
            return 0

        lax.fori_loop(0, 2, one, 0)
        q = jnp.broadcast_to(jnp.sum(acc[...], axis=1, keepdims=True), acc.shape)
        q_b[n] = q

    def sums_start(n, sums):
        for i in range(4):
            sums_send[n, i:i + 1, :] = sums[i] if i < len(sums) else jnp.zeros((1, LANES), F32)
        for i in sorted(range(1, tiles), key=lambda i: -min(i, tiles - i)):
            pltpu.make_async_remote_copy(
                src_ref=sums_send.at[n], dst_ref=sums_tile.at[n, i], send_sem=t_sem.at[n, 0], recv_sem=t_sem.at[n, 1],
                device_id=(reg, lax.rem(til + i, tiles)), device_id_type=MESH).start()
        late.append(lambda: wait_all(sums_tile.at[n, pl.ds(1, tiles - 1)], t_sem.at[n, 0]))
        sums_tile[n, 0] = sums_send[n]

    def sums_middle(n):
        wait_all(sums_tile.at[n, pl.ds(1, tiles - 1)], t_sem.at[n, 1])
        sums_mid[n] = jnp.sum(sums_tile[n], axis=0)
        for i in sorted(range(1, regions), key=lambda i: -min(i, regions - i)):
            pltpu.make_async_remote_copy(
                src_ref=sums_mid.at[n], dst_ref=sums_region.at[n, i], send_sem=r_sem.at[n, 0], recv_sem=r_sem.at[n, 1],
                device_id=(lax.rem(reg + i, regions), til), device_id_type=MESH).start()
        late.append(lambda: wait_all(sums_region.at[n, pl.ds(1, regions - 1)], r_sem.at[n, 0]))
        sums_region[n, 0] = sums_mid[n]

    def sums_finish(n):
        wait_all(sums_region.at[n, pl.ds(1, regions - 1)], r_sem.at[n, 1])
        return jnp.sum(jnp.sum(sums_region[n], axis=0), axis=1, keepdims=True)

    def product(a, b):
        return jnp.sum(a * b, axis=0, keepdims=True)

    lane1 = iota((1, LANES), 1)

    def energy(a, b):
        return jnp.where(lane1 == 0, product(var_b[...] * q_b[a], q_b[b]), 0.0)

    halo_pack(3)
    arrive = halo_start(3)

    coef_arrive()
    for e in range(3):
        for side in range(2):
            to_cells(lambda r: coef_in[side, r, 8 * e:8 * e + 8, :], rows_in.at[e, side], 8)
        frame_halo(e, coef.at[e])

    def make_faces(k, _):
        base = pl.multiple_of(k * WIDE, 8)
        wet = coef[0, pl.ds(base, WIDE), :]
        coef[1, pl.ds(base, WIDE), :] = coef[1, pl.ds(base, WIDE), :] * wet * coef[0, pl.ds(base + WIDE, WIDE), :]
        coef[2, pl.ds(base, WIDE), :] = coef[2, pl.ds(base, WIDE), :] * wet * coef[0, pl.ds(base + 1, WIDE), :]
        return 0

    lax.fori_loop(0, TALL, make_faces, 0)

    def make_centre(k, _):
        base = pl.multiple_of(k * WIDE, 8)
        faces = coef[1, pl.ds(base, WIDE), :] + coef[1, pl.ds(base - WIDE, WIDE), :]
        faces = faces + coef[2, pl.ds(base, WIDE), :] + coef[2, pl.ds(base - 1, WIDE), :]
        coef[0, pl.ds(base, WIDE), :] = coef[0, pl.ds(base, WIDE), :] - faces
        return 0

    lax.fori_loop(1, TALL, make_centre, 0)

    build_frame(3, arrive, frame_a)
    diffuse(1, 4)
    inner(fields.at[0])
    diffuse(5, 8)
    inner(fields.at[1])

    norm = product(fields[0, :512, :], fields[0, :512, :])
    observe(fields.at[1], 0)
    sums_start(0, (norm, energy(0, 0)))
    z_b[...] = var_b[...] * q_b[0]
    adjoint(4)
    halo_pack(4)
    arrive = halo_start(4)
    to_natural(fields.at[0], natural.at[0])
    leaving = [pltpu.make_async_copy(natural.at[i], natural_out.at[i], out_sem.at[i]) for i in range(4)]
    leaving[0].start()
    build_frame(4, arrive, frame_a)
    diffuse(1, 4)
    sums_middle(0)
    inner(fields.at[2])
    diffuse(5, 8)
    inner(fields.at[4])
    observe(fields.at[4], 1)
    fields[2, :512, :] = fields[0, :512, :] + fields[2, :512, :]
    found = sums_finish(0)
    norm_0, energy_0 = found[0:1], found[1:2]
    alpha_0 = norm_0 / (norm_0 + energy_0)
    q_b[1] = q_b[0] - alpha_0 * (q_b[0] + q_b[1])
    fields[3, :512, :] = fields[0, :512, :] - alpha_0 * fields[2, :512, :]
    sums_start(1, (
        product(fields[3, :512, :], fields[3, :512, :]), product(fields[3, :512, :], fields[0, :512, :]), energy(1, 1), energy(1, 0)))
    z_b[...] = var_b[...] * q_b[1]
    adjoint(5)
    halo_pack(5)
    arrive = halo_start(5, 4)
    for i in (1, 2):
        to_natural(fields.at[i + 1], natural.at[i])
        leaving[i].start()
    build_frame(5, arrive, frame_a, 4, lambda: sums_middle(1))
    diffuse(5, 8)
    inner(fields.at[5])
    to_natural(fields.at[5], natural.at[3])
    leaving[3].start()
    drain()
    found = sums_finish(1)
    norm_1 = found[0:1]
    beta = norm_1 / norm_0
    curve = norm_1 + 2.0 * beta * found[1:2] + beta * beta * norm_0 + found[2:3] + 2.0 * beta * found[3:4] + beta * beta * energy_0
    alpha_1 = norm_1 / curve
    factor_out[...] = jnp.zeros_like(factor_out)
    for i, x in enumerate((alpha_0 + alpha_1 * beta, alpha_1, alpha_1 * beta)):
        factor_out[i:i + 1, :] = jnp.broadcast_to(x, (1, LANES))
    for c in leaving:
        c.wait()


def combine(natural, factor, control, residual):
    whole, second, mixed = factor[0:1, :], factor[1:2, :], factor[2:3, :]
    control[...] = whole * natural[0] + second * natural[2]
    residual[...] = natural[2] - second * (natural[2] + natural[3]) - mixed * natural[1]


def body(regions, tiles, kx, ky, mask, obs_owner, obs_row, obs_col, obs_weight, innovation, inverse_var):
    levels, rows_x, cols_y = kx.shape
    count = obs_row.shape[0]
    slots = tiles * CAP
    cells = rows_x * cols_y // GROUPS
    line, flat = (1, count), (levels * rows_x, cols_y)
    out = jax.ShapeDtypeStruct((32 * rows_x, cols_y), F32)
    dma = pltpu.SemaphoreType.DMA
    args = (
        kx.reshape(flat), ky.reshape(flat), mask.reshape(flat), obs_owner.reshape(line), obs_row.reshape(line),
        obs_col.reshape(line), innovation.reshape(line), inverse_var.reshape(line), obs_weight,
    )
    natural, factor = pl.pallas_call(
        functools.partial(kernel, regions, tiles),
        out_shape=(jax.ShapeDtypeStruct((4, 32 * rows_x, cols_y), F32), jax.ShapeDtypeStruct((8, LANES), F32)),
        in_specs=[pl.BlockSpec(memory_space=pl.ANY)] * 9,
        out_specs=[pl.BlockSpec(memory_space=pl.ANY), pl.BlockSpec(memory_space=pltpu.VMEM)],
        scratch_shapes=[
            *[pltpu.VMEM(x.shape, x.dtype) for x in args],
            pltpu.VMEM((EXCHANGES, cells, LANES), F32),
            pltpu.VMEM((EXCHANGES, 2, 32 * HALO, LANES), F32),
            pltpu.VMEM((EXCHANGES, 8, 8, LANES), F32),
            pltpu.VMEM((EXCHANGES, 8, 8, LANES), F32),
            pltpu.VMEM((EXCHANGES, 8, 8, LANES), F32),
            pltpu.VMEM((FRAME, LANES), F32),
            pltpu.VMEM((FRAME, LANES), F32),
            pltpu.VMEM((3, FRAME, LANES), F32),
            pltpu.VMEM((count, 3 * LANES), BF16),
            pltpu.VMEM((tiles, CAP, LANES), F32),
            pltpu.VMEM((tiles, CAP, LANES), F32),
            pltpu.VMEM((tiles, 1, LANES), F32),
            pltpu.VMEM((tiles, 1, LANES), F32),
            pltpu.VMEM((4, slots, LANES), F32),
            pltpu.VMEM((4, slots, LANES), F32),
            pltpu.VMEM((16, 24, LANES), F32),
            pltpu.VMEM((2, HALO, 24, LANES), F32),
            pltpu.VMEM((slots, 2 * cells), BF16),
            pltpu.VMEM((cells, 4 * slots), BF16),
            pltpu.VMEM((4 * slots, 2 * LANES), BF16),
            pltpu.VMEM((slots, LANES), F32),
            pltpu.VMEM((slots, LANES), F32),
            pltpu.VMEM((2, slots, LANES), F32),
            pltpu.VMEM((slots, LANES), F32),
            pltpu.VMEM((4, slots, LANES), F32),
            pltpu.VMEM((2 * cells, 4 * LANES), BF16),
            pltpu.VMEM((6, cells + 8, LANES), F32),
            pltpu.VMEM((4, cells, LANES), F32),
            pltpu.VMEM((2, 4, LANES), F32),
            pltpu.VMEM((2, regions, 4, LANES), F32),
            pltpu.VMEM((2, 4, LANES), F32),
            pltpu.VMEM((2, tiles, 4, LANES), F32),
            dma((9,)), dma((4,)), dma((EXCHANGES,)), dma((EXCHANGES,)), dma((1,)), dma((tiles // 4,)), dma((2,)), dma((2, 2)), dma((2, 2)),
        ],
        compiler_params=pltpu.CompilerParams(collective_id=0, has_side_effects=True, vmem_limit_bytes=60 * 1024 * 1024),
    )(*args)
    control, residual = pl.pallas_call(
        combine,
        out_shape=(out, out),
        in_specs=[pl.BlockSpec(memory_space=pltpu.VMEM)] * 2,
        out_specs=[pl.BlockSpec(memory_space=pltpu.VMEM)] * 2,
        compiler_params=pltpu.CompilerParams(vmem_limit_bytes=60 * 1024 * 1024),
    )(natural, factor)
    shape = (32 // levels, levels, rows_x, cols_y)
    return control.reshape(shape), residual.reshape(shape)


def solution(mesh):
    return jax.shard_map(
        functools.partial(body, mesh.shape["region"], mesh.shape["tile"]),
        mesh=mesh,
        in_specs=(
            P(None, "region", "tile"),
            P(None, "region", "tile"),
            P(None, "region", "tile"),
            P(("region", "tile"), None),
            P(("region", "tile")),
            P(("region", "tile")),
            P(("region", "tile"), None),
            P(("region", "tile")),
            P(("region", "tile")),
        ),
        out_specs=(P(None, None, "region", "tile"), P(None, None, "region", "tile")),
        check_vma=False,
    )
```

```python
import functools

import jax
import jax.numpy as jnp
from jax import lax
from jax.experimental import pallas as pl
from jax.experimental.pallas import tpu as pltpu
from jax.sharding import PartitionSpec as P

MESH = pl.DeviceIdType.MESH
F32 = jnp.float32
BF16 = jnp.bfloat16
CAP = 32
LANES = 128
GROUPS = 4
HALO = 8
WIDE = HALO + 32 + HALO
TALL = HALO + 16 + HALO
ROWS_AT_ONCE = 3
FRAME = (TALL + 3) * WIDE
EXCHANGES = 6


def iota(shape, dim):
    return lax.broadcasted_iota(jnp.int32, shape, dim)


def split(x, parts):
    out = []
    for i in range(parts):
        part = x.astype(BF16)
        out.append(part)
        if i + 1 < parts:
            x = x - part.astype(F32)
    return out


def dot(a, b):
    return jnp.dot(a, b, preferred_element_type=F32)


def dot_nt(a, b):
    return lax.dot_general(a, b, (((1,), (1,)), ((), ())), preferred_element_type=F32)


def swap_blocks(four):
    lane = iota(four[0].shape, 1)
    low = lane < 64
    even = (lane // 32) % 2 == 0
    a, b, c, d = four
    a, c = jnp.where(low, a, pltpu.roll(c, 64, 1)), jnp.where(low, pltpu.roll(a, 64, 1), c)
    b, d = jnp.where(low, b, pltpu.roll(d, 64, 1)), jnp.where(low, pltpu.roll(b, 64, 1), d)
    a, b = jnp.where(even, a, pltpu.roll(b, 32, 1)), jnp.where(even, pltpu.roll(a, 96, 1), b)
    c, d = jnp.where(even, c, pltpu.roll(d, 32, 1)), jnp.where(even, pltpu.roll(c, 96, 1), d)
    return a, b, c, d


def kernel(
    regions, tiles, kx_any, ky_any, mask_any, owner_any, row_any, col_any, innov_any, var_any, weight_any,
    natural_out, factor_out,
    kx_ref, ky_ref, mask_ref, owner_ref, row_ref, col_ref, innov_ref, var_ref, weight_ref,
    dense, rows_in, left_in, right_in, packed, frame_a, frame_b, coef, wsplit, wsend, wrecv, msend, mrecv, expanded, expanded_0, coef_rows, coef_in,
    pick, pick_t, terms, var_b, z_b, q_b, acc, group_b, state16, fields, natural, sums_send, sums_region, sums_mid, sums_tile,
    in_sem, out_sem, halo_send, halo_recv, w_send_sem, w_recv_sem, m_sem, r_sem, t_sem,
):
    reg, til = lax.axis_index("region"), lax.axis_index("tile")
    up, down = lax.rem(reg + regions - 1, regions), lax.rem(reg + 1, regions)
    left, right = lax.rem(til + tiles - 1, tiles), lax.rem(til + 1, tiles)
    count = owner_ref.shape[1]
    slots = tiles * CAP
    planes = tiles // 4
    late = []

    def wait_all(ref, sem):
        pltpu.make_async_copy(ref, ref, sem).wait()

    barrier = pltpu.get_barrier_semaphore()
    for i in sorted(range(1, tiles), key=lambda i: -min(i, tiles - i)):
        pl.semaphore_signal(barrier, inc=1, device_id=(reg, lax.rem(til + i, tiles)), device_id_type=MESH)
    for i in range(1, regions):
        pl.semaphore_signal(barrier, inc=1, device_id=(lax.rem(reg + i, regions), til), device_id_type=MESH)
    for a in (up, down):
        for b in (left, right):
            pl.semaphore_signal(barrier, inc=1, device_id=(a, b), device_id_type=MESH)

    pairs = (
        (owner_any, owner_ref), (row_any, row_ref), (col_any, col_ref), (innov_any, innov_ref), (var_any, var_ref),
        (weight_any, weight_ref), (mask_any, mask_ref), (kx_any, kx_ref), (ky_any, ky_ref),
    )
    loads = [pltpu.make_async_copy(a, b, in_sem.at[i]) for i, (a, b) in enumerate(pairs)]
    for c in loads:
        c.start()
    for c in loads[:5]:
        c.wait()
    lane8 = iota((8, LANES), 1)

    def halo_copies(e, deep, fields):
        def copy(src, dst, device):
            return pltpu.make_async_remote_copy(
                src_ref=src, dst_ref=dst, send_sem=halo_send.at[e], recv_sem=halo_recv.at[e],
                device_id=device, device_id_type=MESH)
        size, packs, at = deep * 32, deep // 4, pl.ds(e, fields)
        return [
            copy(packed.at[at, pl.ds(0, packs)], left_in.at[at, pl.ds(6, packs)], (up, right)),
            copy(packed.at[at, pl.ds(4 - packs, packs)], left_in.at[at, pl.ds(2 - packs, packs)], (down, right)),
            copy(packed.at[at, pl.ds(4, packs)], right_in.at[at, pl.ds(6, packs)], (up, left)),
            copy(packed.at[at, pl.ds(8 - packs, packs)], right_in.at[at, pl.ds(2 - packs, packs)], (down, left)),
            copy(packed.at[at, pl.ds(0, 4)], left_in.at[at, pl.ds(2, 4)], (reg, right)),
            copy(packed.at[at, pl.ds(4, 4)], right_in.at[at, pl.ds(2, 4)], (reg, left)),
            copy(coef_rows.at[pl.ds(0, 8)], coef_in.at[1], (up, til)) if e == 0 else
            copy(dense.at[e, pl.ds(0, size)], rows_in.at[e, 1, pl.ds(0, size)], (up, til)),
            copy(coef_rows.at[pl.ds(8, 8)], coef_in.at[0], (down, til)) if e == 0 else
            copy(dense.at[e, pl.ds(512 - size, size)], rows_in.at[e, 0, pl.ds(256 - size, size)], (down, til)),
        ]

    def halo_pack(e):
        for j in range(4):
            first = swap_blocks([dense[e, (4 * j + b) * 32:(4 * j + b) * 32 + 8, :] for b in range(4)])
            last = swap_blocks([dense[e, (4 * j + b) * 32 + 24:(4 * j + b) * 32 + 32, :] for b in range(4)])
            packed[e, j] = last[3]
            packed[e, 4 + j] = first[0]

    def halo_start(e, deep=8, fields=1):
        copies = halo_copies(e, deep, fields)
        for c in copies[6:]:
            c.start()
        if e == 0:
            for i in range(3):
                to_cells(lambda r: coef_rows[r, 8 * i:8 * i + 8, :], dense.at[i], 16)
        for i in range(fields):
            halo_pack(e + i)
        for c in copies[:6]:
            c.start()
        amount = frame_b.at[pl.ds(0, 768 if e == 0 else 72 * deep + 64)]
        late.append(lambda: wait_all(amount, halo_send.at[e]))
        return lambda: wait_all(amount, halo_recv.at[e])

    def frame_own(e, out):
        def four_rows(j, _):
            for b in range(4):
                row = 4 * j + b
                base = pl.multiple_of((row + 8) * WIDE, 8)
                own = dense[e, pl.ds(pl.multiple_of(row * 32, 32), 32), :]
                out[pl.ds(base + 16, 32), :] = own
                out[pl.ds(base + 8, 8), :] = pltpu.roll(own[24:], 32, 1)
                out[pl.ds(base + WIDE, 8), :] = pltpu.roll(own[:8], 96, 1)
            return 0
        lax.fori_loop(0, 4, four_rows, 0)

    def frame_halo(e, out, deep=8):
        if e == 0:
            inside_up = jnp.where(reg > 0, 1.0, 0.0)
            inside_down = jnp.where(reg < regions - 1, 1.0, 0.0)
            rows_in[0, 0] = rows_in[0, 0] * inside_up
            rows_in[0, 1] = rows_in[0, 1] * inside_down
            for side, inside in ((left_in, jnp.where(til > 0, 1.0, 0.0)), (right_in, jnp.where(til < tiles - 1, 1.0, 0.0))):
                for j in range(8):
                    side[0, j] = side[0, j] * (inside * inside_up if j < 2 else inside if j < 6 else inside * inside_down)

        def beside(j, b):
            return pltpu.roll(left_in[e, j], -b * 32 % LANES, 1), pltpu.roll(right_in[e, j], (3 - b) * 32, 1)

        def own_rows(j, _):
            for b in range(4):
                base = pl.multiple_of((4 * j + b) * WIDE, 8)
                start, end = beside(j, b)
                out[pl.ds(base + 8, 8), :] = jnp.where(lane8 < 32, start, out[pl.ds(base + 8, 8), :])
                out[pl.ds(base + WIDE, 8), :] = jnp.where(lane8 >= 96, end, out[pl.ds(base + WIDE, 8), :])
            return 0

        lax.fori_loop(2, 6, own_rows, 0)
        for side in range(2):
            def outer_rows(j, _):
                for b in range(4):
                    row = 4 * j + b
                    base = pl.multiple_of((row + 24 * side) * WIDE, 8)
                    came = rows_in[e, side, pl.ds(pl.multiple_of(row * 32, 32), 32), :]
                    start, end = beside(j + 6 * side, b)
                    out[pl.ds(base + 16, 32), :] = came
                    out[pl.ds(base + 8, 8), :] = jnp.where(lane8 < 32, start, pltpu.roll(came[24:], 32, 1))
                    out[pl.ds(base + WIDE, 8), :] = jnp.where(lane8 >= 96, end, pltpu.roll(came[:8], 96, 1))
                return 0
            lax.fori_loop(0 if side else 2 - deep // 4, deep // 4 if side else 2, outer_rows, 0)

    def build_frame(e, arrive, out, deep=8, meanwhile=lambda: None):
        frame_own(e, out)
        drain()
        meanwhile()
        arrive()
        frame_halo(e, out, deep)

    def to_cells(line, out, rows):
        def four_rows(j, _):
            lines = [line(4 * j + b) for b in range(4)]
            many = jnp.concatenate([x for x in lines for _ in range(4)], axis=0).T
            for b, x in enumerate(swap_blocks([many[32 * g:32 * g + 32] for g in range(4)])):
                out[pl.ds(pl.multiple_of((4 * j + b) * 32, 32), 32), :] = x
            return 0
        lax.fori_loop(0, rows // 4, four_rows, 0)

    def to_natural(field, out):
        def four_rows(j, _):
            lines = [field[pl.ds(pl.multiple_of((4 * j + b) * 32, 32), 32), :] for b in range(4)]
            many = jnp.concatenate(swap_blocks(lines), axis=0).T
            for b in range(4):
                out[pl.ds(4 * j + b, 32, stride=16), :] = many[32 * b:32 * b + 32]
            return 0
        lax.fori_loop(0, 4, four_rows, 0)

    owner = owner_ref[...]
    marks = jnp.where(iota((tiles, count), 0) == owner, 1.0, 0.0)
    upper = jnp.where(iota((count, count), 0) < iota((count, count), 1), 1.0, 0.0).astype(BF16)
    before = dot(marks.astype(BF16), upper)
    slot = owner * CAP + jnp.sum(before * marks, axis=0, keepdims=True).astype(jnp.int32)
    meta_rows = [row_ref[...].astype(F32), col_ref[...].astype(F32)]
    meta_rows += [p.astype(F32) for p in split(innov_ref[...], 3) + split(var_ref[...], 3)]
    meta = jnp.zeros((8, count), F32)
    for i, line in enumerate(meta_rows):
        meta = jnp.where(iota((8, count), 0) == i, line, meta)
    meta = meta.astype(BF16)

    def choose(b, _):
        chosen = jnp.where(iota((LANES, count), 0) + b * LANES == slot, 1.0, 0.0).astype(BF16)
        pick[pl.ds(pl.multiple_of(b * LANES, LANES), LANES), :count] = chosen
        return 0

    lax.fori_loop(0, planes, choose, 0)
    facts = dot_nt(meta, pick[:, :count])
    place = facts[0:1] * LANES + facts[1:2]
    innov = facts[2:3] + facts[3:4] + facts[4:5]
    var = facts[5:6] + facts[6:7] + facts[7:8]
    for b in range(planes):
        at = slice(b * LANES, (b + 1) * LANES)
        three = [jnp.broadcast_to(x[:, at], (8, LANES)) for x in (place, innov, var)]
        for k in range(4):
            turned = [pltpu.roll(x, (i - k) * 32 % LANES, 1) for i, x in enumerate(three)]
            line = jnp.where(lane8 < 32, turned[0], jnp.where(lane8 < 64, turned[1], jnp.where(lane8 < 96, turned[2], 0.0)))
            msend[4 * b + k] = line[0:1]
    loads[5].wait()
    for i, part in enumerate(split(weight_ref[...], 3)):
        wsplit[:, i * LANES:(i + 1) * LANES] = part
    block = dot(pick[:, :count], wsplit[...])
    wsend[...] = (block[:, :LANES] + block[:, LANES:2 * LANES] + block[:, 2 * LANES:]).reshape(tiles, CAP, LANES)

    turns = sorted(range(planes), key=lambda i: (min(i, planes - i), i))
    plane, place_in = til // 4, lax.rem(til, 4)

    def sends(src, dst, send_sem, recv_sem, together):
        out = []
        for j, turn in enumerate(turns):
            for k in range(4):
                if j or k:
                    to = lax.rem(plane + turn, planes) * 4 + lax.rem(place_in + k, 4)
                    n = 4 * j + k
                    out.append(pltpu.make_async_remote_copy(
                        src_ref=src.at[to], dst_ref=dst.at[n], send_sem=send_sem, recv_sem=recv_sem.at[n // together],
                        device_id=(reg, to), device_id_type=MESH))
        return out

    def both_ways(copies):
        order = list(range(3))
        for j in range(1, planes, 2):
            order += [4 * i + k - 1 for k in range(4) for i in (j, j + 1) if i < planes]
        return [copies[i] for i in order]

    m_copies = sends(msend, mrecv, m_sem.at[0], m_sem.at[pl.ds(1, 1)], tiles)
    w_copies = sends(wsend, wrecv, w_send_sem.at[0], w_recv_sem, 4)
    late.append(lambda: wait_all(msend.at[pl.ds(1, tiles - 1)], m_sem.at[0]))
    late.append(lambda: wait_all(wsend.at[pl.ds(1, tiles - 1)], w_send_sem.at[0]))
    def drain():
        for wait in late:
            wait()
        late.clear()

    pl.semaphore_wait(barrier, (tiles - 1) + (regions - 1) + 4)
    for c in both_ways(m_copies) + both_ways(w_copies):
        c.start()
    wrecv[0] = wsend[til]
    mrecv[0] = msend[til]

    for c in loads[6:]:
        c.wait()

    def stage(r, _):
        for e, source in enumerate((mask_ref, kx_ref, ky_ref)):
            coef_rows[r, 8 * e:8 * e + 8, :] = source[pl.ds(r, 8, stride=16), :].astype(F32)
        return 0

    lax.fori_loop(0, 16, stage, 0)
    coef_arrive = halo_start(0, 8, 3)

    def diffuse(first, last):
        for s in range(first, last + 1):
            src, dst = (frame_a, frame_b) if (s - first) % 2 == 0 else (frame_b, frame_a)

            def lines(i, carry):
                before, here, west = carry
                base = pl.multiple_of((s + ROWS_AT_ONCE * i) * WIDE, 8)
                for u in range(ROWS_AT_ONCE):
                    at = base + u * WIDE
                    after = src[pl.ds(at + WIDE, WIDE), :]
                    east = coef[1, pl.ds(at, WIDE), :]
                    out = (coef[0, pl.ds(at, WIDE), :] * here + east * after) + west * before
                    dst[pl.ds(at, WIDE), :] = out + (
                        coef[2, pl.ds(at, WIDE), :] * src[pl.ds(at + 1, WIDE), :]
                        + coef[2, pl.ds(at - 1, WIDE), :] * src[pl.ds(at - 1, WIDE), :])
                    before, here, west = here, after, east
                return before, here, west

            at = (s - 1) * WIDE
            rows = 16 if s == HALO else TALL + 1 - 2 * s
            lax.fori_loop(
                0, -(-rows // ROWS_AT_ONCE), lines, (src[at:at + WIDE, :], src[at + WIDE:at + 2 * WIDE, :], coef[1, at:at + WIDE, :]))

    def inner(out):
        for j in range(16):
            out[j * 32:(j + 1) * 32, :] = frame_a[(8 + j) * WIDE + 16:(9 + j) * WIDE, :]

    wait_all(mrecv.at[pl.ds(1, tiles - 1)], m_sem.at[1])
    lane = iota((LANES, LANES), 1)
    seat = iota((LANES, LANES), 0) % CAP
    ones = jnp.ones((3 * LANES, LANES), BF16)
    cells = pick_t.shape[0]

    def corner_of(place, c):
        row = (place >> 7) + c // 2
        col = (place & 127) + c % 2
        return row * 32 + (col & 31), col >> 5

    def read_facts(j, _):
        at = pl.ds(pl.multiple_of(j * LANES, LANES), LANES)
        facts = jnp.broadcast_to(mrecv[pl.ds(4 * j, 4)], (4, CAP, LANES)).reshape(LANES, LANES)

        def spread_lanes(kind):
            return jnp.concatenate(split(jnp.where(lane == seat + 32 * kind, facts, 0.0), 3), axis=1)

        place3 = spread_lanes(0)
        place_col = dot(place3, ones).astype(jnp.int32)
        place_row = dot_nt(jnp.ones((8, 3 * LANES), BF16), place3).astype(jnp.int32)[0:1]
        var = dot(spread_lanes(2), ones)
        var_b[at, :] = var
        z_b[at, :] = var * dot(spread_lanes(1), ones)
        for c in range(4):
            cell, group = corner_of(place_col, c)
            group_b[c, at, :] = jnp.where(group == lane // 32, 1.0, 0.0)
            if c == 0:
                for t in range(cells // LANES):
                    hit = jnp.where(cell == lane + t * LANES, 1.0, 0.0).astype(BF16)
                    pick[at, t * LANES:(t + 1) * LANES] = hit
                    pick[at, cells + t * LANES:cells + (t + 1) * LANES] = hit
            cell, _ = corner_of(place_row, c)
            there = pl.ds(pl.multiple_of((4 * j + c) * LANES, LANES), LANES)
            pick_t[:, there] = jnp.where(iota((cells, LANES), 0) == cell, 1.0, 0.0).astype(BF16)
        return 0

    lax.fori_loop(0, planes, read_facts, 0)

    def put_terms(j, c):
        at = pl.ds(pl.multiple_of(j * LANES, LANES), LANES)
        there = pl.ds(pl.multiple_of((4 * j + c) * LANES, LANES), LANES)
        hi, lo = split(z_b[at, :] * expanded[c, at, :], 2)
        terms[there, :LANES] = hi
        terms[there, LANES:] = lo

    for e in range(3):
        frame_own(e, coef.at[e])

    copy_lanes = jnp.where(
        iota((3 * LANES, 4 * LANES), 0) % LANES == iota((3 * LANES, 4 * LANES), 1) // LANES * 32 + iota((3 * LANES, 4 * LANES), 1) % 32,
        1.0, 0.0).astype(BF16)
    def take_plane(j, first):
        wait_all(wrecv.at[pl.ds(4 * j + first, 4 - first)], w_recv_sem.at[j])
        wide = dot(jnp.concatenate(split(wrecv[pl.ds(4 * j, 4)].reshape(LANES, LANES), 3), axis=1), copy_lanes)
        at = pl.ds(pl.multiple_of(j * LANES, LANES), LANES)
        for c in range(4):
            expanded[c, at, :] = wide[:, c * LANES:(c + 1) * LANES] * group_b[c, at, :]
            expanded_0[c, at, :] = wide[:, c * LANES:(c + 1) * LANES] * group_b[0, at, :]
            put_terms(j, c)
        there = pl.ds(pl.multiple_of(4 * j * LANES, LANES), 4 * LANES)
        part = dot(pick_t[:, there], terms[there, :])
        return part[:, :LANES] + part[:, LANES:]

    state16[...] = jnp.zeros_like(state16)
    dense[3] = take_plane(0, 1)

    def later_plane(j, _):
        dense[3] = dense[3] + take_plane(j, 0)
        return 0

    lax.fori_loop(1, planes, later_plane, 0)

    def adjoint(e):
        def one(j, _):
            for c in range(4):
                put_terms(j, c)
            return 0
        lax.fori_loop(0, planes, one, 0)
        total = dot(pick_t[...], terms[...])
        dense[e] = total[:, :LANES] + total[:, LANES:]

    def observe(field, n):
        def corners(r, _):
            at = pl.multiple_of(r * 32, 32)
            here = field[pl.ds(at, 32), :]
            past = jnp.broadcast_to(pltpu.roll(here[:8], 96, 1)[0:1], (32, LANES))
            beside = jnp.where(iota((32, LANES), 0) == 31, past, field[pl.ds(at + 1, 32), :])
            above = pl.multiple_of(jnp.maximum(at - 32, 0), 32)
            for c, value in enumerate((here, beside)):
                for h, part in enumerate(split(value, 2)):
                    state16[pl.ds(h * cells + at, 32), c * LANES:(c + 1) * LANES] = part
                    state16[pl.ds(h * cells + above, 32), (2 + c) * LANES:(3 + c) * LANES] = part
            return 0

        lax.fori_loop(0, 16, corners, 0)
        acc[...] = jnp.zeros_like(acc)

        def one(i, _):
            values = dot(pick[...], state16[:, pl.ds(pl.multiple_of(i * 2 * LANES, LANES), 2 * LANES)])
            acc[...] += values[:, :LANES] * expanded_0[2 * i] + values[:, LANES:] * expanded_0[2 * i + 1]
            return 0

        lax.fori_loop(0, 2, one, 0)
        q = jnp.broadcast_to(jnp.sum(acc[...], axis=1, keepdims=True), acc.shape)
        q_b[n] = q

    def sums_start(n, sums):
        for i in range(4):
            sums_send[n, i:i + 1, :] = sums[i] if i < len(sums) else jnp.zeros((1, LANES), F32)
        for i in sorted(range(1, tiles), key=lambda i: -min(i, tiles - i)):
            pltpu.make_async_remote_copy(
                src_ref=sums_send.at[n], dst_ref=sums_tile.at[n, i], send_sem=t_sem.at[n, 0], recv_sem=t_sem.at[n, 1],
                device_id=(reg, lax.rem(til + i, tiles)), device_id_type=MESH).start()
        late.append(lambda: wait_all(sums_tile.at[n, pl.ds(1, tiles - 1)], t_sem.at[n, 0]))
        sums_tile[n, 0] = sums_send[n]

    def sums_middle(n):
        wait_all(sums_tile.at[n, pl.ds(1, tiles - 1)], t_sem.at[n, 1])
        sums_mid[n] = jnp.sum(sums_tile[n], axis=0)
        for i in sorted(range(1, regions), key=lambda i: -min(i, regions - i)):
            pltpu.make_async_remote_copy(
                src_ref=sums_mid.at[n], dst_ref=sums_region.at[n, i], send_sem=r_sem.at[n, 0], recv_sem=r_sem.at[n, 1],
                device_id=(lax.rem(reg + i, regions), til), device_id_type=MESH).start()
        late.append(lambda: wait_all(sums_region.at[n, pl.ds(1, regions - 1)], r_sem.at[n, 0]))
        sums_region[n, 0] = sums_mid[n]

    def sums_finish(n):
        wait_all(sums_region.at[n, pl.ds(1, regions - 1)], r_sem.at[n, 1])
        return jnp.sum(jnp.sum(sums_region[n], axis=0), axis=1, keepdims=True)

    def product(a, b):
        return jnp.sum(a * b, axis=0, keepdims=True)

    lane1 = iota((1, LANES), 1)

    def energy(a, b):
        return jnp.where(lane1 == 0, product(var_b[...] * q_b[a], q_b[b]), 0.0)

    arrive = halo_start(3)

    coef_arrive()
    for e in range(3):
        for side in range(2):
            to_cells(lambda r: coef_in[side, r, 8 * e:8 * e + 8, :], rows_in.at[e, side], 8)
        frame_halo(e, coef.at[e])

    def make_faces(k, _):
        base = pl.multiple_of(k * WIDE, 8)
        wet = coef[0, pl.ds(base, WIDE), :]
        coef[1, pl.ds(base, WIDE), :] = coef[1, pl.ds(base, WIDE), :] * wet * coef[0, pl.ds(base + WIDE, WIDE), :]
        coef[2, pl.ds(base, WIDE), :] = coef[2, pl.ds(base, WIDE), :] * wet * coef[0, pl.ds(base + 1, WIDE), :]
        return 0

    lax.fori_loop(0, TALL, make_faces, 0)

    def make_centre(k, _):
        base = pl.multiple_of(k * WIDE, 8)
        faces = coef[1, pl.ds(base, WIDE), :] + coef[1, pl.ds(base - WIDE, WIDE), :]
        faces = faces + coef[2, pl.ds(base, WIDE), :] + coef[2, pl.ds(base - 1, WIDE), :]
        coef[0, pl.ds(base, WIDE), :] = coef[0, pl.ds(base, WIDE), :] - faces
        return 0

    lax.fori_loop(1, TALL, make_centre, 0)

    build_frame(3, arrive, frame_a)
    diffuse(1, 4)
    inner(fields.at[0])
    diffuse(5, 8)
    inner(fields.at[1])

    norm = product(fields[0, :512, :], fields[0, :512, :])
    observe(fields.at[1], 0)
    z_b[...] = var_b[...] * q_b[0]
    adjoint(4)
    arrive = halo_start(4)
    sums_start(0, (norm, energy(0, 0)))
    to_natural(fields.at[0], natural.at[0])
    leaving = [pltpu.make_async_copy(natural.at[i], natural_out.at[i], out_sem.at[i]) for i in range(4)]
    leaving[0].start()
    build_frame(4, arrive, frame_a)
    diffuse(1, 4)
    sums_middle(0)
    inner(fields.at[2])
    diffuse(5, 8)
    inner(fields.at[4])
    observe(fields.at[4], 1)
    fields[2, :512, :] = fields[0, :512, :] + fields[2, :512, :]
    found = sums_finish(0)
    norm_0, energy_0 = found[0:1], found[1:2]
    alpha_0 = norm_0 / (norm_0 + energy_0)
    q_b[1] = q_b[0] - alpha_0 * (q_b[0] + q_b[1])
    fields[3, :512, :] = fields[0, :512, :] - alpha_0 * fields[2, :512, :]
    sums_start(1, (
        product(fields[3, :512, :], fields[3, :512, :]), product(fields[3, :512, :], fields[0, :512, :]), energy(1, 1), energy(1, 0)))
    z_b[...] = var_b[...] * q_b[1]
    adjoint(5)
    arrive = halo_start(5, 4)
    for i in (1, 2):
        to_natural(fields.at[i + 1], natural.at[i])
        leaving[i].start()
    build_frame(5, arrive, frame_a, 4, lambda: sums_middle(1))
    diffuse(5, 8)
    inner(fields.at[5])
    to_natural(fields.at[5], natural.at[3])
    leaving[3].start()
    drain()
    found = sums_finish(1)
    norm_1 = found[0:1]
    beta = norm_1 / norm_0
    curve = norm_1 + 2.0 * beta * found[1:2] + beta * beta * norm_0 + found[2:3] + 2.0 * beta * found[3:4] + beta * beta * energy_0
    alpha_1 = norm_1 / curve
    factor_out[...] = jnp.zeros_like(factor_out)
    for i, x in enumerate((alpha_0 + alpha_1 * beta, alpha_1, alpha_1 * beta)):
        factor_out[i:i + 1, :] = jnp.broadcast_to(x, (1, LANES))
    for c in leaving:
        c.wait()


def combine(natural, factor, control, residual):
    whole, second, mixed = factor[0:1, :], factor[1:2, :], factor[2:3, :]
    control[...] = whole * natural[0] + second * natural[2]
    residual[...] = natural[2] - second * (natural[2] + natural[3]) - mixed * natural[1]


def body(regions, tiles, kx, ky, mask, obs_owner, obs_row, obs_col, obs_weight, innovation, inverse_var):
    levels, rows_x, cols_y = kx.shape
    count = obs_row.shape[0]
    slots = tiles * CAP
    cells = rows_x * cols_y // GROUPS
    line, flat = (1, count), (levels * rows_x, cols_y)
    out = jax.ShapeDtypeStruct((32 * rows_x, cols_y), F32)
    dma = pltpu.SemaphoreType.DMA
    args = (
        kx.reshape(flat), ky.reshape(flat), mask.reshape(flat), obs_owner.reshape(line), obs_row.reshape(line),
        obs_col.reshape(line), innovation.reshape(line), inverse_var.reshape(line), obs_weight,
    )
    natural, factor = pl.pallas_call(
        functools.partial(kernel, regions, tiles),
        out_shape=(jax.ShapeDtypeStruct((4, 32 * rows_x, cols_y), F32), jax.ShapeDtypeStruct((8, LANES), F32)),
        in_specs=[pl.BlockSpec(memory_space=pl.ANY)] * 9,
        out_specs=[pl.BlockSpec(memory_space=pl.ANY), pl.BlockSpec(memory_space=pltpu.VMEM)],
        scratch_shapes=[
            *[pltpu.VMEM(x.shape, x.dtype) for x in args],
            pltpu.VMEM((EXCHANGES, cells, LANES), F32),
            pltpu.VMEM((EXCHANGES, 2, 32 * HALO, LANES), F32),
            pltpu.VMEM((EXCHANGES, 8, 8, LANES), F32),
            pltpu.VMEM((EXCHANGES, 8, 8, LANES), F32),
            pltpu.VMEM((EXCHANGES, 8, 8, LANES), F32),
            pltpu.VMEM((FRAME, LANES), F32),
            pltpu.VMEM((FRAME, LANES), F32),
            pltpu.VMEM((3, FRAME, LANES), F32),
            pltpu.VMEM((count, 3 * LANES), BF16),
            pltpu.VMEM((tiles, CAP, LANES), F32),
            pltpu.VMEM((tiles, CAP, LANES), F32),
            pltpu.VMEM((tiles, 1, LANES), F32),
            pltpu.VMEM((tiles, 1, LANES), F32),
            pltpu.VMEM((4, slots, LANES), F32),
            pltpu.VMEM((4, slots, LANES), F32),
            pltpu.VMEM((16, 24, LANES), F32),
            pltpu.VMEM((2, HALO, 24, LANES), F32),
            pltpu.VMEM((slots, 2 * cells), BF16),
            pltpu.VMEM((cells, 4 * slots), BF16),
            pltpu.VMEM((4 * slots, 2 * LANES), BF16),
            pltpu.VMEM((slots, LANES), F32),
            pltpu.VMEM((slots, LANES), F32),
            pltpu.VMEM((2, slots, LANES), F32),
            pltpu.VMEM((slots, LANES), F32),
            pltpu.VMEM((4, slots, LANES), F32),
            pltpu.VMEM((2 * cells, 4 * LANES), BF16),
            pltpu.VMEM((6, cells + 8, LANES), F32),
            pltpu.VMEM((4, cells, LANES), F32),
            pltpu.VMEM((2, 4, LANES), F32),
            pltpu.VMEM((2, regions, 4, LANES), F32),
            pltpu.VMEM((2, 4, LANES), F32),
            pltpu.VMEM((2, tiles, 4, LANES), F32),
            dma((9,)), dma((4,)), dma((EXCHANGES,)), dma((EXCHANGES,)), dma((1,)), dma((tiles // 4,)), dma((2,)), dma((2, 2)), dma((2, 2)),
        ],
        compiler_params=pltpu.CompilerParams(collective_id=0, has_side_effects=True, vmem_limit_bytes=60 * 1024 * 1024),
    )(*args)
    control, residual = pl.pallas_call(
        combine,
        out_shape=(out, out),
        in_specs=[pl.BlockSpec(memory_space=pltpu.VMEM)] * 2,
        out_specs=[pl.BlockSpec(memory_space=pltpu.VMEM)] * 2,
        compiler_params=pltpu.CompilerParams(vmem_limit_bytes=60 * 1024 * 1024),
    )(natural, factor)
    shape = (32 // levels, levels, rows_x, cols_y)
    return control.reshape(shape), residual.reshape(shape)


def solution(mesh):
    return jax.shard_map(
        functools.partial(body, mesh.shape["region"], mesh.shape["tile"]),
        mesh=mesh,
        in_specs=(
            P(None, "region", "tile"),
            P(None, "region", "tile"),
            P(None, "region", "tile"),
            P(("region", "tile"), None),
            P(("region", "tile")),
            P(("region", "tile")),
            P(("region", "tile"), None),
            P(("region", "tile")),
            P(("region", "tile")),
        ),
        out_specs=(P(None, None, "region", "tile"), P(None, None, "region", "tile")),
        check_vma=False,
    )
```

```python
import functools

import jax
import jax.numpy as jnp
from jax import lax
from jax.experimental import pallas as pl
from jax.experimental.pallas import tpu as pltpu
from jax.sharding import PartitionSpec as P

MESH = pl.DeviceIdType.MESH
F32 = jnp.float32
BF16 = jnp.bfloat16
CAP = 32
LANES = 128
GROUPS = 4
HALO = 8
WIDE = HALO + 32 + HALO
TALL = HALO + 16 + HALO
ROWS_AT_ONCE = 3
FRAME = (TALL + 3) * WIDE
EXCHANGES = 6


def iota(shape, dim):
    return lax.broadcasted_iota(jnp.int32, shape, dim)


def split(x, parts):
    out = []
    for i in range(parts):
        part = x.astype(BF16)
        out.append(part)
        if i + 1 < parts:
            x = x - part.astype(F32)
    return out


def dot(a, b):
    return jnp.dot(a, b, preferred_element_type=F32)


def dot_nt(a, b):
    return lax.dot_general(a, b, (((1,), (1,)), ((), ())), preferred_element_type=F32)


def swap_blocks(four):
    lane = iota(four[0].shape, 1)
    low = lane < 64
    even = (lane // 32) % 2 == 0
    a, b, c, d = four
    a, c = jnp.where(low, a, pltpu.roll(c, 64, 1)), jnp.where(low, pltpu.roll(a, 64, 1), c)
    b, d = jnp.where(low, b, pltpu.roll(d, 64, 1)), jnp.where(low, pltpu.roll(b, 64, 1), d)
    a, b = jnp.where(even, a, pltpu.roll(b, 32, 1)), jnp.where(even, pltpu.roll(a, 96, 1), b)
    c, d = jnp.where(even, c, pltpu.roll(d, 32, 1)), jnp.where(even, pltpu.roll(c, 96, 1), d)
    return a, b, c, d


def kernel(
    regions, tiles, kx_any, ky_any, mask_any, owner_any, row_any, col_any, innov_any, var_any, weight_any,
    natural_out, factor_out,
    kx_ref, ky_ref, mask_ref, owner_ref, row_ref, col_ref, innov_ref, var_ref, weight_ref,
    dense, rows_in, left_in, right_in, packed, frame_a, frame_b, coef, wsplit, wsend, wrecv, expanded, expanded_0, coef_rows, coef_in,
    pick, pick_t, terms, var_b, z_b, q_b, acc, group_b, state16, fields, natural, sums_send, sums_region, sums_mid, sums_tile,
    in_sem, out_sem, halo_send, halo_recv, w_send_sem, w_recv_sem, r_sem, t_sem,
):
    reg, til = lax.axis_index("region"), lax.axis_index("tile")
    up, down = lax.rem(reg + regions - 1, regions), lax.rem(reg + 1, regions)
    left, right = lax.rem(til + tiles - 1, tiles), lax.rem(til + 1, tiles)
    count = owner_ref.shape[1]
    slots = tiles * CAP
    planes = tiles // 4
    late = []

    def wait_all(ref, sem):
        pltpu.make_async_copy(ref, ref, sem).wait()

    barrier = pltpu.get_barrier_semaphore()
    for i in sorted(range(1, tiles), key=lambda i: -min(i, tiles - i)):
        pl.semaphore_signal(barrier, inc=1, device_id=(reg, lax.rem(til + i, tiles)), device_id_type=MESH)
    for i in range(1, regions):
        pl.semaphore_signal(barrier, inc=1, device_id=(lax.rem(reg + i, regions), til), device_id_type=MESH)
    for a in (up, down):
        for b in (left, right):
            pl.semaphore_signal(barrier, inc=1, device_id=(a, b), device_id_type=MESH)

    pairs = (
        (owner_any, owner_ref), (row_any, row_ref), (col_any, col_ref), (innov_any, innov_ref), (var_any, var_ref),
        (weight_any, weight_ref), (mask_any, mask_ref), (kx_any, kx_ref), (ky_any, ky_ref),
    )
    loads = [pltpu.make_async_copy(a, b, in_sem.at[i]) for i, (a, b) in enumerate(pairs)]
    for c in loads:
        c.start()
    for c in loads[:5]:
        c.wait()
    lane8 = iota((8, LANES), 1)

    def halo_copies(e, deep, fields):
        def copy(src, dst, device):
            return pltpu.make_async_remote_copy(
                src_ref=src, dst_ref=dst, send_sem=halo_send.at[e], recv_sem=halo_recv.at[e],
                device_id=device, device_id_type=MESH)
        size, packs, at = deep * 32, deep // 4, pl.ds(e, fields)
        return [
            copy(packed.at[at, pl.ds(0, packs)], left_in.at[at, pl.ds(6, packs)], (up, right)),
            copy(packed.at[at, pl.ds(4 - packs, packs)], left_in.at[at, pl.ds(2 - packs, packs)], (down, right)),
            copy(packed.at[at, pl.ds(4, packs)], right_in.at[at, pl.ds(6, packs)], (up, left)),
            copy(packed.at[at, pl.ds(8 - packs, packs)], right_in.at[at, pl.ds(2 - packs, packs)], (down, left)),
            copy(packed.at[at, pl.ds(0, 4)], left_in.at[at, pl.ds(2, 4)], (reg, right)),
            copy(packed.at[at, pl.ds(4, 4)], right_in.at[at, pl.ds(2, 4)], (reg, left)),
            copy(coef_rows.at[pl.ds(0, 8)], coef_in.at[1], (up, til)) if e == 0 else
            copy(dense.at[e, pl.ds(0, size)], rows_in.at[e, 1, pl.ds(0, size)], (up, til)),
            copy(coef_rows.at[pl.ds(8, 8)], coef_in.at[0], (down, til)) if e == 0 else
            copy(dense.at[e, pl.ds(512 - size, size)], rows_in.at[e, 0, pl.ds(256 - size, size)], (down, til)),
        ]

    def halo_pack(e):
        for j in range(4):
            first = swap_blocks([dense[e, (4 * j + b) * 32:(4 * j + b) * 32 + 8, :] for b in range(4)])
            last = swap_blocks([dense[e, (4 * j + b) * 32 + 24:(4 * j + b) * 32 + 32, :] for b in range(4)])
            packed[e, j] = last[3]
            packed[e, 4 + j] = first[0]

    def halo_start(e, deep=8, fields=1):
        copies = halo_copies(e, deep, fields)
        for c in copies[6:]:
            c.start()
        if e == 0:
            for i in range(3):
                to_cells(lambda r: coef_rows[r, 8 * i:8 * i + 8, :], dense.at[i], 16)
        for i in range(fields):
            halo_pack(e + i)
        for c in copies[:6]:
            c.start()
        amount = frame_b.at[pl.ds(0, 768 if e == 0 else 72 * deep + 64)]
        late.append(lambda: wait_all(amount, halo_send.at[e]))
        return lambda: wait_all(amount, halo_recv.at[e])

    def frame_own(e, out):
        def four_rows(j, _):
            for b in range(4):
                row = 4 * j + b
                base = pl.multiple_of((row + 8) * WIDE, 8)
                own = dense[e, pl.ds(pl.multiple_of(row * 32, 32), 32), :]
                out[pl.ds(base + 16, 32), :] = own
                out[pl.ds(base + 8, 8), :] = pltpu.roll(own[24:], 32, 1)
                out[pl.ds(base + WIDE, 8), :] = pltpu.roll(own[:8], 96, 1)
            return 0
        lax.fori_loop(0, 4, four_rows, 0)

    def frame_halo(e, out, deep=8):
        if e == 0:
            inside_up = jnp.where(reg > 0, 1.0, 0.0)
            inside_down = jnp.where(reg < regions - 1, 1.0, 0.0)
            rows_in[0, 0] = rows_in[0, 0] * inside_up
            rows_in[0, 1] = rows_in[0, 1] * inside_down
            for side, inside in ((left_in, jnp.where(til > 0, 1.0, 0.0)), (right_in, jnp.where(til < tiles - 1, 1.0, 0.0))):
                for j in range(8):
                    side[0, j] = side[0, j] * (inside * inside_up if j < 2 else inside if j < 6 else inside * inside_down)

        def beside(j, b):
            return pltpu.roll(left_in[e, j], -b * 32 % LANES, 1), pltpu.roll(right_in[e, j], (3 - b) * 32, 1)

        def own_rows(j, _):
            for b in range(4):
                base = pl.multiple_of((4 * j + b) * WIDE, 8)
                start, end = beside(j, b)
                out[pl.ds(base + 8, 8), :] = jnp.where(lane8 < 32, start, out[pl.ds(base + 8, 8), :])
                out[pl.ds(base + WIDE, 8), :] = jnp.where(lane8 >= 96, end, out[pl.ds(base + WIDE, 8), :])
            return 0

        lax.fori_loop(2, 6, own_rows, 0)
        for side in range(2):
            def outer_rows(j, _):
                for b in range(4):
                    row = 4 * j + b
                    base = pl.multiple_of((row + 24 * side) * WIDE, 8)
                    came = rows_in[e, side, pl.ds(pl.multiple_of(row * 32, 32), 32), :]
                    start, end = beside(j + 6 * side, b)
                    out[pl.ds(base + 16, 32), :] = came
                    out[pl.ds(base + 8, 8), :] = jnp.where(lane8 < 32, start, pltpu.roll(came[24:], 32, 1))
                    out[pl.ds(base + WIDE, 8), :] = jnp.where(lane8 >= 96, end, pltpu.roll(came[:8], 96, 1))
                return 0
            lax.fori_loop(0 if side else 2 - deep // 4, deep // 4 if side else 2, outer_rows, 0)

    def build_frame(e, arrive, out, deep=8, meanwhile=lambda: None):
        frame_own(e, out)
        drain()
        meanwhile()
        arrive()
        frame_halo(e, out, deep)

    def to_cells(line, out, rows):
        def four_rows(j, _):
            lines = [line(4 * j + b) for b in range(4)]
            many = jnp.concatenate([x for x in lines for _ in range(4)], axis=0).T
            for b, x in enumerate(swap_blocks([many[32 * g:32 * g + 32] for g in range(4)])):
                out[pl.ds(pl.multiple_of((4 * j + b) * 32, 32), 32), :] = x
            return 0
        lax.fori_loop(0, rows // 4, four_rows, 0)

    def to_natural(field, out):
        def four_rows(j, _):
            lines = [field[pl.ds(pl.multiple_of((4 * j + b) * 32, 32), 32), :] for b in range(4)]
            many = jnp.concatenate(swap_blocks(lines), axis=0).T
            for b in range(4):
                out[pl.ds(4 * j + b, 32, stride=16), :] = many[32 * b:32 * b + 32]
            return 0
        lax.fori_loop(0, 4, four_rows, 0)

    owner = owner_ref[...]
    marks = jnp.where(iota((tiles, count), 0) == owner, 1.0, 0.0)
    upper = jnp.where(iota((count, count), 0) < iota((count, count), 1), 1.0, 0.0).astype(BF16)
    before = dot(marks.astype(BF16), upper)
    slot = owner * CAP + jnp.sum(before * marks, axis=0, keepdims=True).astype(jnp.int32)
    meta_rows = [row_ref[...].astype(F32), col_ref[...].astype(F32)]
    meta_rows += [p.astype(F32) for p in split(innov_ref[...], 3) + split(var_ref[...], 3)]
    meta = jnp.zeros((8, count), F32)
    for i, line in enumerate(meta_rows):
        meta = jnp.where(iota((8, count), 0) == i, line, meta)
    meta = meta.astype(BF16)

    def choose(b, _):
        chosen = jnp.where(iota((LANES, count), 0) + b * LANES == slot, 1.0, 0.0).astype(BF16)
        pick[pl.ds(pl.multiple_of(b * LANES, LANES), LANES), :count] = chosen
        return 0

    lax.fori_loop(0, planes, choose, 0)
    facts = dot_nt(meta, pick[:, :count])
    place = facts[0:1] * LANES + facts[1:2]
    innov = facts[2:3] + facts[3:4] + facts[4:5]
    var = facts[5:6] + facts[6:7] + facts[7:8]
    for b in range(planes):
        at = slice(b * LANES, (b + 1) * LANES)
        three = [jnp.broadcast_to(x[:, at], (8, LANES)) for x in (place, innov, var)]
        for k in range(4):
            turned = [pltpu.roll(x, (i - k) * 32 % LANES, 1) for i, x in enumerate(three)]
            line = jnp.where(lane8 < 32, turned[0], jnp.where(lane8 < 64, turned[1], jnp.where(lane8 < 96, turned[2], 0.0)))
            wsend[4 * b + k, CAP:CAP + 1, :] = line[0:1]
    loads[5].wait()
    for i, part in enumerate(split(weight_ref[...], 3)):
        wsplit[:, i * LANES:(i + 1) * LANES] = part
    block = dot(pick[:, :count], wsplit[...])
    wsend[:, :CAP, :] = (block[:, :LANES] + block[:, LANES:2 * LANES] + block[:, 2 * LANES:]).reshape(tiles, CAP, LANES)

    turns = sorted(range(planes), key=lambda i: (min(i, planes - i), i))
    plane, place_in = til // 4, lax.rem(til, 4)

    def sends(src, dst, send_sem, recv_sem, together):
        out = []
        for j, turn in enumerate(turns):
            for k in range(4):
                if j or k:
                    to = lax.rem(plane + turn, planes) * 4 + lax.rem(place_in + k, 4)
                    n = 4 * j + k
                    out.append(pltpu.make_async_remote_copy(
                        src_ref=src.at[to], dst_ref=dst.at[n], send_sem=send_sem, recv_sem=recv_sem.at[n // together],
                        device_id=(reg, to), device_id_type=MESH))
        return out

    def both_ways(copies):
        order = list(range(3))
        for j in range(1, planes, 2):
            order += [4 * i + k - 1 for k in range(4) for i in (j, j + 1) if i < planes]
        return [copies[i] for i in order]

    w_copies = sends(wsend, wrecv, w_send_sem.at[0], w_recv_sem, 4)
    late.append(lambda: wait_all(wsend.at[pl.ds(1, tiles - 1)], w_send_sem.at[0]))
    def drain():
        for wait in late:
            wait()
        late.clear()

    pl.semaphore_wait(barrier, (tiles - 1) + (regions - 1) + 4)
    for c in both_ways(w_copies):
        c.start()
    wrecv[0] = wsend[til]

    for c in loads[6:]:
        c.wait()

    def stage(r, _):
        for e, source in enumerate((mask_ref, kx_ref, ky_ref)):
            coef_rows[r, 8 * e:8 * e + 8, :] = source[pl.ds(r, 8, stride=16), :].astype(F32)
        return 0

    lax.fori_loop(0, 16, stage, 0)
    coef_arrive = halo_start(0, 8, 3)

    def diffuse(first, last):
        for s in range(first, last + 1):
            src, dst = (frame_a, frame_b) if (s - first) % 2 == 0 else (frame_b, frame_a)

            def lines(i, carry):
                before, here, west = carry
                base = pl.multiple_of((s + ROWS_AT_ONCE * i) * WIDE, 8)
                for u in range(ROWS_AT_ONCE):
                    at = base + u * WIDE
                    after = src[pl.ds(at + WIDE, WIDE), :]
                    east = coef[1, pl.ds(at, WIDE), :]
                    out = (coef[0, pl.ds(at, WIDE), :] * here + east * after) + west * before
                    dst[pl.ds(at, WIDE), :] = out + (
                        coef[2, pl.ds(at, WIDE), :] * src[pl.ds(at + 1, WIDE), :]
                        + coef[2, pl.ds(at - 1, WIDE), :] * src[pl.ds(at - 1, WIDE), :])
                    before, here, west = here, after, east
                return before, here, west

            at = (s - 1) * WIDE
            rows = 16 if s == HALO else TALL + 1 - 2 * s
            lax.fori_loop(
                0, -(-rows // ROWS_AT_ONCE), lines, (src[at:at + WIDE, :], src[at + WIDE:at + 2 * WIDE, :], coef[1, at:at + WIDE, :]))

    def inner(out):
        for j in range(16):
            out[j * 32:(j + 1) * 32, :] = frame_a[(8 + j) * WIDE + 16:(9 + j) * WIDE, :]

    lane = iota((LANES, LANES), 1)
    seat = iota((LANES, LANES), 0) % CAP
    ones = jnp.ones((3 * LANES, LANES), BF16)
    cells = pick_t.shape[0]

    def corner_of(place, c):
        row = (place >> 7) + c // 2
        col = (place & 127) + c % 2
        return row * 32 + (col & 31), col >> 5

    def read_facts(j):
        at = pl.ds(pl.multiple_of(j * LANES, LANES), LANES)
        facts = jnp.broadcast_to(wrecv[pl.ds(4 * j, 4), CAP:CAP + 1, :], (4, CAP, LANES)).reshape(LANES, LANES)

        def spread_lanes(kind):
            return jnp.concatenate(split(jnp.where(lane == seat + 32 * kind, facts, 0.0), 3), axis=1)

        place3 = spread_lanes(0)
        place_col = dot(place3, ones).astype(jnp.int32)
        place_row = dot_nt(jnp.ones((8, 3 * LANES), BF16), place3).astype(jnp.int32)[0:1]
        var = dot(spread_lanes(2), ones)
        var_b[at, :] = var
        z_b[at, :] = var * dot(spread_lanes(1), ones)
        for c in range(4):
            cell, group = corner_of(place_col, c)
            group_b[c, at, :] = jnp.where(group == lane // 32, 1.0, 0.0)
            if c == 0:
                for t in range(cells // LANES):
                    hit = jnp.where(cell == lane + t * LANES, 1.0, 0.0).astype(BF16)
                    pick[at, t * LANES:(t + 1) * LANES] = hit
                    pick[at, cells + t * LANES:cells + (t + 1) * LANES] = hit
            cell, _ = corner_of(place_row, c)
            there = pl.ds(pl.multiple_of((4 * j + c) * LANES, LANES), LANES)
            pick_t[:, there] = jnp.where(iota((cells, LANES), 0) == cell, 1.0, 0.0).astype(BF16)

    def put_terms(j, c):
        at = pl.ds(pl.multiple_of(j * LANES, LANES), LANES)
        there = pl.ds(pl.multiple_of((4 * j + c) * LANES, LANES), LANES)
        hi, lo = split(z_b[at, :] * expanded[c, at, :], 2)
        terms[there, :LANES] = hi
        terms[there, LANES:] = lo

    for e in range(3):
        frame_own(e, coef.at[e])

    copy_lanes = jnp.where(
        iota((3 * LANES, 4 * LANES), 0) % LANES == iota((3 * LANES, 4 * LANES), 1) // LANES * 32 + iota((3 * LANES, 4 * LANES), 1) % 32,
        1.0, 0.0).astype(BF16)
    def take_plane(j, first):
        wait_all(wrecv.at[pl.ds(4 * j + first, 4 - first)], w_recv_sem.at[j])
        read_facts(j)
        wide = dot(jnp.concatenate(split(wrecv[pl.ds(4 * j, 4), :CAP, :].reshape(LANES, LANES), 3), axis=1), copy_lanes)
        at = pl.ds(pl.multiple_of(j * LANES, LANES), LANES)
        for c in range(4):
            expanded[c, at, :] = wide[:, c * LANES:(c + 1) * LANES] * group_b[c, at, :]
            expanded_0[c, at, :] = wide[:, c * LANES:(c + 1) * LANES] * group_b[0, at, :]
            put_terms(j, c)
        there = pl.ds(pl.multiple_of(4 * j * LANES, LANES), 4 * LANES)
        part = dot(pick_t[:, there], terms[there, :])
        return part[:, :LANES] + part[:, LANES:]

    state16[...] = jnp.zeros_like(state16)
    dense[3] = take_plane(0, 1)

    def later_plane(j, _):
        dense[3] = dense[3] + take_plane(j, 0)
        return 0

    lax.fori_loop(1, planes, later_plane, 0)

    def adjoint(e):
        def one(j, _):
            for c in range(4):
                put_terms(j, c)
            return 0
        lax.fori_loop(0, planes, one, 0)
        total = dot(pick_t[...], terms[...])
        dense[e] = total[:, :LANES] + total[:, LANES:]

    def observe(field, n):
        def corners(r, _):
            at = pl.multiple_of(r * 32, 32)
            here = field[pl.ds(at, 32), :]
            past = jnp.broadcast_to(pltpu.roll(here[:8], 96, 1)[0:1], (32, LANES))
            beside = jnp.where(iota((32, LANES), 0) == 31, past, field[pl.ds(at + 1, 32), :])
            above = pl.multiple_of(jnp.maximum(at - 32, 0), 32)
            for c, value in enumerate((here, beside)):
                for h, part in enumerate(split(value, 2)):
                    state16[pl.ds(h * cells + at, 32), c * LANES:(c + 1) * LANES] = part
                    state16[pl.ds(h * cells + above, 32), (2 + c) * LANES:(3 + c) * LANES] = part
            return 0

        lax.fori_loop(0, 16, corners, 0)
        acc[...] = jnp.zeros_like(acc)

        def one(i, _):
            values = dot(pick[...], state16[:, pl.ds(pl.multiple_of(i * 2 * LANES, LANES), 2 * LANES)])
            acc[...] += values[:, :LANES] * expanded_0[2 * i] + values[:, LANES:] * expanded_0[2 * i + 1]
            return 0

        lax.fori_loop(0, 2, one, 0)
        q = jnp.broadcast_to(jnp.sum(acc[...], axis=1, keepdims=True), acc.shape)
        q_b[n] = q

    def sums_start(n, sums):
        for i in range(4):
            sums_send[n, i:i + 1, :] = sums[i] if i < len(sums) else jnp.zeros((1, LANES), F32)
        for i in sorted(range(1, tiles), key=lambda i: -min(i, tiles - i)):
            pltpu.make_async_remote_copy(
                src_ref=sums_send.at[n], dst_ref=sums_tile.at[n, i], send_sem=t_sem.at[n, 0], recv_sem=t_sem.at[n, 1],
                device_id=(reg, lax.rem(til + i, tiles)), device_id_type=MESH).start()
        late.append(lambda: wait_all(sums_tile.at[n, pl.ds(1, tiles - 1)], t_sem.at[n, 0]))
        sums_tile[n, 0] = sums_send[n]

    def sums_middle(n):
        wait_all(sums_tile.at[n, pl.ds(1, tiles - 1)], t_sem.at[n, 1])
        sums_mid[n] = jnp.sum(sums_tile[n], axis=0)
        for i in sorted(range(1, regions), key=lambda i: -min(i, regions - i)):
            pltpu.make_async_remote_copy(
                src_ref=sums_mid.at[n], dst_ref=sums_region.at[n, i], send_sem=r_sem.at[n, 0], recv_sem=r_sem.at[n, 1],
                device_id=(lax.rem(reg + i, regions), til), device_id_type=MESH).start()
        late.append(lambda: wait_all(sums_region.at[n, pl.ds(1, regions - 1)], r_sem.at[n, 0]))
        sums_region[n, 0] = sums_mid[n]

    def sums_finish(n):
        wait_all(sums_region.at[n, pl.ds(1, regions - 1)], r_sem.at[n, 1])
        return jnp.sum(jnp.sum(sums_region[n], axis=0), axis=1, keepdims=True)

    def product(a, b):
        return jnp.sum(a * b, axis=0, keepdims=True)

    lane1 = iota((1, LANES), 1)

    def energy(a, b):
        return jnp.where(lane1 == 0, product(var_b[...] * q_b[a], q_b[b]), 0.0)

    arrive = halo_start(3)

    coef_arrive()
    for e in range(3):
        for side in range(2):
            to_cells(lambda r: coef_in[side, r, 8 * e:8 * e + 8, :], rows_in.at[e, side], 8)
        frame_halo(e, coef.at[e])

    def make_faces(k, _):
        base = pl.multiple_of(k * WIDE, 8)
        wet = coef[0, pl.ds(base, WIDE), :]
        coef[1, pl.ds(base, WIDE), :] = coef[1, pl.ds(base, WIDE), :] * wet * coef[0, pl.ds(base + WIDE, WIDE), :]
        coef[2, pl.ds(base, WIDE), :] = coef[2, pl.ds(base, WIDE), :] * wet * coef[0, pl.ds(base + 1, WIDE), :]
        return 0

    lax.fori_loop(0, TALL, make_faces, 0)

    def make_centre(k, _):
        base = pl.multiple_of(k * WIDE, 8)
        faces = coef[1, pl.ds(base, WIDE), :] + coef[1, pl.ds(base - WIDE, WIDE), :]
        faces = faces + coef[2, pl.ds(base, WIDE), :] + coef[2, pl.ds(base - 1, WIDE), :]
        coef[0, pl.ds(base, WIDE), :] = coef[0, pl.ds(base, WIDE), :] - faces
        return 0

    lax.fori_loop(1, TALL, make_centre, 0)

    build_frame(3, arrive, frame_a)
    diffuse(1, 4)
    inner(fields.at[0])
    diffuse(5, 8)
    inner(fields.at[1])

    norm = product(fields[0, :512, :], fields[0, :512, :])
    observe(fields.at[1], 0)
    z_b[...] = var_b[...] * q_b[0]
    adjoint(4)
    arrive = halo_start(4)
    sums_start(0, (norm, energy(0, 0)))
    to_natural(fields.at[0], natural.at[0])
    leaving = [pltpu.make_async_copy(natural.at[i], natural_out.at[i], out_sem.at[i]) for i in range(4)]
    leaving[0].start()
    build_frame(4, arrive, frame_a)
    diffuse(1, 4)
    sums_middle(0)
    inner(fields.at[2])
    diffuse(5, 8)
    inner(fields.at[4])
    observe(fields.at[4], 1)
    fields[2, :512, :] = fields[0, :512, :] + fields[2, :512, :]
    found = sums_finish(0)
    norm_0, energy_0 = found[0:1], found[1:2]
    alpha_0 = norm_0 / (norm_0 + energy_0)
    q_b[1] = q_b[0] - alpha_0 * (q_b[0] + q_b[1])
    fields[3, :512, :] = fields[0, :512, :] - alpha_0 * fields[2, :512, :]
    sums_start(1, (
        product(fields[3, :512, :], fields[3, :512, :]), product(fields[3, :512, :], fields[0, :512, :]), energy(1, 1), energy(1, 0)))
    z_b[...] = var_b[...] * q_b[1]
    adjoint(5)
    arrive = halo_start(5, 4)
    for i in (1, 2):
        to_natural(fields.at[i + 1], natural.at[i])
        leaving[i].start()
    build_frame(5, arrive, frame_a, 4, lambda: sums_middle(1))
    diffuse(5, 8)
    inner(fields.at[5])
    to_natural(fields.at[5], natural.at[3])
    leaving[3].start()
    drain()
    found = sums_finish(1)
    norm_1 = found[0:1]
    beta = norm_1 / norm_0
    curve = norm_1 + 2.0 * beta * found[1:2] + beta * beta * norm_0 + found[2:3] + 2.0 * beta * found[3:4] + beta * beta * energy_0
    alpha_1 = norm_1 / curve
    factor_out[...] = jnp.zeros_like(factor_out)
    for i, x in enumerate((alpha_0 + alpha_1 * beta, alpha_1, alpha_1 * beta)):
        factor_out[i:i + 1, :] = jnp.broadcast_to(x, (1, LANES))
    for c in leaving:
        c.wait()


def combine(natural, factor, control, residual):
    whole, second, mixed = factor[0:1, :], factor[1:2, :], factor[2:3, :]
    control[...] = whole * natural[0] + second * natural[2]
    residual[...] = natural[2] - second * (natural[2] + natural[3]) - mixed * natural[1]


def body(regions, tiles, kx, ky, mask, obs_owner, obs_row, obs_col, obs_weight, innovation, inverse_var):
    levels, rows_x, cols_y = kx.shape
    count = obs_row.shape[0]
    slots = tiles * CAP
    cells = rows_x * cols_y // GROUPS
    line, flat = (1, count), (levels * rows_x, cols_y)
    out = jax.ShapeDtypeStruct((32 * rows_x, cols_y), F32)
    dma = pltpu.SemaphoreType.DMA
    args = (
        kx.reshape(flat), ky.reshape(flat), mask.reshape(flat), obs_owner.reshape(line), obs_row.reshape(line),
        obs_col.reshape(line), innovation.reshape(line), inverse_var.reshape(line), obs_weight,
    )
    natural, factor = pl.pallas_call(
        functools.partial(kernel, regions, tiles),
        out_shape=(jax.ShapeDtypeStruct((4, 32 * rows_x, cols_y), F32), jax.ShapeDtypeStruct((8, LANES), F32)),
        in_specs=[pl.BlockSpec(memory_space=pl.ANY)] * 9,
        out_specs=[pl.BlockSpec(memory_space=pl.ANY), pl.BlockSpec(memory_space=pltpu.VMEM)],
        scratch_shapes=[
            *[pltpu.VMEM(x.shape, x.dtype) for x in args],
            pltpu.VMEM((EXCHANGES, cells, LANES), F32),
            pltpu.VMEM((EXCHANGES, 2, 32 * HALO, LANES), F32),
            pltpu.VMEM((EXCHANGES, 8, 8, LANES), F32),
            pltpu.VMEM((EXCHANGES, 8, 8, LANES), F32),
            pltpu.VMEM((EXCHANGES, 8, 8, LANES), F32),
            pltpu.VMEM((FRAME, LANES), F32),
            pltpu.VMEM((FRAME, LANES), F32),
            pltpu.VMEM((3, FRAME, LANES), F32),
            pltpu.VMEM((count, 3 * LANES), BF16),
            pltpu.VMEM((tiles, CAP + 1, LANES), F32),
            pltpu.VMEM((tiles, CAP + 1, LANES), F32),
            pltpu.VMEM((4, slots, LANES), F32),
            pltpu.VMEM((4, slots, LANES), F32),
            pltpu.VMEM((16, 24, LANES), F32),
            pltpu.VMEM((2, HALO, 24, LANES), F32),
            pltpu.VMEM((slots, 2 * cells), BF16),
            pltpu.VMEM((cells, 4 * slots), BF16),
            pltpu.VMEM((4 * slots, 2 * LANES), BF16),
            pltpu.VMEM((slots, LANES), F32),
            pltpu.VMEM((slots, LANES), F32),
            pltpu.VMEM((2, slots, LANES), F32),
            pltpu.VMEM((slots, LANES), F32),
            pltpu.VMEM((4, slots, LANES), F32),
            pltpu.VMEM((2 * cells, 4 * LANES), BF16),
            pltpu.VMEM((6, cells + 8, LANES), F32),
            pltpu.VMEM((4, cells, LANES), F32),
            pltpu.VMEM((2, 4, LANES), F32),
            pltpu.VMEM((2, regions, 4, LANES), F32),
            pltpu.VMEM((2, 4, LANES), F32),
            pltpu.VMEM((2, tiles, 4, LANES), F32),
            dma((9,)), dma((4,)), dma((EXCHANGES,)), dma((EXCHANGES,)), dma((1,)), dma((tiles // 4,)), dma((2, 2)), dma((2, 2)),
        ],
        compiler_params=pltpu.CompilerParams(collective_id=0, has_side_effects=True, vmem_limit_bytes=60 * 1024 * 1024),
    )(*args)
    control, residual = pl.pallas_call(
        combine,
        out_shape=(out, out),
        in_specs=[pl.BlockSpec(memory_space=pltpu.VMEM)] * 2,
        out_specs=[pl.BlockSpec(memory_space=pltpu.VMEM)] * 2,
        compiler_params=pltpu.CompilerParams(vmem_limit_bytes=60 * 1024 * 1024),
    )(natural, factor)
    shape = (32 // levels, levels, rows_x, cols_y)
    return control.reshape(shape), residual.reshape(shape)


def solution(mesh):
    return jax.shard_map(
        functools.partial(body, mesh.shape["region"], mesh.shape["tile"]),
        mesh=mesh,
        in_specs=(
            P(None, "region", "tile"),
            P(None, "region", "tile"),
            P(None, "region", "tile"),
            P(("region", "tile"), None),
            P(("region", "tile")),
            P(("region", "tile")),
            P(("region", "tile"), None),
            P(("region", "tile")),
            P(("region", "tile")),
        ),
        out_specs=(P(None, None, "region", "tile"), P(None, None, "region", "tile")),
        check_vma=False,
    )
```

```python
import functools

import jax
import jax.numpy as jnp
from jax import lax
from jax.experimental import pallas as pl
from jax.experimental.pallas import tpu as pltpu
from jax.sharding import PartitionSpec as P

MESH = pl.DeviceIdType.MESH
F32 = jnp.float32
BF16 = jnp.bfloat16
CAP = 32
LANES = 128
GROUPS = 4
HALO = 8
WIDE = HALO + 32 + HALO
TALL = HALO + 16 + HALO
ROWS_AT_ONCE = 3
FRAME = (TALL + 3) * WIDE
EXCHANGES = 6


def iota(shape, dim):
    return lax.broadcasted_iota(jnp.int32, shape, dim)


def split(x, parts):
    out = []
    for i in range(parts):
        part = x.astype(BF16)
        out.append(part)
        if i + 1 < parts:
            x = x - part.astype(F32)
    return out


def dot(a, b):
    return jnp.dot(a, b, preferred_element_type=F32)


def dot_nt(a, b):
    return lax.dot_general(a, b, (((1,), (1,)), ((), ())), preferred_element_type=F32)


def swap_blocks(four):
    lane = iota(four[0].shape, 1)
    low = lane < 64
    even = (lane // 32) % 2 == 0
    a, b, c, d = four
    a, c = jnp.where(low, a, pltpu.roll(c, 64, 1)), jnp.where(low, pltpu.roll(a, 64, 1), c)
    b, d = jnp.where(low, b, pltpu.roll(d, 64, 1)), jnp.where(low, pltpu.roll(b, 64, 1), d)
    a, b = jnp.where(even, a, pltpu.roll(b, 32, 1)), jnp.where(even, pltpu.roll(a, 96, 1), b)
    c, d = jnp.where(even, c, pltpu.roll(d, 32, 1)), jnp.where(even, pltpu.roll(c, 96, 1), d)
    return a, b, c, d


def kernel(
    regions, tiles, kx_any, ky_any, mask_any, owner_any, row_any, col_any, innov_any, var_any, weight_any,
    natural_out, factor_out,
    kx_ref, ky_ref, mask_ref, owner_ref, row_ref, col_ref, innov_ref, var_ref, weight_ref,
    dense, rows_in, left_in, right_in, packed, frame_a, frame_b, coef, wsplit, wsend, wrecv, msend, mrecv, expanded, expanded_0, coef_rows, coef_in,
    pick, pick_t, terms, var_b, z_b, q_b, acc, group_b, state16, fields, natural, sums_send, sums_region, sums_mid, sums_tile,
    in_sem, out_sem, halo_send, halo_recv, w_send_sem, w_recv_sem, m_sem, r_sem, t_sem,
):
    reg, til = lax.axis_index("region"), lax.axis_index("tile")
    up, down = lax.rem(reg + regions - 1, regions), lax.rem(reg + 1, regions)
    left, right = lax.rem(til + tiles - 1, tiles), lax.rem(til + 1, tiles)
    count = owner_ref.shape[1]
    slots = tiles * CAP
    planes = tiles // 4
    late = []

    def wait_all(ref, sem):
        pltpu.make_async_copy(ref, ref, sem).wait()

    barrier = pltpu.get_barrier_semaphore()
    for i in sorted(range(1, tiles), key=lambda i: -min(i, tiles - i)):
        pl.semaphore_signal(barrier, inc=1, device_id=(reg, lax.rem(til + i, tiles)), device_id_type=MESH)
    for i in range(1, regions):
        pl.semaphore_signal(barrier, inc=1, device_id=(lax.rem(reg + i, regions), til), device_id_type=MESH)
    for a in (up, down):
        for b in (left, right):
            pl.semaphore_signal(barrier, inc=1, device_id=(a, b), device_id_type=MESH)

    pairs = (
        (owner_any, owner_ref), (row_any, row_ref), (col_any, col_ref), (innov_any, innov_ref), (var_any, var_ref),
        (weight_any, weight_ref), (mask_any, mask_ref), (kx_any, kx_ref), (ky_any, ky_ref),
    )
    loads = [pltpu.make_async_copy(a, b.at[pl.ds(0, a.shape[0])] if i > 5 else b, in_sem.at[i]) for i, (a, b) in enumerate(pairs)]
    for c in loads:
        c.start()
    for c in loads[:5]:
        c.wait()
    lane8 = iota((8, LANES), 1)

    def halo_copies(e, deep, fields):
        def copy(src, dst, device):
            return pltpu.make_async_remote_copy(
                src_ref=src, dst_ref=dst, send_sem=halo_send.at[e], recv_sem=halo_recv.at[e],
                device_id=device, device_id_type=MESH)
        size, packs, at = deep * 32, deep // 4, pl.ds(e, fields)
        return [
            copy(packed.at[at, pl.ds(0, packs)], left_in.at[at, pl.ds(6, packs)], (up, right)),
            copy(packed.at[at, pl.ds(4 - packs, packs)], left_in.at[at, pl.ds(2 - packs, packs)], (down, right)),
            copy(packed.at[at, pl.ds(4, packs)], right_in.at[at, pl.ds(6, packs)], (up, left)),
            copy(packed.at[at, pl.ds(8 - packs, packs)], right_in.at[at, pl.ds(2 - packs, packs)], (down, left)),
            copy(packed.at[at, pl.ds(0, 4)], left_in.at[at, pl.ds(2, 4)], (reg, right)),
            copy(packed.at[at, pl.ds(4, 4)], right_in.at[at, pl.ds(2, 4)], (reg, left)),
            copy(coef_rows.at[pl.ds(0, 8)], coef_in.at[1], (up, til)) if e == 0 else
            copy(dense.at[e, pl.ds(0, size)], rows_in.at[e, 1, pl.ds(0, size)], (up, til)),
            copy(coef_rows.at[pl.ds(8, 8)], coef_in.at[0], (down, til)) if e == 0 else
            copy(dense.at[e, pl.ds(512 - size, size)], rows_in.at[e, 0, pl.ds(256 - size, size)], (down, til)),
        ]

    def halo_pack(e):
        for j in range(4):
            first = swap_blocks([dense[e, (4 * j + b) * 32:(4 * j + b) * 32 + 8, :] for b in range(4)])
            last = swap_blocks([dense[e, (4 * j + b) * 32 + 24:(4 * j + b) * 32 + 32, :] for b in range(4)])
            packed[e, j] = last[3]
            packed[e, 4 + j] = first[0]

    def halo_start(e, deep=8, fields=1):
        copies = halo_copies(e, deep, fields)
        for c in copies[6:]:
            c.start()
        if e == 0:
            for i in range(3):
                to_cells(lambda r: coef_rows[r, 8 * i:8 * i + 8, :], dense.at[i], 16)
        for i in range(fields):
            halo_pack(e + i)
        for c in copies[:6]:
            c.start()
        amount = frame_b.at[pl.ds(0, 768 if e == 0 else 72 * deep + 64)]
        late.append(lambda: wait_all(amount, halo_send.at[e]))
        return lambda: wait_all(amount, halo_recv.at[e])

    def frame_own(e, out):
        def four_rows(j, _):
            for b in range(4):
                row = 4 * j + b
                base = pl.multiple_of((row + 8) * WIDE, 8)
                own = dense[e, pl.ds(pl.multiple_of(row * 32, 32), 32), :]
                out[pl.ds(base + 16, 32), :] = own
                out[pl.ds(base + 8, 8), :] = pltpu.roll(own[24:], 32, 1)
                out[pl.ds(base + WIDE, 8), :] = pltpu.roll(own[:8], 96, 1)
            return 0
        lax.fori_loop(0, 4, four_rows, 0)

    def frame_halo(e, out, deep=8):
        if e == 0:
            inside_up = jnp.where(reg > 0, 1.0, 0.0)
            inside_down = jnp.where(reg < regions - 1, 1.0, 0.0)
            rows_in[0, 0] = rows_in[0, 0] * inside_up
            rows_in[0, 1] = rows_in[0, 1] * inside_down
            for side, inside in ((left_in, jnp.where(til > 0, 1.0, 0.0)), (right_in, jnp.where(til < tiles - 1, 1.0, 0.0))):
                for j in range(8):
                    side[0, j] = side[0, j] * (inside * inside_up if j < 2 else inside if j < 6 else inside * inside_down)

        def beside(j, b):
            return pltpu.roll(left_in[e, j], -b * 32 % LANES, 1), pltpu.roll(right_in[e, j], (3 - b) * 32, 1)

        def own_rows(j, _):
            for b in range(4):
                base = pl.multiple_of((4 * j + b) * WIDE, 8)
                start, end = beside(j, b)
                out[pl.ds(base + 8, 8), :] = jnp.where(lane8 < 32, start, out[pl.ds(base + 8, 8), :])
                out[pl.ds(base + WIDE, 8), :] = jnp.where(lane8 >= 96, end, out[pl.ds(base + WIDE, 8), :])
            return 0

        lax.fori_loop(2, 6, own_rows, 0)
        for side in range(2):
            def outer_rows(j, _):
                for b in range(4):
                    row = 4 * j + b
                    base = pl.multiple_of((row + 24 * side) * WIDE, 8)
                    came = rows_in[e, side, pl.ds(pl.multiple_of(row * 32, 32), 32), :]
                    start, end = beside(j + 6 * side, b)
                    out[pl.ds(base + 16, 32), :] = came
                    out[pl.ds(base + 8, 8), :] = jnp.where(lane8 < 32, start, pltpu.roll(came[24:], 32, 1))
                    out[pl.ds(base + WIDE, 8), :] = jnp.where(lane8 >= 96, end, pltpu.roll(came[:8], 96, 1))
                return 0
            lax.fori_loop(0 if side else 2 - deep // 4, deep // 4 if side else 2, outer_rows, 0)

    def build_frame(e, arrive, out, deep=8, meanwhile=lambda: None):
        frame_own(e, out)
        drain()
        meanwhile()
        arrive()
        frame_halo(e, out, deep)

    def to_cells(line, out, rows):
        def four_rows(j, _):
            lines = [line(4 * j + b) for b in range(4)]
            many = jnp.concatenate([x for x in lines for _ in range(4)], axis=0).T
            for b, x in enumerate(swap_blocks([many[32 * g:32 * g + 32] for g in range(4)])):
                out[pl.ds(pl.multiple_of((4 * j + b) * 32, 32), 32), :] = x
            return 0
        lax.fori_loop(0, rows // 4, four_rows, 0)

    def to_natural(field, out):
        def four_rows(j, _):
            lines = [field[pl.ds(pl.multiple_of((4 * j + b) * 32, 32), 32), :] for b in range(4)]
            many = jnp.concatenate(swap_blocks(lines), axis=0).T
            for b in range(4):
                out[pl.ds(4 * j + b, 32, stride=16), :] = many[32 * b:32 * b + 32]
            return 0
        lax.fori_loop(0, 4, four_rows, 0)

    owner = owner_ref[...]
    marks = jnp.where(iota((tiles, count), 0) == owner, 1.0, 0.0)
    upper = jnp.where(iota((count, count), 0) < iota((count, count), 1), 1.0, 0.0).astype(BF16)
    before = dot(marks.astype(BF16), upper)
    slot = owner * CAP + jnp.sum(before * marks, axis=0, keepdims=True).astype(jnp.int32)
    meta_rows = [row_ref[...].astype(F32), col_ref[...].astype(F32)]
    meta_rows += [p.astype(F32) for p in split(innov_ref[...], 3) + split(var_ref[...], 3)]
    meta = jnp.zeros((8, count), F32)
    for i, line in enumerate(meta_rows):
        meta = jnp.where(iota((8, count), 0) == i, line, meta)
    meta = meta.astype(BF16)

    def choose(b, _):
        chosen = jnp.where(iota((LANES, count), 0) + b * LANES == slot, 1.0, 0.0).astype(BF16)
        pick[pl.ds(pl.multiple_of(b * LANES, LANES), LANES), :count] = chosen
        return 0

    lax.fori_loop(0, planes, choose, 0)
    facts = dot_nt(meta, pick[:, :count])
    place = facts[0:1] * LANES + facts[1:2]
    innov = facts[2:3] + facts[3:4] + facts[4:5]
    var = facts[5:6] + facts[6:7] + facts[7:8]
    for b in range(planes):
        at = slice(b * LANES, (b + 1) * LANES)
        three = [jnp.broadcast_to(x[:, at], (8, LANES)) for x in (place, innov, var)]
        for k in range(4):
            turned = [pltpu.roll(x, (i - k) * 32 % LANES, 1) for i, x in enumerate(three)]
            line = jnp.where(lane8 < 32, turned[0], jnp.where(lane8 < 64, turned[1], jnp.where(lane8 < 96, turned[2], 0.0)))
            msend[4 * b + k] = line[0:1]
    loads[5].wait()
    for i, part in enumerate(split(weight_ref[...], 3)):
        wsplit[:, i * LANES:(i + 1) * LANES] = part
    block = dot(pick[:, :count], wsplit[...])
    wsend[...] = (block[:, :LANES] + block[:, LANES:2 * LANES] + block[:, 2 * LANES:]).reshape(tiles, CAP, LANES)

    turns = sorted(range(planes), key=lambda i: (min(i, planes - i), i))
    plane, place_in = til // 4, lax.rem(til, 4)

    def sends(src, dst, send_sem, recv_sem, together):
        out = []
        for j, turn in enumerate(turns):
            for k in range(4):
                if j or k:
                    to = lax.rem(plane + turn, planes) * 4 + lax.rem(place_in + k, 4)
                    n = 4 * j + k
                    out.append(pltpu.make_async_remote_copy(
                        src_ref=src.at[to], dst_ref=dst.at[n], send_sem=send_sem, recv_sem=recv_sem.at[n // together],
                        device_id=(reg, to), device_id_type=MESH))
        return out

    def both_ways(copies):
        order = list(range(3))
        for j in range(1, planes, 2):
            order += [4 * i + k - 1 for k in range(4) for i in (j, j + 1) if i < planes]
        return [copies[i] for i in order]

    m_copies = sends(msend, mrecv, m_sem.at[0], m_sem.at[pl.ds(1, 1)], tiles)
    w_copies = sends(wsend, wrecv, w_send_sem.at[0], w_recv_sem, 4)
    late.append(lambda: wait_all(msend.at[pl.ds(1, tiles - 1)], m_sem.at[0]))
    late.append(lambda: wait_all(wsend.at[pl.ds(1, tiles - 1)], w_send_sem.at[0]))
    def drain():
        for wait in late:
            wait()
        late.clear()

    pl.semaphore_wait(barrier, (tiles - 1) + (regions - 1) + 4)
    for c in both_ways(m_copies) + both_ways(w_copies):
        c.start()
    wrecv[0] = wsend[til]
    mrecv[0] = msend[til]

    for c in loads[6:]:
        c.wait()

    def stage(r, _):
        for e, source in enumerate((mask_ref, kx_ref, ky_ref)):
            coef_rows[r, 8 * e:8 * e + 8, :] = source[pl.ds(r, 8, stride=16), :].astype(F32)
        return 0

    lax.fori_loop(0, 16, stage, 0)
    coef_arrive = halo_start(0, 8, 3)

    def diffuse(first, last):
        for s in range(first, last + 1):
            src, dst = (frame_a, frame_b) if (s - first) % 2 == 0 else (frame_b, frame_a)

            def lines(i, carry):
                before, here, west = carry
                base = pl.multiple_of((s + ROWS_AT_ONCE * i) * WIDE, 8)
                for u in range(ROWS_AT_ONCE):
                    at = base + u * WIDE
                    after = src[pl.ds(at + WIDE, WIDE), :]
                    east = coef[1, pl.ds(at, WIDE), :]
                    out = (coef[0, pl.ds(at, WIDE), :] * here + east * after) + west * before
                    dst[pl.ds(at, WIDE), :] = out + (
                        coef[2, pl.ds(at, WIDE), :] * src[pl.ds(at + 1, WIDE), :]
                        + coef[2, pl.ds(at - 1, WIDE), :] * src[pl.ds(at - 1, WIDE), :])
                    before, here, west = here, after, east
                return before, here, west

            at = (s - 1) * WIDE
            rows = 16 if s == HALO else TALL + 1 - 2 * s
            lax.fori_loop(
                0, -(-rows // ROWS_AT_ONCE), lines, (src[at:at + WIDE, :], src[at + WIDE:at + 2 * WIDE, :], coef[1, at:at + WIDE, :]))

    def inner(out):
        for j in range(16):
            out[j * 32:(j + 1) * 32, :] = frame_a[(8 + j) * WIDE + 16:(9 + j) * WIDE, :]

    wait_all(mrecv.at[pl.ds(1, tiles - 1)], m_sem.at[1])
    lane = iota((LANES, LANES), 1)
    seat = iota((LANES, LANES), 0) % CAP
    ones = jnp.ones((3 * LANES, LANES), BF16)
    cells = pick_t.shape[0]

    def corner_of(place, c):
        row = (place >> 7) + c // 2
        col = (place & 127) + c % 2
        return row * 32 + (col & 31), col >> 5

    def read_facts(j, _):
        at = pl.ds(pl.multiple_of(j * LANES, LANES), LANES)
        facts = jnp.broadcast_to(mrecv[pl.ds(4 * j, 4)], (4, CAP, LANES)).reshape(LANES, LANES)

        def spread_lanes(kind):
            return jnp.concatenate(split(jnp.where(lane == seat + 32 * kind, facts, 0.0), 3), axis=1)

        place3 = spread_lanes(0)
        place_col = dot(place3, ones).astype(jnp.int32)
        place_row = dot_nt(jnp.ones((8, 3 * LANES), BF16), place3).astype(jnp.int32)[0:1]
        var = dot(spread_lanes(2), ones)
        var_b[at, :] = var
        z_b[at, :] = var * dot(spread_lanes(1), ones)
        for c in range(4):
            cell, group = corner_of(place_col, c)
            group_b[c, at, :] = jnp.where(group == lane // 32, 1.0, 0.0)
            if c == 0:
                for t in range(cells // LANES):
                    hit = jnp.where(cell == lane + t * LANES, 1.0, 0.0).astype(BF16)
                    pick[at, t * LANES:(t + 1) * LANES] = hit
                    pick[at, cells + t * LANES:cells + (t + 1) * LANES] = hit
            cell, _ = corner_of(place_row, c)
            there = pl.ds(pl.multiple_of((4 * j + c) * LANES, LANES), LANES)
            pick_t[:, there] = jnp.where(iota((cells, LANES), 0) == cell, 1.0, 0.0).astype(BF16)
        return 0

    lax.fori_loop(0, planes, read_facts, 0)

    def put_terms(j, c):
        at = pl.ds(pl.multiple_of(j * LANES, LANES), LANES)
        there = pl.ds(pl.multiple_of((4 * j + c) * LANES, LANES), LANES)
        hi, lo = split(z_b[at, :] * expanded[c, at, :], 2)
        terms[there, :LANES] = hi
        terms[there, LANES:] = lo

    for e in range(3):
        frame_own(e, coef.at[e])

    copy_lanes = jnp.where(
        iota((3 * LANES, 4 * LANES), 0) % LANES == iota((3 * LANES, 4 * LANES), 1) // LANES * 32 + iota((3 * LANES, 4 * LANES), 1) % 32,
        1.0, 0.0).astype(BF16)
    def take_plane(j, first):
        wait_all(wrecv.at[pl.ds(4 * j + first, 4 - first)], w_recv_sem.at[j])
        wide = dot(jnp.concatenate(split(wrecv[pl.ds(4 * j, 4)].reshape(LANES, LANES), 3), axis=1), copy_lanes)
        at = pl.ds(pl.multiple_of(j * LANES, LANES), LANES)
        for c in range(4):
            expanded[c, at, :] = wide[:, c * LANES:(c + 1) * LANES] * group_b[c, at, :]
            expanded_0[c, at, :] = wide[:, c * LANES:(c + 1) * LANES] * group_b[0, at, :]
            put_terms(j, c)
        there = pl.ds(pl.multiple_of(4 * j * LANES, LANES), 4 * LANES)
        part = dot(pick_t[:, there], terms[there, :])
        return part[:, :LANES] + part[:, LANES:]

    state16[...] = jnp.zeros_like(state16)
    dense[3] = take_plane(0, 1)

    def later_plane(j, _):
        dense[3] = dense[3] + take_plane(j, 0)
        return 0

    lax.fori_loop(1, planes, later_plane, 0)

    def adjoint(e):
        def one(j, _):
            for c in range(4):
                put_terms(j, c)
            return 0
        lax.fori_loop(0, planes, one, 0)
        total = dot(pick_t[...], terms[...])
        dense[e] = total[:, :LANES] + total[:, LANES:]

    def observe(field, n):
        def corners(r, _):
            at = pl.multiple_of(r * 32, 32)
            here = field[pl.ds(at, 32), :]
            past = jnp.broadcast_to(pltpu.roll(here[:8], 96, 1)[0:1], (32, LANES))
            beside = jnp.where(iota((32, LANES), 0) == 31, past, field[pl.ds(at + 1, 32), :])
            above = pl.multiple_of(jnp.maximum(at - 32, 0), 32)
            for c, value in enumerate((here, beside)):
                for h, part in enumerate(split(value, 2)):
                    state16[pl.ds(h * cells + at, 32), c * LANES:(c + 1) * LANES] = part
                    state16[pl.ds(h * cells + above, 32), (2 + c) * LANES:(3 + c) * LANES] = part
            return 0

        lax.fori_loop(0, 16, corners, 0)
        acc[...] = jnp.zeros_like(acc)

        def one(i, _):
            values = dot(pick[...], state16[:, pl.ds(pl.multiple_of(i * 2 * LANES, LANES), 2 * LANES)])
            acc[...] += values[:, :LANES] * expanded_0[2 * i] + values[:, LANES:] * expanded_0[2 * i + 1]
            return 0

        lax.fori_loop(0, 2, one, 0)
        q = jnp.broadcast_to(jnp.sum(acc[...], axis=1, keepdims=True), acc.shape)
        q_b[n] = q

    def sums_start(n, sums):
        for i in range(4):
            sums_send[n, i:i + 1, :] = sums[i] if i < len(sums) else jnp.zeros((1, LANES), F32)
        for i in sorted(range(1, tiles), key=lambda i: -min(i, tiles - i)):
            pltpu.make_async_remote_copy(
                src_ref=sums_send.at[n], dst_ref=sums_tile.at[n, i], send_sem=t_sem.at[n, 0], recv_sem=t_sem.at[n, 1],
                device_id=(reg, lax.rem(til + i, tiles)), device_id_type=MESH).start()
        late.append(lambda: wait_all(sums_tile.at[n, pl.ds(1, tiles - 1)], t_sem.at[n, 0]))
        sums_tile[n, 0] = sums_send[n]

    def sums_middle(n):
        wait_all(sums_tile.at[n, pl.ds(1, tiles - 1)], t_sem.at[n, 1])
        sums_mid[n] = jnp.sum(sums_tile[n], axis=0)
        for i in sorted(range(1, regions), key=lambda i: -min(i, regions - i)):
            pltpu.make_async_remote_copy(
                src_ref=sums_mid.at[n], dst_ref=sums_region.at[n, i], send_sem=r_sem.at[n, 0], recv_sem=r_sem.at[n, 1],
                device_id=(lax.rem(reg + i, regions), til), device_id_type=MESH).start()
        late.append(lambda: wait_all(sums_region.at[n, pl.ds(1, regions - 1)], r_sem.at[n, 0]))
        sums_region[n, 0] = sums_mid[n]

    def sums_finish(n):
        wait_all(sums_region.at[n, pl.ds(1, regions - 1)], r_sem.at[n, 1])
        return jnp.sum(jnp.sum(sums_region[n], axis=0), axis=1, keepdims=True)

    def product(a, b):
        return jnp.sum(a * b, axis=0, keepdims=True)

    lane1 = iota((1, LANES), 1)

    def energy(a, b):
        return jnp.where(lane1 == 0, product(var_b[...] * q_b[a], q_b[b]), 0.0)

    arrive = halo_start(3)

    coef_arrive()
    for e in range(3):
        for side in range(2):
            to_cells(lambda r: coef_in[side, r, 8 * e:8 * e + 8, :], rows_in.at[e, side], 8)
        frame_halo(e, coef.at[e])

    def make_faces(k, _):
        base = pl.multiple_of(k * WIDE, 8)
        wet = coef[0, pl.ds(base, WIDE), :]
        coef[1, pl.ds(base, WIDE), :] = coef[1, pl.ds(base, WIDE), :] * wet * coef[0, pl.ds(base + WIDE, WIDE), :]
        coef[2, pl.ds(base, WIDE), :] = coef[2, pl.ds(base, WIDE), :] * wet * coef[0, pl.ds(base + 1, WIDE), :]
        return 0

    lax.fori_loop(0, TALL, make_faces, 0)

    def make_centre(k, _):
        base = pl.multiple_of(k * WIDE, 8)
        faces = coef[1, pl.ds(base, WIDE), :] + coef[1, pl.ds(base - WIDE, WIDE), :]
        faces = faces + coef[2, pl.ds(base, WIDE), :] + coef[2, pl.ds(base - 1, WIDE), :]
        coef[0, pl.ds(base, WIDE), :] = coef[0, pl.ds(base, WIDE), :] - faces
        return 0

    lax.fori_loop(1, TALL, make_centre, 0)

    build_frame(3, arrive, frame_a)
    diffuse(1, 4)
    inner(fields.at[0])
    diffuse(5, 8)
    inner(fields.at[1])

    norm = product(fields[0, :512, :], fields[0, :512, :])
    observe(fields.at[1], 0)
    z_b[...] = var_b[...] * q_b[0]
    adjoint(4)
    arrive = halo_start(4)
    sums_start(0, (norm, energy(0, 0)))
    to_natural(fields.at[0], natural.at[0])
    leaving = [pltpu.make_async_copy(natural.at[i, pl.ds(0, 512)], natural_out.at[i], out_sem.at[i]) for i in range(4)]
    leaving[0].start()
    build_frame(4, arrive, frame_a)
    diffuse(1, 4)
    sums_middle(0)
    inner(fields.at[2])
    diffuse(5, 8)
    inner(fields.at[4])
    observe(fields.at[4], 1)
    fields[2, :512, :] = fields[0, :512, :] + fields[2, :512, :]
    found = sums_finish(0)
    norm_0, energy_0 = found[0:1], found[1:2]
    alpha_0 = norm_0 / (norm_0 + energy_0)
    q_b[1] = q_b[0] - alpha_0 * (q_b[0] + q_b[1])
    fields[3, :512, :] = fields[0, :512, :] - alpha_0 * fields[2, :512, :]
    sums_start(1, (
        product(fields[3, :512, :], fields[3, :512, :]), product(fields[3, :512, :], fields[0, :512, :]), energy(1, 1), energy(1, 0)))
    z_b[...] = var_b[...] * q_b[1]
    adjoint(5)
    arrive = halo_start(5, 4)
    for i in (1, 2):
        to_natural(fields.at[i + 1], natural.at[i])
        leaving[i].start()
    build_frame(5, arrive, frame_a, 4, lambda: sums_middle(1))
    diffuse(5, 8)
    inner(fields.at[5])
    to_natural(fields.at[5], natural.at[3])
    leaving[3].start()
    drain()
    found = sums_finish(1)
    norm_1 = found[0:1]
    beta = norm_1 / norm_0
    curve = norm_1 + 2.0 * beta * found[1:2] + beta * beta * norm_0 + found[2:3] + 2.0 * beta * found[3:4] + beta * beta * energy_0
    alpha_1 = norm_1 / curve
    factor_out[...] = jnp.zeros_like(factor_out)
    for i, x in enumerate((alpha_0 + alpha_1 * beta, alpha_1, alpha_1 * beta)):
        factor_out[i:i + 1, :] = jnp.broadcast_to(x, (1, LANES))
    for c in leaving:
        c.wait()


def combine(natural, factor, control, residual):
    whole, second, mixed = factor[0:1, :], factor[1:2, :], factor[2:3, :]
    control[...] = whole * natural[0] + second * natural[2]
    residual[...] = natural[2] - second * (natural[2] + natural[3]) - mixed * natural[1]


def body(regions, tiles, kx, ky, mask, obs_owner, obs_row, obs_col, obs_weight, innovation, inverse_var):
    levels, rows_x, cols_y = kx.shape
    count = obs_row.shape[0]
    slots = tiles * CAP
    cells = rows_x * cols_y // GROUPS
    line, flat = (1, count), (levels * rows_x, cols_y)
    out = jax.ShapeDtypeStruct((32 * rows_x, cols_y), F32)
    dma = pltpu.SemaphoreType.DMA
    args = (
        kx.reshape(flat), ky.reshape(flat), mask.reshape(flat), obs_owner.reshape(line), obs_row.reshape(line),
        obs_col.reshape(line), innovation.reshape(line), inverse_var.reshape(line), obs_weight,
    )
    natural, factor = pl.pallas_call(
        functools.partial(kernel, regions, tiles),
        out_shape=(jax.ShapeDtypeStruct((4, 32 * rows_x, cols_y), F32), jax.ShapeDtypeStruct((8, LANES), F32)),
        in_specs=[pl.BlockSpec(memory_space=pl.ANY)] * 9,
        out_specs=[pl.BlockSpec(memory_space=pl.ANY), pl.BlockSpec(memory_space=pltpu.VMEM)],
        scratch_shapes=[
            *[pltpu.VMEM((x.shape[0] + (16 if i < 3 else 0), x.shape[1]), x.dtype) for i, x in enumerate(args)],
            pltpu.VMEM((EXCHANGES, cells, LANES), F32),
            pltpu.VMEM((EXCHANGES, 2, 32 * HALO, LANES), F32),
            pltpu.VMEM((EXCHANGES, 8, 8, LANES), F32),
            pltpu.VMEM((EXCHANGES, 8, 8, LANES), F32),
            pltpu.VMEM((EXCHANGES, 8, 8, LANES), F32),
            pltpu.VMEM((FRAME, LANES), F32),
            pltpu.VMEM((FRAME, LANES), F32),
            pltpu.VMEM((3, FRAME, LANES), F32),
            pltpu.VMEM((count, 3 * LANES), BF16),
            pltpu.VMEM((tiles, CAP, LANES), F32),
            pltpu.VMEM((tiles, CAP, LANES), F32),
            pltpu.VMEM((tiles, 1, LANES), F32),
            pltpu.VMEM((tiles, 1, LANES), F32),
            pltpu.VMEM((4, slots, LANES), F32),
            pltpu.VMEM((4, slots, LANES), F32),
            pltpu.VMEM((16, 24, LANES), F32),
            pltpu.VMEM((2, HALO, 24, LANES), F32),
            pltpu.VMEM((slots, 2 * cells), BF16),
            pltpu.VMEM((cells, 4 * slots), BF16),
            pltpu.VMEM((4 * slots, 2 * LANES), BF16),
            pltpu.VMEM((slots, LANES), F32),
            pltpu.VMEM((slots, LANES), F32),
            pltpu.VMEM((2, slots, LANES), F32),
            pltpu.VMEM((slots, LANES), F32),
            pltpu.VMEM((4, slots, LANES), F32),
            pltpu.VMEM((2 * cells, 4 * LANES), BF16),
            pltpu.VMEM((6, cells + 8, LANES), F32),
            pltpu.VMEM((4, cells + 16, LANES), F32),
            pltpu.VMEM((2, 4, LANES), F32),
            pltpu.VMEM((2, regions, 4, LANES), F32),
            pltpu.VMEM((2, 4, LANES), F32),
            pltpu.VMEM((2, tiles, 4, LANES), F32),
            dma((9,)), dma((4,)), dma((EXCHANGES,)), dma((EXCHANGES,)), dma((1,)), dma((tiles // 4,)), dma((2,)), dma((2, 2)), dma((2, 2)),
        ],
        compiler_params=pltpu.CompilerParams(collective_id=0, has_side_effects=True, vmem_limit_bytes=60 * 1024 * 1024),
    )(*args)
    control, residual = pl.pallas_call(
        combine,
        out_shape=(out, out),
        in_specs=[pl.BlockSpec(memory_space=pltpu.VMEM)] * 2,
        out_specs=[pl.BlockSpec(memory_space=pltpu.VMEM)] * 2,
        compiler_params=pltpu.CompilerParams(vmem_limit_bytes=60 * 1024 * 1024),
    )(natural, factor)
    shape = (32 // levels, levels, rows_x, cols_y)
    return control.reshape(shape), residual.reshape(shape)


def solution(mesh):
    return jax.shard_map(
        functools.partial(body, mesh.shape["region"], mesh.shape["tile"]),
        mesh=mesh,
        in_specs=(
            P(None, "region", "tile"),
            P(None, "region", "tile"),
            P(None, "region", "tile"),
            P(("region", "tile"), None),
            P(("region", "tile")),
            P(("region", "tile")),
            P(("region", "tile"), None),
            P(("region", "tile")),
            P(("region", "tile")),
        ),
        out_specs=(P(None, None, "region", "tile"), P(None, None, "region", "tile")),
        check_vma=False,
    )
```
